32 devices in a mesh: seq: 16 (over z, y, x), tp: 2 (over core).
Axes of the slice: x: 2, y: 2, z: 4, core: 2. Of those that a mesh axis runs over, the one named last changes fastest.
Arguments:
- tokens: bfloat16 [8192, 768], P(('seq', 'tp')), may hold values from -6 to 6
- seq_lengths: int32 [16], P('seq'), may hold values from 64 to 512, as said below
- cotangent: bfloat16 [8192, 768], P(('seq', 'tp')), may hold values from -6 to 6
- norm1_gain: bfloat16 [768], replicated, may hold values from 0.099609375 to 1.8984375
- norm1_shift: bfloat16 [768], replicated, may hold values from -3 to 3
- qkv1_weight: bfloat16 [768, 3, 768], P(None, None, 'tp'), may hold values from -0.21875 to 0.21875
- qv1_bias: bfloat16 [2, 768], P(None, 'tp'), may hold values from -3 to 3
- out1_weight: bfloat16 [768, 768], P('tp'), may hold values from -0.875 to 0.875
- out1_bias: bfloat16 [768], replicated, may hold values from -3 to 3
- norm2_gain: bfloat16 [768], replicated, may hold values from 0.099609375 to 1.8984375
- norm2_shift: bfloat16 [768], replicated, may hold values from -3 to 3
- fc1_weight: bfloat16 [768, 3072], P(None, 'tp'), may hold values from -0.21875 to 0.21875
- fc1_bias: bfloat16 [3072], P('tp'), may hold values from -3 to 3
- proj1_weight: bfloat16 [3072, 768], P('tp'), may hold values from -0.15625 to 0.15625
- proj1_bias: bfloat16 [768], replicated, may hold values from -3 to 3
- norm3_gain: bfloat16 [768], replicated, may hold values from 0.099609375 to 1.8984375
- norm3_shift: bfloat16 [768], replicated, may hold values from -3 to 3
- qk2_weight: bfloat16 [768, 2, 768], P(None, None, 'tp'), may hold values from -0.21875 to 0.21875
- v2_weight: bfloat16 [768, 384], P(None, 'tp'), may hold values from -0.21875 to 0.21875
- q2_bias: bfloat16 [768], P('tp'), may hold values from -3 to 3
- v2_bias: bfloat16 [384], P('tp'), may hold values from -3 to 3
- out2_weight: bfloat16 [768, 768], P('tp'), may hold values from -0.875 to 0.875
- out2_bias: bfloat16 [768], replicated, may hold values from -3 to 3
- norm4_gain: bfloat16 [768], replicated, may hold values from 0.099609375 to 1.8984375
- norm4_shift: bfloat16 [768], replicated, may hold values from -3 to 3
- fc2_weight: bfloat16 [768, 3072], P(None, 'tp'), may hold values from -0.21875 to 0.21875
- fc2_bias: bfloat16 [3072], P('tp'), may hold values from -3 to 3
- proj2_weight: bfloat16 [3072, 768], P('tp'), may hold values from -0.15625 to 0.15625
- proj2_bias: bfloat16 [768], replicated, may hold values from -3 to 3
Outputs:
- layer_output: bfloat16 [8192, 768], P(('seq', 'tp'))
- tokens_grad: bfloat16 [8192, 768], P(('seq', 'tp'))
- grad_norm1_gain: float32 [768], replicated
- grad_norm1_shift: float32 [768], replicated
- grad_qkv1_weight: float32 [768, 3, 768], P('seq', None, 'tp')
- grad_qv1_bias: float32 [2, 768], replicated
- grad_out1_weight: float32 [768, 768], P('tp', 'seq')
- grad_out1_bias: float32 [768], replicated
- grad_norm2_gain: float32 [768], replicated
- grad_norm2_shift: float32 [768], replicated
- grad_fc1_weight: float32 [768, 3072], P('seq', 'tp')
- grad_fc1_bias: float32 [3072], replicated
- grad_proj1_weight: float32 [3072, 768], P('tp', 'seq')
- grad_proj1_bias: float32 [768], replicated
- grad_norm3_gain: float32 [768], replicated
- grad_norm3_shift: float32 [768], replicated
- grad_qk2_weight: float32 [768, 2, 768], P('seq', None, 'tp')
- grad_v2_weight: float32 [768, 384], P('seq', 'tp')
- grad_q2_bias: float32 [768], replicated
- grad_v2_bias: float32 [384], replicated
- grad_out2_weight: float32 [768, 768], P('tp', 'seq')
- grad_out2_bias: float32 [768], replicated
- grad_norm4_gain: float32 [768], replicated
- grad_norm4_shift: float32 [768], replicated
- grad_fc2_weight: float32 [768, 3072], P('seq', 'tp')
- grad_fc2_bias: float32 [3072], replicated
- grad_proj2_weight: float32 [3072, 768], P('tp', 'seq')
- grad_proj2_bias: float32 [768], replicated
The draws below stay inside these ranges and needn't reach their ends.
Inputs may be any that keep to these rules, and one draw needn't show every extreme that they name: seq_lengths[b] is the number of real tokens at the start of slot b; some slot is full in every draw.
All inputs are finite; a program needn't handle non-finite values.
Results may differ from the reference program's by a relative error of at most 0.038.
Values may be sent and summed in bfloat16 or wider, within the bound.
No kernel may reach another device: no remote copies, remote signals or barrier semaphores. Data moves between devices by JAX's collectives and lax.ppermute only.
A program may use at most 192 MiB of HBM per device.

```python
import math
import jax
import jax.numpy as jnp
from jax import lax

HEADS = 12
HEAD_DIM = 64
D = 768
FF = 3072
SLOT = 512
MIN_LEN = 64
BUCKETS = 16
TOKENS = 8192


def draw_seq_lengths(key, part):
    key = jax.random.fold_in(key, 7)
    levels = (SLOT // MIN_LEN).bit_length() - 1
    key_power, key_spread, key_full = jax.random.split(key, 3)
    power = jax.random.randint(key_power, (BUCKETS,), 0, levels + 2)
    lowest = jnp.left_shift(jnp.full((BUCKETS,), MIN_LEN, jnp.int32), power)
    spread = jax.random.randint(key_spread, (BUCKETS,), 0, 1 << 30) % lowest
    lengths = jnp.minimum(lowest + spread, SLOT)
    chosen = jax.random.randint(key_full, (), 0, BUCKETS)
    lengths = jnp.where(jnp.arange(BUCKETS) == chosen, SLOT, lengths)
    return lengths.astype(jnp.int32)


def strengthened(entries, stream_key, source, target, blocks, factor):
    def block_of(position):
        return (jnp.arange(entries.shape[position]) // (entries.shape[position] // blocks)).reshape((-1,) + (1,) * (entries.ndim - 1 - position))

    one_side = jax.random.permutation(stream_key, blocks)[block_of(target)]
    second = (block_of(target) + blocks // 2) % blocks
    return jnp.where((block_of(source) == one_side) | (block_of(source) == second), factor * entries, entries)


def level_of(stream_key, shape, cuts, low, high):
    level, own = 1.0, jax.random.fold_in(stream_key, 6)
    for dim, blocks in cuts:
        steps = jnp.exp(jax.random.uniform(jax.random.fold_in(own, dim), (blocks,), jnp.float32, low / len(cuts), high / len(cuts)))
        level = level * jnp.repeat(steps, shape[dim] // blocks).reshape([-1 if axis == dim else 1 for axis in range(len(shape))])
    return level


def noise(own_key, extent, deviation, limit, cuts=(), kind=jnp.bfloat16):
    result = jax.random.normal(own_key, extent, jnp.float32) * deviation
    if len(cuts) > 0:
        result = level_of(own_key, extent, cuts, -0.22, 0.18) * result
    return jnp.clip(result, min=-limit, max=limit).astype(kind)


def noise_with(own_key, shape, scale, most, shards, heavy, held_as=jnp.bfloat16):
    array = scale * jax.random.normal(own_key, shape, jnp.float32)
    if shards:
        array = array * level_of(own_key, shape, shards, -0.22, 0.18)
    return jnp.clip(strengthened(array, jax.random.fold_in(own_key, 3), *heavy), -most, most).astype(held_as)


def setup_inputs(seed: int = 0) -> dict:
    streams_of = jax.random.split(jax.random.key(seed), 30)
    tokens = noise_with(streams_of[0], (TOKENS, D), 1.0, 6.0, ((0, 32),), (0, 1, 32, 2.75))
    seq_lengths = draw_seq_lengths(jax.random.fold_in(streams_of[29], 71), 0)
    cotangent = noise_with(streams_of[2], (TOKENS, D), 1.0, 6.0, ((0, 32),), (0, 1, 32, 2.75))
    norm1_gain = jnp.clip(1.0 + 0.18 * jax.random.normal(streams_of[3], (D,), jnp.float32), 0.099609375, 1.8984375).astype(jnp.bfloat16)
    norm1_shift = noise(streams_of[4], (D,), 0.3, 3.0)
    qkv1_weight = noise(streams_of[5], (D, 3, D), D ** -0.5, 0.21875, ((2, 2),))
    qv1_bias = noise(streams_of[6], (2, D), 0.5, 3.0, ((1, 2),))
    out1_weight = noise(streams_of[7], (D, D), (D // 16) ** -0.5, 0.875, ((0, 2),))
    out1_bias = noise(streams_of[8], (D,), 0.5, 3.0)
    norm2_gain = jnp.clip(1.0 + 0.18 * jax.random.normal(streams_of[9], (D,), jnp.float32), 0.099609375, 1.8984375).astype(jnp.bfloat16)
    norm2_shift = noise(streams_of[10], (D,), 0.3, 3.0)
    fc1_weight = noise(streams_of[11], (D, FF), D ** -0.5, 0.21875, ((1, 2),))
    fc1_bias = noise(streams_of[12], (FF,), 0.5, 3.0, ((0, 2),))
    proj1_weight = noise(streams_of[13], (FF, D), (FF // 2) ** -0.5, 0.15625, ((0, 2),))
    proj1_bias = noise(streams_of[14], (D,), 0.5, 3.0)
    norm3_gain = jnp.clip(1.0 + 0.18 * jax.random.normal(streams_of[15], (D,), jnp.float32), 0.099609375, 1.8984375).astype(jnp.bfloat16)
    norm3_shift = noise(streams_of[16], (D,), 0.3, 3.0)
    qk2_weight = noise(streams_of[17], (D, 2, D), D ** -0.5, 0.21875, ((2, 2),))
    v2_weight = noise(streams_of[18], (D, D // 2), D ** -0.5, 0.21875, ((1, 2),))
    q2_bias = noise(streams_of[19], (D,), 0.5, 3.0, ((0, 2),))
    v2_bias = noise(streams_of[20], (D // 2,), 0.5, 3.0, ((0, 2),))
    out2_weight = noise(streams_of[21], (D, D), (D // 16) ** -0.5, 0.875, ((0, 2),))
    out2_bias = noise(streams_of[22], (D,), 0.5, 3.0)
    norm4_gain = jnp.clip(1.0 + 0.18 * jax.random.normal(streams_of[23], (D,), jnp.float32), 0.099609375, 1.8984375).astype(jnp.bfloat16)
    norm4_shift = noise(streams_of[24], (D,), 0.3, 3.0)
    fc2_weight = noise(streams_of[25], (D, FF), D ** -0.5, 0.21875, ((1, 2),))
    fc2_bias = noise(streams_of[26], (FF,), 0.5, 3.0, ((0, 2),))
    proj2_weight = noise(streams_of[27], (FF, D), (FF // 2) ** -0.5, 0.15625, ((0, 2),))
    proj2_bias = noise(streams_of[28], (D,), 0.5, 3.0)
    return dict(tokens=tokens, seq_lengths=seq_lengths, cotangent=cotangent, norm1_gain=norm1_gain, norm1_shift=norm1_shift, qkv1_weight=qkv1_weight, qv1_bias=qv1_bias, out1_weight=out1_weight, out1_bias=out1_bias, norm2_gain=norm2_gain, norm2_shift=norm2_shift, fc1_weight=fc1_weight, fc1_bias=fc1_bias, proj1_weight=proj1_weight, proj1_bias=proj1_bias, norm3_gain=norm3_gain, norm3_shift=norm3_shift, qk2_weight=qk2_weight, v2_weight=v2_weight, q2_bias=q2_bias, v2_bias=v2_bias, out2_weight=out2_weight, out2_bias=out2_bias, norm4_gain=norm4_gain, norm4_shift=norm4_shift, fc2_weight=fc2_weight, fc2_bias=fc2_bias, proj2_weight=proj2_weight, proj2_bias=proj2_bias)


@jax.custom_vjp
def low(v):
    return lax.optimization_barrier(v.astype(jnp.bfloat16)).astype(jnp.float32)

@jax.custom_vjp
def low_back(v):
    return v

def low_keep(v):
    return (low(v), None)

def low_pass(kept, grad):
    return (grad,)

def back_keep(v):
    return (v, None)

def back_low(kept, grad):
    return (low(grad),)
low.defvjp(low_keep, low_pass)
low_back.defvjp(back_keep, back_low)

def matmul(left_side, right_side):
    return jnp.dot(left_side, right_side, precision=lax.Precision.HIGHEST)

def layer_norm(values, norm_gain, norm_shift):
    average = lax.optimization_barrier(jnp.mean(values, axis=-1, keepdims=True))
    centered = values - average
    variance = lax.optimization_barrier(jnp.mean(centered * centered, axis=-1, keepdims=True))
    return centered * lax.rsqrt(variance + 1e-05) * norm_gain + norm_shift

def gelu_tanh(values):
    return 0.5 * values * (1.0 + jnp.tanh(0.7978845608028654 * (values + 0.044715 * values * values * values)))

def attend(query_rows, key_rows, value_rows, length):
    scores = jnp.einsum('qhd,khd->hqk', query_rows, key_rows, precision=lax.Precision.HIGHEST) * HEAD_DIM ** (-0.5)
    scores = low_back(scores)
    places = jnp.arange(SLOT)
    allowed = (places[None, :] <= places[:, None]) & (places[None, :] < length)
    scores = jnp.where(allowed[None], scores, -1e+30)
    largest = lax.optimization_barrier(jnp.max(scores, axis=-1, keepdims=True))
    weights = jnp.exp(scores - largest)
    weights = low(weights / lax.optimization_barrier(jnp.sum(weights, axis=-1, keepdims=True)))
    mixed_rows = jnp.einsum('hqk,khd->qhd', weights, value_rows, precision=lax.Precision.HIGHEST)
    return mixed_rows.reshape(SLOT, HEADS * HEAD_DIM)

def attention(query_rows, key_rows, value_rows, lengths):
    seq_count = lengths.shape[0]

    def shaped(matrix):
        return matrix.reshape(seq_count, SLOT, HEADS, HEAD_DIM)

    def per_slot(packed):
        return jax.checkpoint(attend)(packed[0], packed[1], packed[2], packed[3])
    mixed_rows = lax.map(per_slot, (shaped(query_rows), shaped(key_rows), shaped(value_rows), lengths))
    return mixed_rows.reshape(seq_count * SLOT, HEADS * HEAD_DIM)

def feed_block(residual, norm_gain, norm_shift, fc_weight, fc_bias, proj_weight, proj_bias):
    normed = low(layer_norm(residual, norm_gain, norm_shift))
    hidden = low_back(matmul(normed, fc_weight) + fc_bias)
    hidden = low(gelu_tanh(hidden))
    return residual + low_back(matmul(hidden, proj_weight)) + proj_bias

def forward(residual, lengths, params):
    norm1_gain, norm1_shift, qkv1_weight, qv1_bias, out1_weight, out1_bias, norm2_gain, norm2_shift, fc1_weight, fc1_bias, proj1_weight, proj1_bias, norm3_gain, norm3_shift, qk2_weight, v2_weight, q2_bias, v2_bias, out2_weight, out2_bias, norm4_gain, norm4_shift, fc2_weight, fc2_bias, proj2_weight, proj2_bias = params
    model_width = HEADS * HEAD_DIM
    row_count = residual.shape[0]
    normed = low(layer_norm(residual, norm1_gain, norm1_shift))
    joined = matmul(normed, qkv1_weight.reshape(model_width, 3 * model_width))
    query_rows = low(low_back(joined[:, :model_width] + qv1_bias[0]))
    key_rows = low(low_back(joined[:, model_width:2 * model_width]))
    first_values = low(low_back(joined[:, 2 * model_width:] + qv1_bias[1]))
    mixed_rows = low(low_back(attention(query_rows, key_rows, first_values, lengths)))
    residual = residual + low_back(matmul(mixed_rows, out1_weight)) + out1_bias
    residual = feed_block(residual, norm2_gain, norm2_shift, fc1_weight, fc1_bias, proj1_weight, proj1_bias)
    normed = low(layer_norm(residual, norm3_gain, norm3_shift))
    joined = matmul(normed, qk2_weight.reshape(model_width, 2 * model_width))
    query_rows = low(low_back(joined[:, :model_width] + q2_bias))
    key_rows = low(low_back(joined[:, model_width:]))
    fresh_values = low(low_back(matmul(normed, v2_weight) + v2_bias))
    quarter = HEADS // 4
    second_values = jnp.concatenate([fresh_values.reshape(row_count, 2, quarter, HEAD_DIM), first_values.reshape(row_count, 2, 2 * quarter, HEAD_DIM)[:, :, quarter:]], axis=2).reshape(row_count, model_width)
    mixed_rows = low(low_back(attention(query_rows, key_rows, second_values, lengths)))
    residual = residual + low_back(matmul(mixed_rows, out2_weight)) + out2_bias
    residual = feed_block(residual, norm4_gain, norm4_shift, fc2_weight, fc2_bias, proj2_weight, proj2_bias)
    places = jnp.arange(SLOT)
    live_rows = (places[None, :] < lengths[:, None]).astype(residual.dtype).reshape(row_count)
    return residual * live_rows[:, None]

def reference(tokens, seq_lengths, cotangent, norm1_gain, norm1_shift, qkv1_weight, qv1_bias, out1_weight, out1_bias, norm2_gain, norm2_shift, fc1_weight, fc1_bias, proj1_weight, proj1_bias, norm3_gain, norm3_shift, qk2_weight, v2_weight, q2_bias, v2_bias, out2_weight, out2_bias, norm4_gain, norm4_shift, fc2_weight, fc2_bias, proj2_weight, proj2_bias):
    params = tuple((weight.astype(jnp.float32) for weight in (norm1_gain, norm1_shift, qkv1_weight, qv1_bias, out1_weight, out1_bias, norm2_gain, norm2_shift, fc1_weight, fc1_bias, proj1_weight, proj1_bias, norm3_gain, norm3_shift, qk2_weight, v2_weight, q2_bias, v2_bias, out2_weight, out2_bias, norm4_gain, norm4_shift, fc2_weight, fc2_bias, proj2_weight, proj2_bias)))
    model_width = HEADS * HEAD_DIM
    group_size = math.gcd(BUCKETS, max(1, 4096 // SLOT))
    group_count = BUCKETS // group_size
    inputs = tokens.astype(jnp.float32).reshape(group_count, group_size * SLOT, model_width)
    cotangents = cotangent.astype(jnp.float32).reshape(group_count, group_size * SLOT, model_width)
    lengths = seq_lengths.reshape(group_count, group_size)

    def one_group(totals, packed):
        group_rows, group_cotangent, group_lengths = packed

        def apply_layers(rows_in, weights_in):
            return forward(rows_in, group_lengths, weights_in)
        output, pull_back = jax.vjp(apply_layers, group_rows, params)
        rows_grad, weight_grads = pull_back(group_cotangent)
        totals = jax.tree.map(jnp.add, totals, weight_grads)
        return (totals, (output.astype(jnp.bfloat16), rows_grad.astype(jnp.bfloat16)))
    zero_grads = jax.tree.map(jnp.zeros_like, params)
    totals, (outputs, input_grads) = lax.scan(one_group, zero_grads, (inputs, cotangents, lengths))
    return (outputs.reshape(TOKENS, model_width), input_grads.reshape(TOKENS, model_width), totals[0], totals[1], totals[2], totals[3], totals[4], totals[5], totals[6], totals[7], totals[8], totals[9], totals[10], totals[11], totals[12], totals[13], totals[14], totals[15], totals[16], totals[17], totals[18], totals[19], totals[20], totals[21], totals[22], totals[23], totals[24], totals[25])
```

```python
import jax
import jax.numpy as jnp
from jax import lax
from jax.sharding import PartitionSpec as P

HEAD_DIM = 64
F32 = jnp.float32
BF16 = jnp.bfloat16


def half(values):
    return values.astype(BF16)


def full(values):
    return values.astype(F32)


def dot(left, right):
    return lax.dot_general(left, right, (((1,), (0,)), ((), ())), preferred_element_type=F32)


def dot_nt(left, right):
    return lax.dot_general(left, right, (((1,), (1,)), ((), ())), preferred_element_type=F32)


def dot_tn(left, right):
    return lax.dot_general(left, right, (((0,), (0,)), ((), ())), preferred_element_type=F32)


def swap(values):
    return lax.ppermute(values, "tp", [(0, 1), (1, 0)])


def norm_stats(values):
    mean = jnp.mean(values, axis=-1, keepdims=True)
    centered = values - mean
    scale = lax.rsqrt(jnp.mean(centered * centered, axis=-1, keepdims=True) + 1e-05)
    return centered * scale, scale


def norm_forward(values, gain, shift):
    hat, _ = norm_stats(values)
    return half(hat * full(gain) + full(shift))


def norm_backward(grad, values, gain):
    hat, scale = norm_stats(values)
    inner = grad * full(gain)
    mean_inner = jnp.mean(inner, axis=-1, keepdims=True)
    mean_hat = jnp.mean(inner * hat, axis=-1, keepdims=True)
    pulled = scale * (inner - mean_inner - hat * mean_hat)
    return pulled, jnp.sum(grad * hat, axis=0), jnp.sum(grad, axis=0)


def gelu_both(values):
    inner = 0.7978845608028654 * (values + 0.044715 * values * values * values)
    bent = jnp.tanh(inner)
    slope = 0.7978845608028654 * (1.0 + 0.134145 * values * values)
    value = 0.5 * values * (1.0 + bent)
    pull = 0.5 * (1.0 + bent) + 0.5 * values * (1.0 - bent * bent) * slope
    return value, pull


def split_heads(rows):
    return rows.reshape(rows.shape[0], rows.shape[1] // HEAD_DIM, HEAD_DIM)


def soft_weights(query, key, length):
    scores = jnp.einsum("qhd,khd->hqk", query, key, preferred_element_type=F32) * HEAD_DIM ** (-0.5)
    place = jnp.arange(query.shape[0])
    allowed = (place[None, :] <= place[:, None]) & (place[None, :] < length)
    scores = jnp.where(allowed[None], scores, -1e30)
    weights = jnp.exp(scores - jnp.max(scores, axis=-1, keepdims=True))
    return weights / jnp.sum(weights, axis=-1, keepdims=True)


def attend(query, key, value, length):
    weights = half(soft_weights(split_heads(query), split_heads(key), length))
    mixed = jnp.einsum("hqk,khd->qhd", weights, split_heads(value), preferred_element_type=F32)
    return half(mixed.reshape(query.shape))


def attend_backward(query, key, value, grad, length):
    shape = query.shape
    query, key, value, grad = (split_heads(rows) for rows in (query, key, value, grad))
    weights = soft_weights(query, key, length)
    pulled = jnp.einsum("qhd,khd->hqk", grad, value, preferred_element_type=F32)
    centre = jnp.sum(pulled * weights, axis=-1, keepdims=True)
    score = half(weights * (pulled - centre))
    scale = HEAD_DIM ** (-0.5)
    dq = jnp.einsum("hqk,khd->qhd", score, key, preferred_element_type=F32) * scale
    dk = jnp.einsum("hqk,qhd->khd", score, query, preferred_element_type=F32) * scale
    dv = jnp.einsum("hqk,qhd->khd", half(weights), grad, preferred_element_type=F32)
    return dq.reshape(shape), dk.reshape(shape), dv.reshape(shape)


def axis_sizes(count):
    bits = count.bit_length() - 1
    fours = max(0, (bits - 1) // 2)
    return (4,) * fours + (2,) * (bits - 2 * fours)


def strides_of(sizes):
    strides, stride = [], 1
    for size in reversed(sizes):
        strides.append(stride)
        stride *= size
    return tuple(reversed(strides))


def shift_pairs(count, size, stride, step, senders):
    pairs = []
    for index in range(count):
        place = (index // stride) % size
        if place in senders:
            pairs.append((index, index + step * stride))
    return pairs


def scatter_sum(rows, order, count):
    sizes = axis_sizes(count)
    strides = strides_of(sizes)
    me = lax.axis_index("seq")
    width = rows.shape[1]
    work = rows.reshape(sizes + (rows.shape[0] // count, width))
    left = list(range(len(sizes)))
    for axis in order:
        size, stride = sizes[axis], strides[axis]
        dim = left.index(axis)
        mine = (me // stride) % size

        def pick(place):
            return lax.dynamic_index_in_dim(work, place, dim, keepdims=False)

        if size == 2:
            pairs = shift_pairs(count, 2, stride, 1, (0,)) + shift_pairs(count, 2, stride, -1, (1,))
            total = full(pick(mine)) + full(lax.ppermute(half(pick(1 - mine)), "seq", pairs))
        else:
            up = down = None
            for step in range(1, size):
                far = size - step
                up_part = full(pick(jnp.minimum(mine + far, size - 1)))
                down_part = full(pick(jnp.maximum(mine - far, 0)))
                if up is not None:
                    up_part, down_part = up_part + full(up), down_part + full(down)
                up = lax.ppermute(
                    half(up_part), "seq", shift_pairs(count, size, stride, 1, range(step))
                )
                down = lax.ppermute(
                    half(down_part), "seq", shift_pairs(count, size, stride, -1, range(far, size))
                )
            total = full(pick(mine)) + full(up) + full(down)
        left.remove(axis)
        work = total if not left else half(total)
    return full(work)


def all_sum(vector, count):
    distance = 1
    while distance < count:
        pairs = [(index, index ^ distance) for index in range(count)]
        vector = vector + lax.ppermute(vector, "seq", pairs)
        distance *= 2
    return vector


def on_device(count, *arguments):
    (
        tokens, seq_lengths, cotangent, norm1_gain, norm1_shift, qkv1_weight, qv1_bias, out1_weight, out1_bias,
        norm2_gain, norm2_shift, fc1_weight, fc1_bias, proj1_weight, proj1_bias, norm3_gain, norm3_shift,
        qk2_weight, v2_weight, q2_bias, v2_bias, out2_weight, out2_bias, norm4_gain, norm4_shift, fc2_weight,
        fc2_bias, proj2_weight, proj2_bias,
    ) = arguments
    half_rows, model = tokens.shape
    rows = 2 * half_rows
    local = qkv1_weight.shape[2]
    fresh = v2_weight.shape[1]
    core = lax.axis_index("tp")
    length = seq_lengths[0]
    sizes = axis_sizes(count)
    order_a = tuple(reversed(range(len(sizes))))
    order_b = order_a[1::-1] + order_a[2:]

    def whole(mine):
        other = swap(mine)
        return jnp.where(
            core == 0, jnp.concatenate([mine, other], 0), jnp.concatenate([other, mine], 0)
        )

    def own(values):
        return lax.dynamic_slice_in_dim(values, core * half_rows, half_rows, 0)

    def others(values):
        return lax.dynamic_slice_in_dim(values, (1 - core) * half_rows, half_rows, 0)

    def join(partial):
        return full(partial) + full(swap(partial))

    def own_sum(partial):
        return full(own(partial)) + full(swap(others(partial)))

    live = (jnp.arange(rows) < length).astype(F32)[:, None]
    x0 = full(whole(tokens))
    g4 = full(whole(cotangent)) * live

    n1 = norm_forward(x0, norm1_gain, norm1_shift)
    joined = dot(n1, qkv1_weight.reshape(model, 3 * local))
    q1 = half(joined[:, :local] + full(qv1_bias[0]))
    k1 = half(joined[:, local : 2 * local])
    v1 = half(joined[:, 2 * local :] + full(qv1_bias[1]))
    o1 = attend(q1, k1, v1, length)
    x1 = x0 + join(half(dot(o1, out1_weight))) + full(out1_bias)
    m1 = norm_forward(x1, norm2_gain, norm2_shift)
    z1, pull1 = gelu_both(dot(m1, fc1_weight) + full(fc1_bias))
    z1, pull1 = half(z1), half(pull1)
    x2 = x1 + join(half(dot(z1, proj1_weight))) + full(proj1_bias)

    n3 = norm_forward(x2, norm3_gain, norm3_shift)
    joined = dot(n3, qk2_weight.reshape(model, 2 * local))
    q2 = half(joined[:, :local] + full(q2_bias))
    k2 = half(joined[:, local:])
    f2 = half(dot(n3, v2_weight) + full(v2_bias))
    v2 = jnp.concatenate([f2, v1[:, fresh:]], axis=1)
    o2 = attend(q2, k2, v2, length)
    x3 = x2 + join(half(dot(o2, out2_weight))) + full(out2_bias)
    m3 = norm_forward(x3, norm4_gain, norm4_shift)
    z3, pull3 = gelu_both(dot(m3, fc2_weight) + full(fc2_bias))
    z3 = half(z3)
    x4_part = half(dot(z3, proj2_weight))

    gb4 = half(g4)
    du3 = half(dot_nt(gb4, proj2_weight) * pull3)
    dm3 = join(half(dot_nt(du3, fc2_weight)))
    layer_output = half((own(x3) + own_sum(x4_part) + full(proj2_bias)) * own(live))
    sum_fc2 = scatter_sum(half(dot_tn(m3, du3)), order_a, count)
    sum_proj2 = scatter_sum(half(dot_tn(gb4, z3)), order_b, count).T
    fc2_bias_grad = jnp.sum(full(du3), axis=0)
    proj2_bias_grad = jnp.sum(g4, axis=0)

    pulled, gain4_grad, shift4_grad = norm_backward(dm3, x3, norm4_gain)
    g3 = g4 + pulled
    gb3 = half(g3)
    do2 = half(dot_nt(gb3, out2_weight))
    dq2, dk2, dv2 = attend_backward(q2, k2, v2, do2, length)
    dq2, dk2, df2, reused = half(dq2), half(dk2), half(dv2[:, :fresh]), dv2[:, fresh:]
    dn3 = join(
        half(dot_nt(dq2, qk2_weight[:, 0]) + dot_nt(dk2, qk2_weight[:, 1]) + dot_nt(df2, v2_weight))
    )
    dqk2 = jnp.concatenate([dq2, dk2], axis=1)
    sum_qk2 = scatter_sum(half(dot_tn(n3, dqk2)), order_a, count)
    sum_qk2 = sum_qk2.reshape(sum_qk2.shape[0], 2, local)
    second = half(jnp.concatenate([dot_tn(gb3, o2), dot_tn(n3, df2)], axis=1))
    second = scatter_sum(second, order_b, count)
    sum_out2, sum_v2 = second[:, :local].T, second[:, local:]
    q2_bias_grad = jnp.sum(full(dq2), axis=0)
    v2_bias_grad = jnp.sum(full(df2), axis=0)
    out2_bias_grad = jnp.sum(g3, axis=0)

    pulled, gain3_grad, shift3_grad = norm_backward(dn3, x2, norm3_gain)
    g2 = g3 + pulled
    gb2 = half(g2)
    du1 = half(dot_nt(gb2, proj1_weight) * full(pull1))
    dm1 = join(half(dot_nt(du1, fc1_weight)))
    sum_fc1 = scatter_sum(half(dot_tn(m1, du1)), order_a, count)
    sum_proj1 = scatter_sum(half(dot_tn(gb2, z1)), order_b, count).T
    fc1_bias_grad = jnp.sum(full(du1), axis=0)
    proj1_bias_grad = jnp.sum(g2, axis=0)

    pulled, gain2_grad, shift2_grad = norm_backward(dm1, x1, norm2_gain)
    g1 = g2 + pulled
    gb1 = half(g1)
    do1 = half(dot_nt(gb1, out1_weight))
    dq1, dk1, dv1 = attend_backward(q1, k1, v1, do1, length)
    dq1, dk1 = half(dq1), half(dk1)
    dv1 = half(jnp.concatenate([dv1[:, :fresh], dv1[:, fresh:] + reused], axis=1))
    dn1_part = half(
        dot_nt(dq1, qkv1_weight[:, 0]) + dot_nt(dk1, qkv1_weight[:, 1]) + dot_nt(dv1, qkv1_weight[:, 2])
    )
    dn1 = own_sum(dn1_part)
    first = half(dot_tn(n1, jnp.concatenate([dq1, dk1], axis=1)))
    first = scatter_sum(first, order_a, count)
    second = half(jnp.concatenate([dot_tn(n1, dv1), dot_tn(gb1, o1)], axis=1))
    second = scatter_sum(second, order_b, count)
    sum_qkv1 = jnp.concatenate([first, second[:, :local]], axis=1)
    sum_qkv1 = sum_qkv1.reshape(sum_qkv1.shape[0], 3, local)
    sum_out1 = second[:, local:].T
    qv1_bias_grad = jnp.concatenate([jnp.sum(full(dq1), axis=0), jnp.sum(full(dv1), axis=0)])
    out1_bias_grad = jnp.sum(g1, axis=0)
    pulled, gain1_part, shift1_part = norm_backward(dn1, own(x0), norm1_gain)
    tokens_grad = half(own(g1) + pulled)

    equal = (
        gain4_grad, shift4_grad, proj2_bias_grad, gain3_grad, shift3_grad, out2_bias_grad,
        gain2_grad, shift2_grad, proj1_bias_grad, out1_bias_grad,
    )
    split = (fc2_bias_grad, q2_bias_grad, v2_bias_grad, fc1_bias_grad, qv1_bias_grad)
    halves = jnp.concatenate([gain1_part, shift1_part])
    halves = halves + swap(halves)
    vector = all_sum(jnp.concatenate(equal + (halves,) + split), count)
    starts = [0]
    for part in equal + (halves,) + split:
        starts.append(starts[-1] + part.shape[0])
    mine = vector[starts[len(equal) + 1] :]
    other = swap(mine)
    pair = jnp.where(core == 0, jnp.stack([mine, other]), jnp.stack([other, mine]))
    same = [vector[starts[i] : starts[i + 1]] for i in range(len(equal))]
    sum_gain4, sum_shift4, sum_proj2_bias, sum_gain3, sum_shift3, sum_out2_bias = same[:6]
    sum_gain2, sum_shift2, sum_proj1_bias, sum_out1_bias = same[6:]
    ends = vector[starts[len(equal)] : starts[len(equal) + 1]]
    sum_gain1, sum_shift1 = ends[:model], ends[model:]
    base = starts[len(equal) + 1]
    cut = [
        pair[:, starts[len(equal) + 1 + i] - base : starts[len(equal) + 2 + i] - base]
        for i in range(len(split))
    ]
    sum_fc2_bias, sum_q2_bias, sum_v2_bias, sum_fc1_bias = (part.reshape(-1) for part in cut[:4])
    sum_qv1_bias = cut[4].reshape(2, 2, local).transpose(1, 0, 2).reshape(2, 2 * local)
    return (
        layer_output, tokens_grad, sum_gain1, sum_shift1, sum_qkv1, sum_qv1_bias, sum_out1, sum_out1_bias,
        sum_gain2, sum_shift2, sum_fc1, sum_fc1_bias, sum_proj1, sum_proj1_bias, sum_gain3, sum_shift3, sum_qk2,
        sum_v2, sum_q2_bias, sum_v2_bias, sum_out2, sum_out2_bias, sum_gain4, sum_shift4, sum_fc2, sum_fc2_bias,
        sum_proj2, sum_proj2_bias,
    )


def solution(mesh):
    rows, copied = P(("seq", "tp"), None), P()
    columns, deep = P(None, "tp"), P("tp", None)
    wide, long = P("seq", "tp"), P("tp", "seq")
    count = mesh.shape["seq"]

    def body(*arguments):
        return on_device(count, *arguments)

    return jax.shard_map(
        body,
        mesh=mesh,
        in_specs=(
            rows, P("seq"), rows, copied, copied, P(None, None, "tp"), columns, deep, copied,
            copied, copied, columns, P("tp"), deep, copied, copied, copied,
            P(None, None, "tp"), columns, P("tp"), P("tp"), deep, copied, copied, copied, columns,
            P("tp"), deep, copied,
        ),
        out_specs=(
            rows, rows, copied, copied, P("seq", None, "tp"), copied, long, copied,
            copied, copied, wide, copied, long, copied, copied, copied, P("seq", None, "tp"),
            wide, copied, copied, long, copied, copied, copied, wide, copied,
            long, copied,
        ),
        check_vma=False,
    )
```

```python
import functools

import jax
import jax.numpy as jnp
import numpy as np
from jax import lax
from jax.experimental import pallas as pl
from jax.experimental.pallas import tpu as pltpu
from jax.sharding import PartitionSpec as P

HEAD_DIM = 64
F32 = jnp.float32
BF16 = jnp.bfloat16


def half(values):
    return values.astype(BF16)


def full(values):
    return values.astype(F32)


def dot(left, right):
    return lax.dot_general(left, right, (((1,), (0,)), ((), ())), preferred_element_type=F32)


def dot_nt(left, right):
    return lax.dot_general(left, right, (((1,), (1,)), ((), ())), preferred_element_type=F32)


def dot_tn(left, right):
    return lax.dot_general(left, right, (((0,), (0,)), ((), ())), preferred_element_type=F32)


def swap(values):
    return lax.ppermute(values, "tp", [(0, 1), (1, 0)])


QUERY_BLOCK, KEY_BLOCK = 512, 256
HIDDEN_CUT = 3
VMEM_BYTES = 56 * 1024 * 1024


class Arriving:
    def __init__(self, source, buffer, sems, first, cut):
        self.source, self.buffer, self.shape, self.dtype = source, buffer, source.shape, source.dtype
        axis, count = cut
        size = source.shape[axis] // count
        self.copies = []
        for index in range(count):
            at = (slice(None),) * axis + (pl.ds(index * size, size),)
            here, there = (source, buffer) if count == 1 else (source.at[at], buffer.at[at])
            self.copies.append(pltpu.make_async_copy(here, there, sems.at[first + index]))
        self.waiting = set(range(count))

    def start(self):
        for copy in self.copies:
            copy.start()

    def piece(self, index):
        if index in self.waiting:
            self.waiting.remove(index)
            self.copies[index].wait()
        return self.buffer

    def whole(self):
        for index in range(len(self.copies)):
            self.piece(index)
        return self.buffer

    def __getitem__(self, at):
        return self.whole()[at]


class Leaving:
    def __init__(self, target, buffer, sems, first, cut):
        self.target, self.buffer, self.shape, self.dtype = target, buffer, target.shape, target.dtype
        axis, count = cut
        size = target.shape[axis] // count
        self.copies = []
        for index in range(count):
            at = (slice(None),) * axis + (pl.ds(index * size, size),)
            here, there = (buffer, target) if count == 1 else (buffer.at[at], target.at[at])
            self.copies.append(pltpu.make_async_copy(here, there, sems.at[first + index]))
        self.held = set(range(count))

    def send(self, index=0):
        self.held.remove(index)
        self.copies[index].start()

    def finish(self):
        for index in sorted(self.held):
            self.send(index)

    def __getitem__(self, at):
        return self.buffer[at]

    def __setitem__(self, at, value):
        self.buffer[at] = value


SCALARS, AFTER, LATE = "scalars", "after", (0, 1)


TOLD = 1.0


def call(body, outs, ins, cuts=None, scratch=(), cost=1.0):
    single = not isinstance(outs, (list, tuple))
    outs = [outs] if single else list(outs)
    cuts = list(cuts) if cuts is not None else [LATE] * len(outs)
    late = [index for index, kind in enumerate(ins) if isinstance(kind, tuple)]
    in_counts = [ins[index][1] for index in late]
    out_counts = [count for _, count in cuts]

    def wrapped(*refs):
        refs = list(refs)
        operands, refs = refs[: len(ins)], refs[len(ins) :]
        targets, refs = refs[: len(outs)], refs[len(outs) :]
        extra, refs = refs[: len(scratch)], refs[len(scratch) :]
        in_buffers, refs = refs[: len(late)], refs[len(late) :]
        out_buffers, (in_sems, out_sems) = refs[: len(outs)], refs[len(outs) :]
        arriving = {
            index: Arriving(operands[index], in_buffers[at], in_sems, sum(in_counts[:at]), ins[index])
            for at, index in enumerate(late)
        }
        for operand in arriving.values():
            operand.start()
        leaving = [
            Leaving(target, out_buffers[at], out_sems, sum(out_counts[:at]), cuts[at])
            for at, target in enumerate(targets)
        ]
        given = [
            arriving[index] if index in arriving else operands[index]
            for index, kind in enumerate(ins)
            if kind != AFTER
        ]
        body(*given, *leaving, *extra)
        for operand in arriving.values():
            operand.whole()
        for result in leaving:
            result.finish()
        for result in leaving:
            for copy in result.copies:
                copy.wait()

    def run(*operands):
        buffers = [pltpu.VMEM(operands[index].shape, operands[index].dtype) for index in late]
        buffers += [pltpu.VMEM(out.shape, out.dtype) for out in outs]
        sems = [pltpu.SemaphoreType.DMA((sum(in_counts),)), pltpu.SemaphoreType.DMA((sum(out_counts),))]
        results = pl.pallas_call(
            wrapped,
            out_shape=outs,
            in_specs=[
                pl.BlockSpec(memory_space=pltpu.SMEM if kind == SCALARS else pltpu.HBM) for kind in ins
            ],
            out_specs=[pl.BlockSpec(memory_space=pltpu.HBM)] * len(outs),
            scratch_shapes=list(scratch) + buffers + sems,
            compiler_params=pltpu.CompilerParams(vmem_limit_bytes=VMEM_BYTES),
            cost_estimate=pl.CostEstimate(
                flops=int(cost * TOLD * 1.1e9), bytes_accessed=int(cost * TOLD * 3.4e6), transcendentals=0
            ),
        )(*operands)
        return results[0] if single else results

    return run


def shaped(shape, kind=BF16):
    return jax.ShapeDtypeStruct(shape, kind)


def row(ref):
    return full(ref[...][None, :])


def norm_stats(values):
    mean = jnp.mean(values, axis=-1, keepdims=True)
    centered = values - mean
    scale = lax.rsqrt(jnp.mean(centered * centered, axis=-1, keepdims=True) + 1e-05)
    return centered * scale, scale


def norm_backward(grad, values, gain):
    hat, scale = norm_stats(values)
    inner = grad * gain
    mean_inner = jnp.mean(inner, axis=-1, keepdims=True)
    mean_hat = jnp.mean(inner * hat, axis=-1, keepdims=True)
    pulled = scale * (inner - mean_inner - hat * mean_hat)
    return (
        pulled,
        jnp.sum(grad * hat, axis=0, keepdims=True),
        jnp.sum(grad, axis=0, keepdims=True),
    )


def gelu_both(values):
    square = values * values
    bent = jnp.tanh(values * (0.7978845608028654 + 0.035677408136300125 * square))
    rise = 0.5 + 0.5 * bent
    slope = 0.7978845608028654 + 0.10703222440890038 * square
    pull = rise + (0.5 * values) * (1.0 - bent * bent) * slope
    return values * rise, pull


def head_lanes(width, which):
    lane = lax.broadcasted_iota(jnp.int32, (1, width), 1)
    return (lane // HEAD_DIM) == which


def keep_lanes(values, lanes):
    return jnp.where(lanes, values, jnp.zeros_like(values))


def fill_bias(bias_ref, length, transposed):
    blocks = bias_ref.shape[0]
    key_dim, query_dim = (0, 1) if transposed else (1, 0)
    size = bias_ref.shape[1]
    shape = (size, size)
    key = lax.broadcasted_iota(jnp.int32, shape, key_dim)
    query = lax.broadcasted_iota(jnp.int32, shape, query_dim)
    for block in range(blocks):
        allowed = (key <= query) & (key + block * size < length)
        bias_ref[block] = jnp.where(allowed, 0.0, -1e30)


def attend_rows(q_ref, k_ref, v_ref, o_ref, bias_ref, length):
    rows, width = q_ref.shape
    for pair in range(width // 128):
        lanes = slice(pair * 128, pair * 128 + 128)
        keys, values = k_ref[:, lanes], v_ref[:, lanes]
        heads = [head_lanes(128, which) for which in range(2)]
        head_values = [keep_lanes(values, mask) for mask in heads]
        for block in range(rows // QUERY_BLOCK):
            start, stop = block * QUERY_BLOCK, (block + 1) * QUERY_BLOCK
            query = q_ref[start:stop, lanes] * 0.125
            column = lax.broadcasted_iota(jnp.int32, (1, max(start, 1)), 1)
            edge = jnp.where(column < length, 0.0, -1e30)
            total = None
            for which in range(2):
                part = keep_lanes(query, heads[which]).astype(BF16)
                scores = dot_nt(part, keys[start:stop]) + bias_ref[block]
                largest = jnp.max(scores, axis=-1, keepdims=True)
                if start:
                    before = dot_nt(part, keys[:start]) + edge
                    largest = jnp.maximum(largest, jnp.max(before, axis=-1, keepdims=True))
                weights = jnp.exp(scores - largest)
                norm = jnp.sum(weights, axis=-1, keepdims=True)
                mixed = dot(half(weights), head_values[which][start:stop])
                if start:
                    weights = jnp.exp(before - largest)
                    norm = norm + jnp.sum(weights, axis=-1, keepdims=True)
                    mixed = mixed + dot(half(weights), head_values[which][:start])
                mixed = mixed * (1.0 / norm)
                total = mixed if total is None else total + mixed
            o_ref[start:stop, lanes] = half(total)


def attend_first(scal_ref, mine_ref, other_ref, gain_ref, shift_ref, bias_refs, w_ref, out_ref,
                 x_ref, n_ref, q_ref, k_ref, v_ref, o_ref, part_ref, bias_ref):
    core, length = scal_ref[0], scal_ref[1]
    mid = mine_ref.shape[0]
    x_ref[pl.ds(pl.multiple_of(core * mid, mid), mid), :] = mine_ref[...]
    x_ref[pl.ds(pl.multiple_of((1 - core) * mid, mid), mid), :] = other_ref[...]
    fill_bias(bias_ref, length, False)
    hat, _ = norm_stats(full(x_ref[...]))
    normed = half(hat * row(gain_ref) + row(shift_ref))
    n_ref[...] = normed
    x_ref.send()
    n_ref.send()
    q_ref[...] = half(dot(normed, w_ref[0]) + full(bias_refs[0:1, :]))
    k_ref[...] = half(dot(normed, w_ref[1]))
    v_ref[...] = half(dot(normed, w_ref[2]) + full(bias_refs[1:2, :]))
    for ref in (q_ref, k_ref, v_ref):
        ref.send()
    attend_rows(q_ref, k_ref, v_ref, o_ref, bias_ref, length)
    part_ref[...] = half(dot(o_ref[...], out_ref[...]))


def attend_second(scal_ref, prev_ref, mine_ref, other_ref, before_ref, gain_ref, shift_ref, qb_ref, fb_ref,
                  w_ref, f_ref, v1_ref, out_ref,
                  x_ref, n_ref, q_ref, k_ref, v_ref, o_ref, part_ref, bias_ref):
    length = scal_ref[1]
    x_ref[...] = prev_ref[...] + (full(mine_ref[...]) + full(other_ref[...])) + row(before_ref)
    fill_bias(bias_ref, length, False)
    hat, _ = norm_stats(x_ref[...])
    normed = half(hat * row(gain_ref) + row(shift_ref))
    n_ref[...] = normed
    x_ref.send()
    n_ref.send()
    fresh = f_ref.shape[0]
    q_ref[...] = half(dot(normed, w_ref[0]) + row(qb_ref))
    k_ref[...] = half(dot(normed, w_ref[1]))
    v_ref[...] = v1_ref[...]
    v_ref[:, :fresh] = half(dot_nt(normed, f_ref[...]) + row(fb_ref))
    for ref in (q_ref, k_ref, v_ref):
        ref.send()
    attend_rows(q_ref, k_ref, v_ref, o_ref, bias_ref, length)
    part_ref[...] = half(dot(o_ref[...], out_ref[...]))


def attend_pull(q_ref, k_ref, v_ref, do_ref, dq_ref, dk_ref, dv_ref, bias_ref, length, dk_sum, dv_sum):
    rows, width = q_ref.shape
    for pair in range(width // 128):
        lanes = slice(pair * 128, pair * 128 + 128)
        keys, values = k_ref[:, lanes], v_ref[:, lanes]
        turned = full(keys).T
        turned = [half(turned[which * HEAD_DIM : (which + 1) * HEAD_DIM]) for which in range(2)]
        heads = [head_lanes(128, which) for which in range(2)]
        dk_sum[...] = jnp.zeros_like(dk_sum)
        dv_sum[...] = jnp.zeros_like(dv_sum)
        for block in range(rows // KEY_BLOCK):
            start, stop = block * KEY_BLOCK, (block + 1) * KEY_BLOCK
            query = q_ref[start:stop, lanes] * 0.125
            grad = do_ref[start:stop, lanes]
            place = lax.broadcasted_iota(jnp.int32, (max(start, 8), 1), 0)
            edge = jnp.where(place < length, 0.0, -1e30)
            pulled_query = []
            for which in range(2):
                part = keep_lanes(query, heads[which]).astype(BF16)
                part_grad = keep_lanes(grad, heads[which])
                spans = [(start, stop, bias_ref[block])] + ([(0, start, edge)] if start else [])
                scores = [dot_nt(keys[low:high], part) + bias for low, high, bias in spans]
                largest = jnp.max(scores[0], axis=0, keepdims=True)
                for score in scores[1:]:
                    largest = jnp.maximum(largest, jnp.max(score, axis=0, keepdims=True))
                weights = [jnp.exp(score - largest) for score in scores]
                norm = sum(jnp.sum(weight, axis=0, keepdims=True) for weight in weights)
                inverse = 1.0 / norm
                weights = [weight * inverse for weight in weights]
                pulled = [dot_nt(values[low:high], part_grad) for low, high, _ in spans]
                centre = sum(
                    jnp.sum(pull * weight, axis=0, keepdims=True) for pull, weight in zip(pulled, weights)
                )
                query_sum = None
                for (low, high, _), weight, pull in zip(spans, weights, pulled):
                    score_grad = half(weight * (pull - centre))
                    dv_sum[low:high, :] += dot(half(weight), part_grad)
                    dk_sum[low:high, :] += dot(score_grad, part)
                    term = dot(turned[which][:, low:high], score_grad)
                    query_sum = term if query_sum is None else query_sum + term
                pulled_query.append(query_sum)
            joined = jnp.concatenate(pulled_query, axis=0) * 0.125
            dq_ref[start:stop, lanes] = half(joined.T)
        dk_ref[:, lanes] = half(dk_sum[...])
        dv_ref[:, lanes] = dv_sum[...]


def column_sum(values):
    return jnp.sum(full(values), axis=0, keepdims=True)


def pull_second(scal_ref, g4_ref, mine_ref, other_ref, x_ref, gain_ref, q_ref, k_ref, v_ref, w_ref, f_ref, out_ref,
                g_ref, gb_ref, dq_ref, dk_ref, dv_ref, dvb_ref, part_ref, rep_ref, loc_ref,
                do_ref, bias_ref, dk_sum, dv_sum):
    length = scal_ref[1]
    fill_bias(bias_ref, length, True)
    grad = full(mine_ref[...]) + full(other_ref[...])
    pulled, gain, shift = norm_backward(grad, x_ref[...], row(gain_ref))
    g_ref[...] = full(g4_ref[...]) + pulled
    rep_ref[...] = jnp.zeros_like(rep_ref)
    loc_ref[...] = jnp.zeros_like(loc_ref)
    rep_ref[0:1, :] = gain
    rep_ref[1:2, :] = shift
    rep_ref[2:3, :] = column_sum(g_ref[...])
    gb_ref[...] = half(g_ref[...])
    g_ref.send()
    gb_ref.send()
    do_ref[...] = half(dot_nt(gb_ref[...], out_ref[...]))
    attend_pull(q_ref, k_ref, v_ref, do_ref, dq_ref, dk_ref, dv_ref, bias_ref, length, dk_sum, dv_sum)
    fresh = f_ref.shape[0]
    dvb_ref[...] = half(dv_ref[...])
    fresh_grad = dvb_ref[:, :fresh]
    part_ref[...] = half(
        dot_nt(dq_ref[...], w_ref[0]) + dot_nt(dk_ref[...], w_ref[1]) + dot(fresh_grad, f_ref[...])
    )
    loc_ref[0:1, :] = column_sum(dq_ref[...])
    loc_ref[1:2, :] = column_sum(dvb_ref[...])


def pull_first(scal_ref, g2_ref, mine_ref, other_ref, x_ref, gain_ref, q_ref, k_ref, v_ref, w_ref, reused_ref, out_ref,
               g_ref, gb_ref, dq_ref, dk_ref, dv_ref, part_ref, rep_ref, loc_ref,
               do_ref, bias_ref, dk_sum, dv_sum, dv_full, *, fresh):
    length = scal_ref[1]
    fill_bias(bias_ref, length, True)
    grad = full(mine_ref[...]) + full(other_ref[...])
    pulled, gain, shift = norm_backward(grad, x_ref[...], row(gain_ref))
    g_ref[...] = g2_ref[...] + pulled
    rep_ref[...] = jnp.zeros_like(rep_ref)
    loc_ref[...] = jnp.zeros_like(loc_ref)
    rep_ref[0:1, :] = gain
    rep_ref[1:2, :] = shift
    rep_ref[2:3, :] = column_sum(g_ref[...])
    gb_ref[...] = half(g_ref[...])
    g_ref.send()
    gb_ref.send()
    do_ref[...] = half(dot_nt(gb_ref[...], out_ref[...]))
    attend_pull(q_ref, k_ref, v_ref, do_ref, dq_ref, dk_ref, dv_full, bias_ref, length, dk_sum, dv_sum)
    column = lax.broadcasted_iota(jnp.int32, (1, dv_full.shape[1]), 1)
    dv_ref[...] = half(dv_full[...] + jnp.where(column >= fresh, reused_ref[...], 0.0))
    part_ref[...] = half(
        dot_nt(dq_ref[...], w_ref[0]) + dot_nt(dk_ref[...], w_ref[1]) + dot_nt(dv_ref[...], w_ref[2])
    )
    loc_ref[0:1, :] = column_sum(dq_ref[...])
    loc_ref[1:2, :] = column_sum(dv_ref[...])


ROW_BLOCK = 256


def hidden_spans(ref):
    size = ref.shape[1] // HIDDEN_CUT
    return [slice(index * size, (index + 1) * size) for index in range(HIDDEN_CUT)]


def add_to(total, span, value, fresh):
    total[span, :] = value if fresh else total[span, :] + value


def feed_first(prev_ref, mine_ref, other_ref, before_ref, gain_ref, shift_ref, bias_ref, fc_ref, proj_ref,
               x_ref, m_ref, z_ref, pull_ref, part_ref, total):
    x_ref[...] = full(prev_ref[...]) + (full(mine_ref[...]) + full(other_ref[...])) + row(before_ref)
    x_ref.send()
    hat, _ = norm_stats(x_ref[...])
    m_ref[...] = half(hat * row(gain_ref) + row(shift_ref))
    m_ref.send()
    for index, columns in enumerate(hidden_spans(fc_ref)):
        fc, proj = fc_ref.piece(index), proj_ref.piece(index)
        bias = full(bias_ref[columns][None, :])
        for low in range(0, m_ref.shape[0], ROW_BLOCK):
            span = slice(low, low + ROW_BLOCK)
            value, pull = gelu_both(dot(m_ref[span, :], fc[:, columns]) + bias)
            value = half(value)
            z_ref[span, columns] = value
            pull_ref[span, columns] = half(pull)
            add_to(total, span, dot(value, proj[columns, :]), index == 0)
        z_ref.send(index)
        pull_ref.send(index)
    part_ref[...] = half(total[...])


def feed_second(scal_ref, prev_ref, mine_ref, other_ref, before_ref, gain_ref, shift_ref, bias_ref,
                cot_ref, cot_other_ref, fc_ref, proj_ref,
                x_ref, m_ref, g_ref, z_ref, du_ref, part_ref, pulled_ref, rep_ref, loc_ref, total, pulled_total):
    core, length = scal_ref[0], scal_ref[1]
    x_ref[...] = prev_ref[...] + (full(mine_ref[...]) + full(other_ref[...])) + row(before_ref)
    x_ref.send()
    hat, _ = norm_stats(x_ref[...])
    m_ref[...] = half(hat * row(gain_ref) + row(shift_ref))
    m_ref.send()
    mid = cot_ref.shape[0]
    place = lax.broadcasted_iota(jnp.int32, (mid, 1), 0)
    for source, owner in ((cot_ref, core), (cot_other_ref, 1 - core)):
        base = pl.multiple_of(owner * mid, mid)
        alive = (place + base < length).astype(F32)
        g_ref[pl.ds(base, mid), :] = half(full(source[...]) * alive)
    g_ref.send()
    rep_ref[...] = jnp.zeros_like(rep_ref)
    loc_ref[...] = jnp.zeros_like(loc_ref)
    rep_ref[0:1, :] = column_sum(g_ref[...])
    for index, columns in enumerate(hidden_spans(fc_ref)):
        fc, proj = fc_ref.piece(index), proj_ref.piece(index)
        bias = full(bias_ref[columns][None, :])
        sums = None
        for low in range(0, m_ref.shape[0], ROW_BLOCK):
            span = slice(low, low + ROW_BLOCK)
            value, pull = gelu_both(dot(m_ref[span, :], fc[:, columns]) + bias)
            value = half(value)
            z_ref[span, columns] = value
            add_to(total, span, dot(value, proj[columns, :]), index == 0)
            du = half(dot_nt(g_ref[span, :], proj[columns, :]) * pull)
            du_ref[span, columns] = du
            add_to(pulled_total, span, dot_nt(du, fc[:, columns]), index == 0)
            sums = column_sum(du) if sums is None else sums + column_sum(du)
        loc_ref[0:1, columns] = sums
        z_ref.send(index)
        du_ref.send(index)
    part_ref[...] = half(total[...])
    pulled_ref[...] = half(pulled_total[...])


def feed_pull(g3_ref, mine_ref, other_ref, xin_ref, gain_ref, pull_ref, fc_ref, proj_ref,
              g_ref, gb_ref, du_ref, pulled_ref, rep_ref, loc_ref, pulled_total):
    grad = full(mine_ref[...]) + full(other_ref[...])
    pulled, gain, shift = norm_backward(grad, xin_ref[...], row(gain_ref))
    g_ref[...] = g3_ref[...] + pulled
    g_ref.send()
    rep_ref[...] = jnp.zeros_like(rep_ref)
    loc_ref[...] = jnp.zeros_like(loc_ref)
    rep_ref[0:1, :] = gain
    rep_ref[1:2, :] = shift
    rep_ref[2:3, :] = column_sum(g_ref[...])
    gb_ref[...] = half(g_ref[...])
    gb_ref.send()
    for index, columns in enumerate(hidden_spans(fc_ref)):
        fc, proj = fc_ref.piece(index), proj_ref.piece(index)
        pull = pull_ref.piece(index)
        sums = None
        for low in range(0, gb_ref.shape[0], ROW_BLOCK):
            span = slice(low, low + ROW_BLOCK)
            du = half(dot_nt(gb_ref[span, :], proj[columns, :]) * full(pull[span, columns]))
            du_ref[span, columns] = du
            add_to(pulled_total, span, dot_nt(du, fc[:, columns]), index == 0)
            sums = column_sum(du) if sums is None else sums + column_sum(du)
        loc_ref[0:1, columns] = sums
        du_ref.send(index)
    pulled_ref[...] = half(pulled_total[...])


PACKED, SHARED = 24, 10


def pull_tokens(scal_ref, g1_ref, mine_ref, other_ref, x_ref, gain_ref,
                rep4_ref, rep3_ref, rep2_ref, rep1_ref, loc4_ref, loc3_ref, loc2_ref, loc1_ref,
                out_ref, pack_ref):
    mid, model = out_ref.shape
    own = pl.ds(pl.multiple_of(scal_ref[0] * mid, mid), mid)
    grad = full(mine_ref[own, :]) + full(other_ref[...])
    pulled, gain, shift = norm_backward(grad, full(x_ref[own, :]), row(gain_ref))
    out_ref[...] = half(g1_ref[own, :] + pulled)
    pack_ref[...] = jnp.zeros_like(pack_ref)
    pack_ref[0:1, :] = rep4_ref[0:1, :]
    for index, ref in enumerate((rep3_ref, rep2_ref, rep1_ref)):
        pack_ref[1 + 3 * index : 4 + 3 * index, :] = ref[0:3, :]
    pack_ref[SHARED : SHARED + 1, :] = gain
    pack_ref[SHARED + 1 : SHARED + 2, :] = shift
    for index, ref in enumerate((loc4_ref, loc2_ref)):
        for part in range(2):
            at = SHARED + 2 + 2 * index + part
            pack_ref[at : at + 1, :] = ref[0:1, part * model : (part + 1) * model]
    for index, ref in enumerate((loc3_ref, loc1_ref)):
        at = SHARED + 6 + index
        for part in range(2):
            pack_ref[at : at + 1, part * model // 2 : (part + 1) * model // 2] = ref[part : part + 1, :]


def unpack_sums(scal_ref, mine_ref, other_ref, *outs):
    first = scal_ref[0] == 0
    (gain1, shift1, qv1, out1, gain2, shift2, fc1, proj1,
     gain3, shift3, q2, v2, out2, gain4, shift4, fc2, proj2) = outs
    same = (proj2, gain4, shift4, out2, gain3, shift3, proj1, gain2, shift2, out1)
    for index, ref in enumerate(same):
        ref[...] = mine_ref[index, :]
    for index, ref in enumerate((gain1, shift1)):
        ref[...] = mine_ref[SHARED + index, :] + other_ref[SHARED + index, :]
    model = gain1.shape[0]

    def both(at):
        mine, other = mine_ref[at : at + 1, :], other_ref[at : at + 1, :]
        return jnp.where(first, mine, other), jnp.where(first, other, mine)

    for index, ref in enumerate((fc2, fc1)):
        for part in range(2):
            for core, value in enumerate(both(SHARED + 2 + 2 * index + part)):
                at = (2 * core + part) * model
                ref[at : at + model] = value[0]
    low, high = both(SHARED + 6)
    middle = model // 2
    q2[:middle] = low[0, :middle]
    q2[middle:] = high[0, :middle]
    fresh = v2.shape[0] // 2
    v2[...] = jnp.concatenate([low[:, middle : middle + fresh], high[:, middle : middle + fresh]], axis=1)[0]
    low, high = both(SHARED + 7)
    for part in range(2):
        span = slice(part * middle, (part + 1) * middle)
        qv1[part : part + 1, :middle] = low[:, span]
        qv1[part : part + 1, middle:] = high[:, span]


def finish_layer(scal_ref, x_ref, mine_ref, other_ref, before_ref, out_ref):
    mid = out_ref.shape[0]
    base = pl.multiple_of(scal_ref[0] * mid, mid)
    own = pl.ds(base, mid)
    total = x_ref[own, :] + (full(mine_ref[own, :]) + full(other_ref[...])) + row(before_ref)
    place = lax.broadcasted_iota(jnp.int32, (mid, 1), 0)
    out_ref[...] = half(total * (place + base < scal_ref[1]).astype(F32))


FIRST_ORDERS = ((0, 1, 2), (1, 2, 0))
SECOND_ORDERS = ((1, 0, 2), (2, 1, 0))
THIRD_ORDERS = ((2, 0, 1), (0, 1, 2))
FOURTH_ORDERS = ((0, 1, 2), (1, 0, 2))


def bit_orders(orders, bits):
    return [[bit for bit in order if bit < bits] + list(range(3, bits)) for order in orders]


def row_table(orders, count):
    bits = count.bit_length() - 1
    table = np.zeros((count, 2, count), np.int32)
    for core, order in enumerate(bit_orders(orders, bits)):
        for me in range(count):
            for block in range(count):
                place = 0
                for bit in order:
                    place = 2 * place + (((block ^ me) >> bit) & 1)
                table[me, core, block] = place
    return table.reshape(count * 2, count)


def fold_pairs(orders, count, phase):
    bits = count.bit_length() - 1
    pairs = []
    for core, order in enumerate(bit_orders(orders, bits)):
        for me in range(count):
            pairs.append((2 * me + core, 2 * (me ^ (1 << order[phase])) + core))
    return pairs


def weight_grads(scalars, orders, count, rows_a, rights_a, rows_b, rights_b, width, after):
    rights = list(rights_a) + list(rights_b)
    block = 768 if all(right.shape[1] % 768 == 0 for right in rights) else 128
    depth, model = rows_a.shape
    span = model // count
    bits = count.bit_length() - 1
    lists = bit_orders(orders, bits)

    def body(scal_ref, rows_a_ref, *refs):
        right_refs, rows_b_ref = refs[: len(rights_a)], refs[len(rights_a)]
        right_refs += refs[len(rights_a) + 1 : len(rights) + 1]
        keep_ref, send_ref, turned = refs[len(rights) + 1 :]
        core, me = scal_ref[0], scal_ref[2]

        def turn(ref):
            columns = ref[...].T
            for index in range(count):
                apart = index ^ me
                places = [
                    sum(((apart >> bit) & 1) << (bits - 1 - at) for at, bit in enumerate(order)) for order in lists
                ]
                place = jnp.where(core == 0, places[0], places[1])
                at = pl.ds(pl.multiple_of(place * span, 16), span)
                turned[at, :] = columns[index * span : (index + 1) * span]

        turn(rows_a_ref)
        start = 0
        for index, ref in enumerate(right_refs):
            if index == len(rights_a):
                turn(rows_b_ref)
            size = min(ref.shape[1], width - start)
            step = min(size, 768)
            for low in range(0, size, step):
                columns = slice(low, low + step)
                at = slice(start + low, start + low + step)
                right = ref[:, columns] if len(ref.copies) == 1 else ref.piece(low // step)[:, columns]
                send_ref[:, at] = half(dot(turned[model // 2 :, :], right))
                keep_ref[:, at] = half(dot(turned[: model // 2, :], right))
                for piece in range((start + low) // block, (start + low + step) // block):
                    send_ref.send(piece)
                    keep_ref.send(piece)
            start += size

    cut = [(1, max(1, right.shape[1] // 768)) for right in rights]
    pieces = (1, width // block)
    return call(
        body,
        [shaped((model // 2, width))] * 2,
        [SCALARS, LATE] + cut[: len(rights_a)] + [LATE] + cut[len(rights_a) :] + [AFTER] * len(after),
        cuts=[pieces, pieces],
        scratch=[pltpu.VMEM((model, depth), BF16)],
        cost=6,
    )(scalars, rows_a, *rights_a, rows_b, *rights_b, *after)


def weight_grads_plain(orders, count, rows_a, rights_a, rows_b, rights_b, width):
    model = rows_a.shape[1]
    parts = [dot_tn(rows_a, right) for right in rights_a] + [dot_tn(rows_b, right) for right in rights_b]
    product = half(jnp.concatenate(parts, axis=1)[:, :width])
    if count == 1:
        return product, product
    table = jnp.asarray(row_table(orders, count))
    me = 2 * lax.axis_index("seq") + lax.axis_index("tp")
    table = lax.dynamic_index_in_dim(table, me, 0, keepdims=False)
    back = jnp.zeros((count,), jnp.int32).at[table].set(jnp.arange(count, dtype=jnp.int32))
    placed = jnp.take(product.reshape(count, model // count, width), back, axis=0)
    placed = placed.reshape(model, width)
    return placed[: model // 2], placed[model // 2 :]


def fold(keep, other, after):
    rows, width = keep.shape
    left = rows // 2
    if left % 16:
        total = half(full(keep) + full(other))
        return total[:left], total[left:]

    def body(keep_ref, other_ref, kept_ref, send_ref):
        for index, ref in ((1, send_ref), (0, kept_ref)):
            ref[...] = half(full(keep_ref.piece(index)[index]) + full(other_ref.piece(index)[index]))
            ref.send()

    return call(body, [shaped((left, width))] * 2, [(0, 2), (0, 2)] + [AFTER] * len(after), cost=3)(
        keep.reshape(2, left, width), other.reshape(2, left, width), *after
    )


def fold_last(keep, other, cuts, after):
    rows, width = keep.shape
    plan, outs, start = [], [], 0
    for cut in cuts:
        stack, parts = (None, cut) if not isinstance(cut, tuple) else (cut[0], cut[1:])
        parts = (parts,) if stack is None else parts
        plan.append((stack, [(start + sum(parts[:i]), part) for i, part in enumerate(parts)]))
        start += sum(parts)
        shape = (rows, parts[0])
        if stack is not None:
            shape = shape[:stack] + (len(parts),) + shape[stack:]
        outs.append(shaped(shape, F32))

    def body(keep_ref, other_ref, *refs):
        for (stack, spans), ref in zip(plan, refs):
            for index, (low, size) in enumerate(spans):
                span = slice(low, low + size)
                value = full(keep_ref[:, span]) + full(other_ref[:, span])
                if stack is None:
                    ref[...] = value
                elif stack == 0:
                    ref[index] = value
                else:
                    ref[:, index, :] = value

    return call(body, outs, [LATE, LATE] + [AFTER] * len(after), cost=2)(keep, other, *after)


class Sum:
    def __init__(self, scalars, orders, count, rows_a, rights_a, rows_b, rights_b, width, after=()):
        self.orders, self.count, self.phase = orders, count, 0
        self.bits = count.bit_length() - 1
        operands = (rows_a, rights_a, rows_b, rights_b, width)
        if count > 1 and (rows_a.shape[1] // count) % 16 == 0:
            self.keep, self.send = weight_grads(scalars, orders, count, *operands, tuple(after))
        else:
            self.keep, self.send = weight_grads_plain(orders, count, *operands)
        self.first = self.keep
        if self.bits:
            self.move()
        else:
            self.other = jnp.zeros_like(self.keep)

    def move(self):
        pairs = fold_pairs(self.orders, self.count, self.phase)
        self.other = lax.ppermute(self.send, ("seq", "tp"), pairs)

    def fold(self, *after):
        if self.phase + 1 < self.bits:
            self.phase += 1
            self.keep, self.send = fold(self.keep, self.other, tuple(after))
            self.move()
        return self.keep

    def finish(self, *cuts, after=()):
        while self.phase + 1 < self.bits:
            self.fold()
        return fold_last(self.keep, self.other, cuts, tuple(after))


class Spread:
    def __init__(self, values, count):
        self.values, self.count, self.distance = values, count, 1
        self.move()

    def move(self):
        if self.distance < self.count:
            pairs = [(index, index ^ self.distance) for index in range(self.count)]
            self.other = lax.ppermute(self.values, "seq", pairs)

    def add(self):
        if self.distance < self.count:
            self.values = self.values + self.other
            self.distance *= 2
            self.move()
        return self.values

    def finish(self):
        while self.distance < self.count:
            self.add()
        return self.values


def on_device(count, *arguments):
    (
        tokens, seq_lengths, cotangent, norm1_gain, norm1_shift, qkv1_weight, qv1_bias, out1_weight, out1_bias,
        norm2_gain, norm2_shift, fc1_weight, fc1_bias, proj1_weight, proj1_bias, norm3_gain, norm3_shift,
        qk2_weight, v2_weight, q2_bias, v2_bias, out2_weight, out2_bias, norm4_gain, norm4_shift, fc2_weight,
        fc2_bias, proj2_weight, proj2_bias,
    ) = arguments
    mid, model = tokens.shape
    rows = 2 * mid
    local = qkv1_weight.shape[2]
    fresh = v2_weight.shape[1]
    hidden = fc1_weight.shape[1]
    core = lax.axis_index("tp")
    scalars = jnp.stack([core, seq_lengths[0], lax.axis_index("seq")]).astype(jnp.int32)
    def others(values):
        return lax.dynamic_slice_in_dim(values, (1 - core) * mid, mid, 0)

    qkv1 = qkv1_weight.transpose(1, 0, 2)
    qk2 = qk2_weight.transpose(1, 0, 2)
    fresh_weight = v2_weight.T

    square, narrow = (rows, model), (rows, local)
    bias_scratch = pltpu.VMEM((rows // QUERY_BLOCK, QUERY_BLOCK, QUERY_BLOCK), F32)
    pull_bias = pltpu.VMEM((rows // KEY_BLOCK, KEY_BLOCK, KEY_BLOCK), F32)
    attend_outs = [shaped(square)] + [shaped(narrow)] * 4 + [shaped(square)]
    pull_scratch = [
        pltpu.VMEM(narrow, BF16), pull_bias, pltpu.VMEM((rows, 128), F32), pltpu.VMEM((rows, 128), F32),
    ]
    pull_outs = [shaped(square, F32), shaped(square), shaped(narrow), shaped(narrow)]
    sums_outs = [shaped(square), shaped((8, model), F32), shaped((8, local), F32)]
    total_scratch = pltpu.VMEM(square, F32)
    hidden_out, by_column, by_row = shaped((rows, hidden)), (1, HIDDEN_CUT), (0, HIDDEN_CUT)
    feed_sums = [shaped(square), shaped((8, model), F32), shaped((8, hidden), F32)]

    x0, n1, q1, k1, v1, o1, part = call(
        attend_first, [shaped(square)] + attend_outs, [SCALARS] + [LATE] * 7, scratch=[bias_scratch], cost=8
    )(scalars, tokens, swap(tokens), norm1_gain, norm1_shift, qv1_bias, qkv1, out1_weight)
    x1, m1, z1, pull1, part = call(
        feed_first,
        [shaped(square, F32), shaped(square), hidden_out, hidden_out, shaped(square)],
        [LATE] * 7 + [by_column, by_row],
        cuts=[LATE, LATE, by_column, by_column, LATE],
        scratch=[total_scratch],
        cost=8,
    )(x0, part, swap(part), out1_bias, norm2_gain, norm2_shift, fc1_bias, fc1_weight, proj1_weight)

    x2, n3, q2, k2, v2, o2, part = call(
        attend_second, [shaped(square, F32)] + attend_outs, [SCALARS] + [LATE] * 12, scratch=[bias_scratch], cost=10
    )(scalars, x1, part, swap(part), proj1_bias, norm3_gain, norm3_shift, q2_bias, v2_bias, qk2, fresh_weight, v1,
      out2_weight)
    x3, m3, gb4, z3, du3, part, pulled, rep4, loc4 = call(
        feed_second,
        [shaped(square, F32), shaped(square), shaped(square), hidden_out, hidden_out, shaped(square)] + feed_sums,
        [SCALARS] + [LATE] * 9 + [by_column, by_row],
        cuts=[LATE, LATE, LATE, by_column, by_column] + [LATE] * 4,
        scratch=[total_scratch, total_scratch],
        cost=12,
    )(scalars, x2, part, swap(part), out2_bias, norm4_gain, norm4_shift, fc2_bias, cotangent, swap(cotangent),
      fc2_weight, proj2_weight)
    pulled_other = swap(pulled)
    out_part, out_other = part, swap(others(part))
    first = Sum(scalars, FIRST_ORDERS, count, m3, [du3], gb4, [z3], 2 * hidden)

    g3, gb3, dq2, dk2, dv2, df2, part, rep3, loc3 = call(
        pull_second, pull_outs + [shaped(narrow, F32), shaped(narrow)] + sums_outs,
        [SCALARS] + [LATE] * 11 + [AFTER], scratch=pull_scratch, cost=14,
    )(scalars, gb4, pulled, pulled_other, x3, norm4_gain, q2, k2, v2, qk2, fresh_weight, out2_weight, first.keep)
    part_other = swap(part)
    second = Sum(scalars, SECOND_ORDERS, count, gb3, [o2], n3, [dq2, dk2, df2], 3 * local + 2 * 128)

    g2, gb2, du1, pulled, rep2, loc2 = call(
        feed_pull,
        [shaped(square, F32), shaped(square), hidden_out] + feed_sums,
        [LATE] * 5 + [by_column, by_column, by_row, AFTER],
        cuts=[LATE, LATE, by_column] + [LATE] * 3,
        scratch=[total_scratch],
        cost=8,
    )(g3, part, part_other, x2, norm3_gain, pull1, fc1_weight, proj1_weight, second.keep)
    pulled_other = swap(pulled)
    first.fold(g2)
    third = Sum(scalars, THIRD_ORDERS, count, m1, [du1], gb2, [z1], 2 * hidden, [first.keep])

    g1, gb1, dq1, dk1, dv1, part, rep1, loc1 = call(
        functools.partial(pull_first, fresh=fresh), pull_outs + [shaped(narrow)] + sums_outs,
        [SCALARS] + [LATE] * 11 + [AFTER], scratch=pull_scratch + [pltpu.VMEM(narrow, F32)], cost=15,
    )(scalars, g2, pulled, pulled_other, x1, norm2_gain, q1, k1, v1, qkv1, dv2, out1_weight, third.keep)
    part_other = swap(others(part))
    fourth = Sum(scalars, FOURTH_ORDERS, count, n1, [dq1, dk1, dv1], gb1, [o1], 4 * local)
    tokens_grad, packed = call(
        pull_tokens, [shaped((mid, model)), shaped((PACKED, model), F32)],
        [SCALARS] + [LATE] * 13 + [AFTER], cost=4,
    )(scalars, g1, part, part_other, x0, norm1_gain, rep4, rep3, rep2, rep1, loc4, loc3, loc2, loc1, fourth.first)
    packed = Spread(packed, count)
    second.fold(packed.values)
    first.fold(second.keep)
    layer_output = call(finish_layer, shaped((mid, model)), [SCALARS] + [LATE] * 4 + [AFTER], cost=3)(
        scalars, x3, out_part, out_other, proj2_bias, first.keep
    )
    third.fold(layer_output)
    second.fold(third.keep, packed.add())
    first.fold(second.keep)
    fourth.fold(first.keep, packed.add())
    third.fold(fourth.keep)
    sum_fc2, sum_proj2 = first.finish(hidden, hidden, after=[third.keep])
    second.fold(sum_fc2)
    fourth.fold(second.keep, packed.add())
    third.fold(fourth.keep)
    sum_out2, sum_qk2, sum_v2 = second.finish(local, (1, local, local), fresh, after=[third.keep])
    fourth.fold(sum_out2, packed.add())
    sum_fc1, sum_proj1 = third.finish(hidden, hidden, after=[fourth.keep])
    sum_qkv1, sum_out1 = fourth.finish((0, local, local, local), local, after=[sum_fc1])
    sum_qkv1 = sum_qkv1.transpose(1, 0, 2)

    packed = packed.finish()
    vector, small = shaped((model,), F32), shaped((2 * fresh,), F32)
    long_vector = shaped((2 * hidden,), F32)
    (
        sum_gain1, sum_shift1, sum_qv1_bias, sum_out1_bias, sum_gain2, sum_shift2, sum_fc1_bias, sum_proj1_bias,
        sum_gain3, sum_shift3, sum_q2_bias, sum_v2_bias, sum_out2_bias, sum_gain4, sum_shift4, sum_fc2_bias,
        sum_proj2_bias,
    ) = call(
        unpack_sums,
        [vector, vector, shaped((2, model), F32), vector, vector, vector, long_vector, vector,
         vector, vector, vector, small, vector, vector, vector, long_vector, vector],
        [SCALARS, LATE, LATE],
        cost=2,
    )(scalars, packed, swap(packed))
    return (
        layer_output, tokens_grad, sum_gain1, sum_shift1, sum_qkv1, sum_qv1_bias, sum_out1.T, sum_out1_bias,
        sum_gain2, sum_shift2, sum_fc1, sum_fc1_bias, sum_proj1.T, sum_proj1_bias, sum_gain3, sum_shift3, sum_qk2,
        sum_v2, sum_q2_bias, sum_v2_bias, sum_out2.T, sum_out2_bias, sum_gain4, sum_shift4, sum_fc2, sum_fc2_bias,
        sum_proj2.T, sum_proj2_bias,
    )


def solution(mesh):
    rows, copied = P(("seq", "tp"), None), P()
    columns, deep = P(None, "tp"), P("tp", None)
    wide, long = P("seq", "tp"), P("tp", "seq")
    count = mesh.shape["seq"]

    def body(*arguments):
        return on_device(count, *arguments)

    return jax.shard_map(
        body,
        mesh=mesh,
        in_specs=(
            rows, P("seq"), rows, copied, copied, P(None, None, "tp"), columns, deep, copied,
            copied, copied, columns, P("tp"), deep, copied, copied, copied,
            P(None, None, "tp"), columns, P("tp"), P("tp"), deep, copied, copied, copied, columns,
            P("tp"), deep, copied,
        ),
        out_specs=(
            rows, rows, copied, copied, P("seq", None, "tp"), copied, long, copied,
            copied, copied, wide, copied, long, copied, copied, copied, P("seq", None, "tp"),
            wide, copied, copied, long, copied, copied, copied, wide, copied,
            long, copied,
        ),
        check_vma=False,
    )
```

```python
import functools

import jax
import jax.numpy as jnp
import numpy as np
from jax import lax
from jax.experimental import pallas as pl
from jax.experimental.pallas import tpu as pltpu
from jax.sharding import PartitionSpec as P

HEAD_DIM = 64
F32 = jnp.float32
BF16 = jnp.bfloat16


def half(values):
    return values.astype(BF16)


def full(values):
    return values.astype(F32)


def dot(left, right):
    return lax.dot_general(left, right, (((1,), (0,)), ((), ())), preferred_element_type=F32)


def dot_nt(left, right):
    return lax.dot_general(left, right, (((1,), (1,)), ((), ())), preferred_element_type=F32)


def dot_tn(left, right):
    return lax.dot_general(left, right, (((0,), (0,)), ((), ())), preferred_element_type=F32)


def swap(values):
    return lax.ppermute(values, "tp", [(0, 1), (1, 0)])


BLOCK = 256
HIDDEN_CUT = 3
VMEM_BYTES, BIG_BYTES = 16 * 1024 * 1024, 16 * 1024 * 1024


class Arriving:
    def __init__(self, source, buffer, sems, first, cut):
        self.source, self.buffer, self.shape, self.dtype = source, buffer, source.shape, source.dtype
        axis, count = cut
        size = source.shape[axis] // count
        self.copies = []
        for index in range(count):
            at = (slice(None),) * axis + (pl.ds(index * size, size),)
            here, there = (source, buffer) if count == 1 else (source.at[at], buffer.at[at])
            self.copies.append(pltpu.make_async_copy(here, there, sems.at[first + index]))
        self.waiting = set(range(count))

    def start(self):
        for copy in self.copies:
            copy.start()

    def piece(self, index):
        if index in self.waiting:
            self.waiting.remove(index)
            self.copies[index].wait()
        return self.buffer

    def whole(self):
        for index in range(len(self.copies)):
            self.piece(index)
        return self.buffer

    def __getitem__(self, at):
        return self.whole()[at]


class Held:
    def __init__(self, ref):
        self.buffer, self.shape, self.dtype, self.copies = ref, ref.shape, ref.dtype, [None]

    def piece(self, index):
        return self.buffer

    def send(self, index=0):
        pass

    def __getitem__(self, at):
        return self.buffer[at]

    def __setitem__(self, at, value):
        self.buffer[at] = value


class Leaving:
    def __init__(self, target, buffer, sems, first, cut):
        self.target, self.buffer, self.shape, self.dtype = target, buffer, target.shape, target.dtype
        axis, count = cut
        size = target.shape[axis] // count
        self.copies = []
        for index in range(count):
            at = (slice(None),) * axis + (pl.ds(index * size, size),)
            here, there = (buffer, target) if count == 1 else (buffer.at[at], target.at[at])
            self.copies.append(pltpu.make_async_copy(here, there, sems.at[first + index]))
        self.held = set(range(count))

    def send(self, index=0):
        self.held.remove(index)
        self.copies[index].start()

    def finish(self):
        for index in sorted(self.held):
            self.send(index)

    def __getitem__(self, at):
        return self.buffer[at]

    def __setitem__(self, at, value):
        self.buffer[at] = value


SCALARS, AFTER, NEAR, LATE = "scalars", "after", "near", (0, 1)


SPACES = {SCALARS: pltpu.SMEM, NEAR: pltpu.VMEM, AFTER: pl.ANY}


def placed(operand, kind):
    if kind in (SCALARS, AFTER):
        return operand
    return pltpu.with_memory_space_constraint(operand, pltpu.VMEM if kind == NEAR else pltpu.HBM)


TOLD = 0.6


def call(body, outs, ins, cuts=None, scratch=(), cost=1.0, vmem=None):
    single = not isinstance(outs, (list, tuple))
    outs = [outs] if single else list(outs)
    cuts = list(cuts) if cuts is not None else [LATE] * len(outs)
    late = [index for index, kind in enumerate(ins) if isinstance(kind, tuple)]
    in_counts = [ins[index][1] for index in late]
    far = [index for index, kind in enumerate(cuts) if isinstance(kind, tuple)]
    out_counts = [cuts[index][1] for index in far]

    def wrapped(*refs):
        refs = list(refs)
        operands, refs = refs[: len(ins)], refs[len(ins) :]
        targets, refs = refs[: len(outs)], refs[len(outs) :]
        extra, refs = refs[: len(scratch)], refs[len(scratch) :]
        in_buffers, refs = refs[: len(late)], refs[len(late) :]
        out_buffers, sems = refs[: len(far)], refs[len(far) :]
        in_sems, out_sems = sems[0] if late else None, sems[-1] if far else None
        arriving = {
            index: Arriving(operands[index], in_buffers[at], in_sems, sum(in_counts[:at]), ins[index])
            for at, index in enumerate(late)
        }
        for operand in arriving.values():
            operand.start()
        leaving = {
            index: Leaving(targets[index], out_buffers[at], out_sems, sum(out_counts[:at]), cuts[index])
            for at, index in enumerate(far)
        }
        results = [leaving[index] if index in leaving else Held(target) for index, target in enumerate(targets)]
        given = [
            arriving[index] if index in arriving else Held(operands[index]) if kind == NEAR else operands[index]
            for index, kind in enumerate(ins)
            if kind != AFTER
        ]
        body(*given, *results, *extra)
        for operand in arriving.values():
            operand.whole()
        for result in leaving.values():
            result.finish()
        for result in leaving.values():
            for copy in result.copies:
                copy.wait()

    def run(*operands):
        buffers = [pltpu.VMEM(operands[index].shape, operands[index].dtype) for index in late]
        buffers += [pltpu.VMEM(outs[index].shape, outs[index].dtype) for index in far]
        sems = [pltpu.SemaphoreType.DMA((sum(counts),)) for counts in (in_counts, out_counts) if counts]
        results = pl.pallas_call(
            wrapped,
            out_shape=[
                (pltpu.VMEM if kind == NEAR else pltpu.HBM)(out.shape, out.dtype) for out, kind in zip(outs, cuts)
            ],
            in_specs=[pl.BlockSpec(memory_space=SPACES.get(kind, pltpu.HBM)) for kind in ins],
            out_specs=[pl.BlockSpec(memory_space=SPACES.get(kind, pltpu.HBM)) for kind in cuts],
            scratch_shapes=list(scratch) + buffers + sems,
            compiler_params=pltpu.CompilerParams(vmem_limit_bytes=vmem or VMEM_BYTES),
            cost_estimate=pl.CostEstimate(
                flops=int(cost * TOLD * 1.1e9), bytes_accessed=int(cost * TOLD * 3.4e6), transcendentals=0
            ),
        )(*(placed(operand, kind) for operand, kind in zip(operands, ins)))
        return results[0] if single else results

    return run


def shaped(shape, kind=BF16):
    return jax.ShapeDtypeStruct(shape, kind)


def row(ref):
    return full(ref[...][None, :])


def norm_stats(values):
    mean = jnp.mean(values, axis=-1, keepdims=True)
    centered = values - mean
    scale = lax.rsqrt(jnp.mean(centered * centered, axis=-1, keepdims=True) + 1e-05)
    return centered * scale, scale


def norm_backward(grad, values, gain):
    hat, scale = norm_stats(values)
    inner = grad * gain
    mean_inner = jnp.mean(inner, axis=-1, keepdims=True)
    mean_hat = jnp.mean(inner * hat, axis=-1, keepdims=True)
    pulled = scale * (inner - mean_inner - hat * mean_hat)
    return (
        pulled,
        jnp.sum(grad * hat, axis=0, keepdims=True),
        jnp.sum(grad, axis=0, keepdims=True),
    )


def gelu_both(values):
    square = values * values
    bent = jnp.tanh(values * (0.7978845608028654 + 0.035677408136300125 * square))
    rise = 0.5 + 0.5 * bent
    slope = 0.7978845608028654 + 0.10703222440890038 * square
    pull = rise + (0.5 * values) * (1.0 - bent * bent) * slope
    return values * rise, pull


def head_lanes(width, which):
    lane = lax.broadcasted_iota(jnp.int32, (1, width), 1)
    return (lane // HEAD_DIM) == which


def keep_lanes(values, lanes):
    return jnp.where(lanes, values, jnp.zeros_like(values))


def fill_bias(bias_ref, length):
    query = lax.broadcasted_iota(jnp.int32, bias_ref.shape, 0)
    key = lax.broadcasted_iota(jnp.int32, bias_ref.shape, 1)
    bias_ref[...] = jnp.where((key <= query) & (key < length), 0.0, -1e30)


def turned_heads(pair):
    turned = full(pair).T
    return [half(turned[which * HEAD_DIM : (which + 1) * HEAD_DIM]) for which in range(2)]


def attend_rows(q_ref, k_ref, v_ref, o_ref, p_ref, bias_ref, length):
    fill_bias(bias_ref, length)
    for pair in range(q_ref.shape[1] // 128):
        lanes = slice(pair * 128, pair * 128 + 128)
        keys, values = k_ref[:, lanes], v_ref[:, lanes]
        total = None
        for which in range(2):
            mask = head_lanes(128, which)
            query = keep_lanes(q_ref[:, lanes] * 0.125, mask).astype(BF16)
            scores = dot_nt(query, keys) + bias_ref[...]
            weights = jnp.exp(scores - jnp.max(scores, axis=-1, keepdims=True))
            weights = weights * (1.0 / jnp.sum(weights, axis=-1, keepdims=True))
            p_ref[2 * pair + which] = half(weights.T)
            p_ref.send(2 * pair + which)
            mixed = dot(half(weights), keep_lanes(values, mask))
            total = mixed if total is None else total + mixed
        o_ref[:, lanes] = half(total)


def attend_first(scal_ref, mine_ref, other_ref, gain_ref, shift_ref, bias_refs, w_ref, out_ref,
                 x_ref, n_ref, q_ref, k_ref, v_ref, o_ref, p_ref, part_ref, bias_ref):
    core, length = scal_ref[0], scal_ref[1]
    mid = mine_ref.shape[0]
    x_ref[pl.ds(pl.multiple_of(core * mid, mid), mid), :] = mine_ref[...]
    x_ref[pl.ds(pl.multiple_of((1 - core) * mid, mid), mid), :] = other_ref[...]
    hat, _ = norm_stats(full(x_ref[...]))
    normed = half(hat * row(gain_ref) + row(shift_ref))
    n_ref[...] = normed
    x_ref.send()
    n_ref.send()
    q_ref[...] = half(dot(normed, w_ref[0]) + full(bias_refs[0:1, :]))
    k_ref[...] = half(dot(normed, w_ref[1]))
    v_ref[...] = half(dot(normed, w_ref[2]) + full(bias_refs[1:2, :]))
    for ref in (q_ref, k_ref, v_ref):
        ref.send()
    attend_rows(q_ref, k_ref, v_ref, o_ref, p_ref, bias_ref, length)
    o_ref.send()
    part_ref[...] = half(dot(o_ref[...], out_ref[...]))


def attend_second(scal_ref, prev_ref, mine_ref, other_ref, before_ref, gain_ref, shift_ref, qb_ref, fb_ref,
                  w_ref, f_ref, v1_ref, out_ref,
                  x_ref, n_ref, q_ref, k_ref, v_ref, o_ref, p_ref, part_ref, bias_ref):
    length = scal_ref[1]
    x_ref[...] = prev_ref[...] + (full(mine_ref[...]) + full(other_ref[...])) + row(before_ref)
    hat, _ = norm_stats(x_ref[...])
    normed = half(hat * row(gain_ref) + row(shift_ref))
    n_ref[...] = normed
    x_ref.send()
    n_ref.send()
    fresh = f_ref.shape[0]
    q_ref[...] = half(dot(normed, w_ref[0]) + row(qb_ref))
    k_ref[...] = half(dot(normed, w_ref[1]))
    v_ref[...] = v1_ref[...]
    v_ref[:, :fresh] = half(dot_nt(normed, f_ref[...]) + row(fb_ref))
    for ref in (q_ref, k_ref, v_ref):
        ref.send()
    attend_rows(q_ref, k_ref, v_ref, o_ref, p_ref, bias_ref, length)
    o_ref.send()
    part_ref[...] = half(dot(o_ref[...], out_ref[...]))


def attend_pull(q_ref, k_ref, v_ref, p_ref, do_ref, dq_ref, dk_ref, dv_ref, ds_ref):
    rows, width = q_ref.shape
    heads = width // HEAD_DIM
    blocks = rows // BLOCK
    for pair in range(heads // 2):
        lanes = slice(pair * 128, pair * 128 + 128)
        keys, values = turned_heads(k_ref[:, lanes]), v_ref[:, lanes]
        pulled_query, queries, grads = {}, {}, {}
        for which in range(2):
            head = 2 * pair + which
            p_ref.piece(head)
            mask = head_lanes(128, which)
            queries[which] = keep_lanes(q_ref[:, lanes] * 0.125, mask).astype(BF16)
            grads[which] = keep_lanes(do_ref[:, lanes], mask)
            for block in range(blocks):
                start, stop = block * BLOCK, (block + 1) * BLOCK
                pulled = dot_nt(values[:stop], grads[which][start:stop])
                weights = full(p_ref.buffer[head, :stop, start:stop])
                total = jnp.sum(weights, axis=0, keepdims=True)
                centre = jnp.sum(weights * pulled, axis=0, keepdims=True) * (1.0 / total)
                score_grad = half(weights * (pulled - centre))
                ds_ref[which, :stop, start:stop] = score_grad
                pulled_query[block, which] = dot(keys[which][:, :stop], score_grad)
        for block in range(blocks):
            start, stop = block * BLOCK, (block + 1) * BLOCK
            joined = jnp.concatenate([pulled_query[block, 0], pulled_query[block, 1]], axis=0) * 0.125
            dq_ref[start:stop, lanes] = half(joined.T)
            dk_ref[start:stop, lanes] = half(
                dot(ds_ref[0, start:stop, start:], queries[0][start:])
                + dot(ds_ref[1, start:stop, start:], queries[1][start:])
            )
            dv_ref[start:stop, lanes] = dot(
                p_ref.buffer[2 * pair, start:stop, start:], grads[0][start:]
            ) + dot(p_ref.buffer[2 * pair + 1, start:stop, start:], grads[1][start:])


def column_sum(values):
    return jnp.sum(full(values), axis=0, keepdims=True)


def pull_second(g4_ref, mine_ref, other_ref, x_ref, gain_ref, q_ref, k_ref, v_ref, p_ref, w_ref, f_ref, out_ref,
                g_ref, gb_ref, dq_ref, dk_ref, dv_ref, dvb_ref, part_ref, rep_ref, loc_ref,
                do_ref, ds_ref):
    grad = full(mine_ref[...]) + full(other_ref[...])
    pulled, gain, shift = norm_backward(grad, x_ref[...], row(gain_ref))
    g_ref[...] = full(g4_ref[...]) + pulled
    rep_ref[...] = jnp.zeros_like(rep_ref)
    loc_ref[...] = jnp.zeros_like(loc_ref)
    rep_ref[0:1, :] = gain
    rep_ref[1:2, :] = shift
    rep_ref[2:3, :] = column_sum(g_ref[...])
    gb_ref[...] = half(g_ref[...])
    g_ref.send()
    gb_ref.send()
    do_ref[...] = half(dot_nt(gb_ref[...], out_ref[...]))
    attend_pull(q_ref, k_ref, v_ref, p_ref, do_ref, dq_ref, dk_ref, dv_ref, ds_ref)
    fresh = f_ref.shape[0]
    dvb_ref[...] = half(dv_ref[...])
    fresh_grad = dvb_ref[:, :fresh]
    part_ref[...] = half(
        dot_nt(dq_ref[...], w_ref[0]) + dot_nt(dk_ref[...], w_ref[1]) + dot(fresh_grad, f_ref[...])
    )
    loc_ref[0:1, :] = column_sum(dq_ref[...])
    loc_ref[1:2, :] = column_sum(dvb_ref[...])


def pull_first(scal_ref, g2_ref, mine_ref, other_ref, x_ref, gain_ref, q_ref, k_ref, v_ref, p_ref, w_ref, reused_ref, out_ref,
               g_ref, gb_ref, dq_ref, dk_ref, dv_ref, own_ref, part_ref, rep_ref, loc_ref,
               do_ref, ds_ref, dv_full, partial, *, fresh):
    grad = full(mine_ref[...]) + full(other_ref[...])
    pulled, gain, shift = norm_backward(grad, x_ref[...], row(gain_ref))
    g_ref[...] = g2_ref[...] + pulled
    rep_ref[...] = jnp.zeros_like(rep_ref)
    loc_ref[...] = jnp.zeros_like(loc_ref)
    rep_ref[0:1, :] = gain
    rep_ref[1:2, :] = shift
    rep_ref[2:3, :] = column_sum(g_ref[...])
    gb_ref[...] = half(g_ref[...])
    g_ref.send()
    gb_ref.send()
    do_ref[...] = half(dot_nt(gb_ref[...], out_ref[...]))
    attend_pull(q_ref, k_ref, v_ref, p_ref, do_ref, dq_ref, dk_ref, dv_full, ds_ref)
    column = lax.broadcasted_iota(jnp.int32, (1, dv_full.shape[1]), 1)
    dv_ref[...] = half(dv_full[...] + jnp.where(column >= fresh, reused_ref[...], 0.0))
    partial[...] = half(
        dot_nt(dq_ref[...], w_ref[0]) + dot_nt(dk_ref[...], w_ref[1]) + dot_nt(dv_ref[...], w_ref[2])
    )
    core, mid = scal_ref[0], own_ref.shape[0]
    own_ref[...] = partial[pl.ds(pl.multiple_of(core * mid, mid), mid), :]
    part_ref[...] = partial[pl.ds(pl.multiple_of((1 - core) * mid, mid), mid), :]
    loc_ref[0:1, :] = column_sum(dq_ref[...])
    loc_ref[1:2, :] = column_sum(dv_ref[...])


ROW_BLOCK = 256


def hidden_spans(ref):
    size = ref.shape[1] // HIDDEN_CUT
    return [slice(index * size, (index + 1) * size) for index in range(HIDDEN_CUT)]


def add_to(total, span, value, fresh):
    total[span, :] = value if fresh else total[span, :] + value


def feed_first(prev_ref, mine_ref, other_ref, before_ref, gain_ref, shift_ref, bias_ref, fc_ref, proj_ref,
               x_ref, m_ref, z_ref, pull_ref, part_ref, total):
    x_ref[...] = full(prev_ref[...]) + (full(mine_ref[...]) + full(other_ref[...])) + row(before_ref)
    x_ref.send()
    hat, _ = norm_stats(x_ref[...])
    m_ref[...] = half(hat * row(gain_ref) + row(shift_ref))
    m_ref.send()
    for index, columns in enumerate(hidden_spans(fc_ref)):
        fc, proj = fc_ref.piece(index), proj_ref.piece(index)
        bias = full(bias_ref[columns][None, :])
        for low in range(0, m_ref.shape[0], ROW_BLOCK):
            span = slice(low, low + ROW_BLOCK)
            value, pull = gelu_both(dot(m_ref[span, :], fc[:, columns]) + bias)
            value = half(value)
            z_ref[span, columns] = value
            pull_ref[span, columns] = half(pull)
            add_to(total, span, dot(value, proj[columns, :]), index == 0)
        z_ref.send(index)
        pull_ref.send(index)
    part_ref[...] = half(total[...])


def feed_second(scal_ref, prev_ref, mine_ref, other_ref, before_ref, gain_ref, shift_ref, bias_ref,
                cot_ref, cot_other_ref, fc_ref, proj_ref,
                x_ref, m_ref, g_ref, z_ref, du_ref, own_ref, part_ref, pulled_ref, rep_ref, loc_ref, total, pulled_total):
    core, length = scal_ref[0], scal_ref[1]
    x_ref[...] = prev_ref[...] + (full(mine_ref[...]) + full(other_ref[...])) + row(before_ref)
    x_ref.send()
    hat, _ = norm_stats(x_ref[...])
    m_ref[...] = half(hat * row(gain_ref) + row(shift_ref))
    m_ref.send()
    mid = cot_ref.shape[0]
    place = lax.broadcasted_iota(jnp.int32, (mid, 1), 0)
    for source, owner in ((cot_ref, core), (cot_other_ref, 1 - core)):
        base = pl.multiple_of(owner * mid, mid)
        alive = (place + base < length).astype(F32)
        g_ref[pl.ds(base, mid), :] = half(full(source[...]) * alive)
    g_ref.send()
    rep_ref[...] = jnp.zeros_like(rep_ref)
    loc_ref[...] = jnp.zeros_like(loc_ref)
    rep_ref[0:1, :] = column_sum(g_ref[...])
    for index, columns in enumerate(hidden_spans(fc_ref)):
        fc, proj = fc_ref.piece(index), proj_ref.piece(index)
        bias = full(bias_ref[columns][None, :])
        sums = None
        for low in range(0, m_ref.shape[0], ROW_BLOCK):
            span = slice(low, low + ROW_BLOCK)
            value, pull = gelu_both(dot(m_ref[span, :], fc[:, columns]) + bias)
            value = half(value)
            z_ref[span, columns] = value
            add_to(total, span, dot(value, proj[columns, :]), index == 0)
            du = half(dot_nt(g_ref[span, :], proj[columns, :]) * pull)
            du_ref[span, columns] = du
            add_to(pulled_total, span, dot_nt(du, fc[:, columns]), index == 0)
            sums = column_sum(du) if sums is None else sums + column_sum(du)
        loc_ref[0:1, columns] = sums
        z_ref.send(index)
        du_ref.send(index)
    own_ref[...] = half(total[pl.ds(pl.multiple_of(core * mid, mid), mid), :])
    part_ref[...] = half(total[pl.ds(pl.multiple_of((1 - core) * mid, mid), mid), :])
    pulled_ref[...] = half(pulled_total[...])


def feed_pull(g3_ref, mine_ref, other_ref, xin_ref, gain_ref, pull_ref, fc_ref, proj_ref,
              g_ref, gb_ref, du_ref, pulled_ref, rep_ref, loc_ref, pulled_total):
    grad = full(mine_ref[...]) + full(other_ref[...])
    pulled, gain, shift = norm_backward(grad, xin_ref[...], row(gain_ref))
    g_ref[...] = g3_ref[...] + pulled
    g_ref.send()
    rep_ref[...] = jnp.zeros_like(rep_ref)
    loc_ref[...] = jnp.zeros_like(loc_ref)
    rep_ref[0:1, :] = gain
    rep_ref[1:2, :] = shift
    rep_ref[2:3, :] = column_sum(g_ref[...])
    gb_ref[...] = half(g_ref[...])
    gb_ref.send()
    for index, columns in enumerate(hidden_spans(fc_ref)):
        fc, proj = fc_ref.piece(index), proj_ref.piece(index)
        pull = pull_ref.piece(index)
        sums = None
        for low in range(0, gb_ref.shape[0], ROW_BLOCK):
            span = slice(low, low + ROW_BLOCK)
            du = half(dot_nt(gb_ref[span, :], proj[columns, :]) * full(pull[span, columns]))
            du_ref[span, columns] = du
            add_to(pulled_total, span, dot_nt(du, fc[:, columns]), index == 0)
            sums = column_sum(du) if sums is None else sums + column_sum(du)
        loc_ref[0:1, columns] = sums
        du_ref.send(index)
    pulled_ref[...] = half(pulled_total[...])


PACKED, SHARED = 24, 10


def pull_tokens(scal_ref, g1_ref, mine_ref, other_ref, x_ref, gain_ref,
                rep4_ref, rep3_ref, rep2_ref, rep1_ref, loc4_ref, loc3_ref, loc2_ref, loc1_ref,
                out_ref, pack_ref):
    mid, model = out_ref.shape
    own = pl.ds(pl.multiple_of(scal_ref[0] * mid, mid), mid)
    grad = full(mine_ref[...]) + full(other_ref[...])
    pulled, gain, shift = norm_backward(grad, full(x_ref[own, :]), row(gain_ref))
    out_ref[...] = half(g1_ref[own, :] + pulled)
    pack_ref[...] = jnp.zeros_like(pack_ref)
    pack_ref[0:1, :] = rep4_ref[0:1, :]
    for index, ref in enumerate((rep3_ref, rep2_ref, rep1_ref)):
        pack_ref[1 + 3 * index : 4 + 3 * index, :] = ref[0:3, :]
    pack_ref[SHARED : SHARED + 1, :] = gain
    pack_ref[SHARED + 1 : SHARED + 2, :] = shift
    for index, ref in enumerate((loc4_ref, loc2_ref)):
        for part in range(2):
            at = SHARED + 2 + 2 * index + part
            pack_ref[at : at + 1, :] = ref[0:1, part * model : (part + 1) * model]
    for index, ref in enumerate((loc3_ref, loc1_ref)):
        at = SHARED + 6 + index
        for part in range(2):
            pack_ref[at : at + 1, part * model // 2 : (part + 1) * model // 2] = ref[part : part + 1, :]


def unpack_sums(scal_ref, mine_ref, other_ref, *outs):
    first = scal_ref[0] == 0
    (gain1, shift1, qv1, out1, gain2, shift2, fc1, proj1,
     gain3, shift3, q2, v2, out2, gain4, shift4, fc2, proj2) = outs
    same = (proj2, gain4, shift4, out2, gain3, shift3, proj1, gain2, shift2, out1)
    for index, ref in enumerate(same):
        ref[...] = mine_ref[index, :]
    for index, ref in enumerate((gain1, shift1)):
        ref[...] = mine_ref[SHARED + index, :] + other_ref[SHARED + index, :]
    model = gain1.shape[0]

    def both(at):
        mine, other = mine_ref[at : at + 1, :], other_ref[at : at + 1, :]
        return jnp.where(first, mine, other), jnp.where(first, other, mine)

    for index, ref in enumerate((fc2, fc1)):
        for part in range(2):
            for core, value in enumerate(both(SHARED + 2 + 2 * index + part)):
                at = (2 * core + part) * model
                ref[at : at + model] = value[0]
    low, high = both(SHARED + 6)
    middle = model // 2
    q2[:middle] = low[0, :middle]
    q2[middle:] = high[0, :middle]
    fresh = v2.shape[0] // 2
    v2[...] = jnp.concatenate([low[:, middle : middle + fresh], high[:, middle : middle + fresh]], axis=1)[0]
    low, high = both(SHARED + 7)
    for part in range(2):
        span = slice(part * middle, (part + 1) * middle)
        qv1[part : part + 1, :middle] = low[:, span]
        qv1[part : part + 1, middle:] = high[:, span]


def finish_layer(scal_ref, x_ref, mine_ref, other_ref, before_ref, out_ref):
    mid = out_ref.shape[0]
    base = pl.multiple_of(scal_ref[0] * mid, mid)
    own = pl.ds(base, mid)
    total = x_ref[own, :] + (full(mine_ref[...]) + full(other_ref[...])) + row(before_ref)
    place = lax.broadcasted_iota(jnp.int32, (mid, 1), 0)
    out_ref[...] = half(total * (place + base < scal_ref[1]).astype(F32))


FIRST_ORDERS = ((0, 1, 2, 3), (1, 0, 3, 2))
SECOND_ORDERS = ((1, 0, 2, 3), (2, 3, 1, 0))
THIRD_ORDERS = ((0, 2, 1, 3), (3, 1, 0, 2))
FOURTH_ORDERS = ((1, 0, 2, 3), (2, 0, 1, 3))
FIFTH_ORDERS = ((0, 1, 3, 2), (1, 0, 2, 3))


def bit_orders(orders, bits):
    return [[bit for bit in order if bit < bits] + list(range(4, bits)) for order in orders]


def row_table(orders, count):
    bits = count.bit_length() - 1
    table = np.zeros((count, 2, count), np.int32)
    for core, order in enumerate(bit_orders(orders, bits)):
        for me in range(count):
            for block in range(count):
                place = 0
                for bit in order:
                    place = 2 * place + (((block ^ me) >> bit) & 1)
                table[me, core, block] = place
    return table.reshape(count * 2, count)


def fold_pairs(orders, count, phase):
    bits = count.bit_length() - 1
    pairs = []
    for core, order in enumerate(bit_orders(orders, bits)):
        for me in range(count):
            pairs.append((2 * me + core, 2 * (me ^ (1 << order[phase])) + core))
    return pairs


def weight_grads(scalars, orders, count, products, width, after, far):
    operands = [operand for rows, rights in products for operand in (rows, *rights)]
    depth, model = products[0][0].shape
    span = model // count
    bits = count.bit_length() - 1
    lists = bit_orders(orders, bits)

    def kind_of(operand):
        if not any(operand is other for other in far):
            return NEAR
        return (1, 2) if operand.shape[1] > model else LATE

    def body(scal_ref, *refs):
        keep_ref, send_ref, turned = refs[len(refs) - 3 :]
        core, me = scal_ref[0], scal_ref[2]

        def turn(ref):
            columns = ref[...].T
            for index in range(count):
                apart = index ^ me
                places = [
                    sum(((apart >> bit) & 1) << (bits - 1 - at) for at, bit in enumerate(order)) for order in lists
                ]
                place = jnp.where(core == 0, places[0], places[1])
                at = pl.ds(pl.multiple_of(place * span, 16), span)
                turned[at, :] = columns[index * span : (index + 1) * span]

        start, taken = 0, 0
        for _, rights in products:
            turn(refs[taken])
            for ref in refs[taken + 1 : taken + 1 + len(rights)]:
                size = min(ref.shape[1], width - start)
                step = size // len(ref.copies)
                for index in range(len(ref.copies)):
                    columns = slice(index * step, (index + 1) * step)
                    at = slice(start + index * step, start + (index + 1) * step)
                    right = ref.piece(index)[:, columns]
                    send_ref[:, at] = half(dot(turned[model // 2 :, :], right))
                    keep_ref[:, at] = half(dot(turned[: model // 2, :], right))
                start += size
            taken += 1 + len(rights)

    return call(
        body,
        [shaped((model // 2, width))] * 2,
        [SCALARS] + [kind_of(operand) for operand in operands] + [AFTER] * len(after),
        cuts=[NEAR, NEAR],
        scratch=[pltpu.VMEM((model, depth), BF16)],
        cost=width / 3072 * 5,
        vmem=GRAD_BYTES,
    )(scalars, *operands, *after)


def weight_grads_plain(orders, count, products, width):
    model = products[0][0].shape[1]
    parts = [dot_tn(rows, right) for rows, rights in products for right in rights]
    product = half(jnp.concatenate(parts, axis=1)[:, :width])
    if count == 1:
        return product, product
    table = jnp.asarray(row_table(orders, count))
    me = 2 * lax.axis_index("seq") + lax.axis_index("tp")
    table = lax.dynamic_index_in_dim(table, me, 0, keepdims=False)
    back = jnp.zeros((count,), jnp.int32).at[table].set(jnp.arange(count, dtype=jnp.int32))
    placed = jnp.take(product.reshape(count, model // count, width), back, axis=0)
    placed = placed.reshape(model, width)
    return placed[: model // 2], placed[model // 2 :]


GRAD_BYTES = 12 * 1024 * 1024
SMALL_BYTES = 8 * 1024 * 1024


def fold(keep, other, after, extra=()):
    rows, width = keep.shape
    left = rows // 2
    if left % 16:
        total = half(full(keep) + full(other))
        return [total[:left], total[left:]] + ([extra[0] + extra[1]] if extra else [])

    def body(keep_ref, other_ref, *refs):
        if extra:
            refs[-1][...] = refs[0][...] + refs[1][...]
        kept_ref, send_ref = refs[len(extra) : len(extra) + 2]
        send_ref[...] = half(full(keep_ref[left:, :]) + full(other_ref[left:, :]))
        kept_ref[...] = half(full(keep_ref[:left, :]) + full(other_ref[:left, :]))

    outs = [shaped((left, width))] * 2 + [shaped(value.shape, F32) for value in extra[:1]]
    kinds = [NEAR] * (2 + len(extra)) + [AFTER] * len(after)
    return call(body, outs, kinds, cuts=[NEAR] * len(outs), cost=2, vmem=SMALL_BYTES)(keep, other, *extra, *after)


def fold_last(keep, other, cuts, after):
    rows, width = keep.shape
    plan, outs, start = [], [], 0
    for cut in cuts:
        stack, parts = (None, cut) if not isinstance(cut, tuple) else (cut[0], cut[1:])
        parts = (parts,) if stack is None else parts
        plan.append((stack, [(start + sum(parts[:i]), part) for i, part in enumerate(parts)]))
        start += sum(parts)
        shape = (rows, parts[0])
        if stack is not None:
            shape = shape[:stack] + (len(parts),) + shape[stack:]
        outs.append(shaped(shape, F32))

    def body(keep_ref, other_ref, *refs):
        for (stack, spans), ref in zip(plan, refs):
            for index, (low, size) in enumerate(spans):
                span = slice(low, low + size)
                value = full(keep_ref[:, span]) + full(other_ref[:, span])
                if stack is None:
                    ref[...] = value
                elif stack == 0:
                    ref[index] = value
                else:
                    ref[:, index, :] = value

    if rows != 48:
        total = full(keep) + full(other)
        cuts = [[total[:, low : low + size] for low, size in spans] for _, spans in plan]
        return [pieces[0] if stack is None else jnp.stack(pieces, stack) for (stack, _), pieces in zip(plan, cuts)]
    kinds = [NEAR, NEAR] + [AFTER] * len(after)
    return call(body, outs, kinds, cuts=[LATE] * len(outs), cost=2, vmem=SMALL_BYTES)(keep, other, *after)


class Sum:
    def __init__(self, scalars, orders, count, products, width, after=(), far=()):
        self.orders, self.count, self.phase = orders, count, 0
        self.bits = count.bit_length() - 1
        if count > 1 and (products[0][0].shape[1] // count) % 16 == 0:
            self.keep, self.send = weight_grads(scalars, orders, count, products, width, tuple(after), far)
        else:
            self.keep, self.send = weight_grads_plain(orders, count, products, width)
        self.first = self.keep
        if self.bits:
            self.move()
        else:
            self.other = jnp.zeros_like(self.keep)

    def move(self):
        pairs = fold_pairs(self.orders, self.count, self.phase)
        self.other = lax.ppermute(self.send, ("seq", "tp"), pairs)

    def fold(self, *after, beside=None):
        if self.phase + 1 < self.bits:
            self.phase += 1
            extra = beside.terms() if beside is not None else ()
            results = fold(self.keep, self.other, tuple(after), extra)
            self.keep, self.send = results[:2]
            if extra:
                beside.take(results[2])
            self.move()
        return self.keep

    def finish(self, *cuts, after=()):
        while self.phase + 1 < self.bits:
            self.fold()
        return fold_last(self.keep, self.other, cuts, tuple(after))


class Spread:
    def __init__(self, values, count):
        self.values, self.count, self.distance = values, count, 1
        self.move()

    def move(self):
        if self.distance < self.count:
            pairs = [(index, index ^ self.distance) for index in range(self.count)]
            self.other = lax.ppermute(self.values, "seq", pairs)

    def terms(self):
        return (self.values, self.other) if self.distance < self.count else ()

    def take(self, total):
        self.values = total
        self.distance *= 2
        self.move()

    def finish(self):
        while self.distance < self.count:
            self.take(self.values + self.other)
        return self.values


def on_device(count, *arguments):
    (
        tokens, seq_lengths, cotangent, norm1_gain, norm1_shift, qkv1_weight, qv1_bias, out1_weight, out1_bias,
        norm2_gain, norm2_shift, fc1_weight, fc1_bias, proj1_weight, proj1_bias, norm3_gain, norm3_shift,
        qk2_weight, v2_weight, q2_bias, v2_bias, out2_weight, out2_bias, norm4_gain, norm4_shift, fc2_weight,
        fc2_bias, proj2_weight, proj2_bias,
    ) = arguments
    mid, model = tokens.shape
    rows = 2 * mid
    local = qkv1_weight.shape[2]
    fresh = v2_weight.shape[1]
    hidden = fc1_weight.shape[1]
    core = lax.axis_index("tp")
    scalars = jnp.stack([core, seq_lengths[0], lax.axis_index("seq")]).astype(jnp.int32)
    qkv1 = qkv1_weight.transpose(1, 0, 2)
    qk2 = qk2_weight.transpose(1, 0, 2)
    fresh_weight = v2_weight.T

    square, narrow = (rows, model), (rows, local)
    heads = local // HEAD_DIM
    by_head = (0, heads)
    weights_out = shaped((heads, rows, rows))
    bias_scratch = pltpu.VMEM((rows, rows), F32)
    attend_outs = [shaped(square)] + [shaped(narrow)] * 4 + [weights_out, shaped(square)]
    pull_scratch = [pltpu.VMEM(narrow, BF16), pltpu.VMEM((2, rows, rows), BF16)]
    pull_outs = [shaped(square, F32), shaped(square), shaped(narrow), shaped(narrow)]
    sums_outs = [shaped(square), shaped((8, model), F32), shaped((8, local), F32)]
    total_scratch = pltpu.VMEM(square, F32)
    hidden_out, by_column, by_row = shaped((rows, hidden)), (1, HIDDEN_CUT), (0, HIDDEN_CUT)
    feed_sums = [shaped(square), shaped((8, model), F32), shaped((8, hidden), F32)]

    x0, n1, q1, k1, v1, o1, p1, part = call(
        attend_first, [shaped(square)] + attend_outs, [SCALARS, LATE, NEAR] + [LATE] * 5,
        cuts=[NEAR, LATE, LATE, LATE, NEAR, LATE, by_head, NEAR], scratch=[bias_scratch], cost=8,
    )(scalars, tokens, swap(tokens), norm1_gain, norm1_shift, qv1_bias, qkv1, out1_weight)
    x1, m1, z1, pull1, part = call(
        feed_first,
        [shaped(square, F32), shaped(square), hidden_out, hidden_out, shaped(square)],
        [NEAR, NEAR, NEAR] + [LATE] * 4 + [by_column, by_row],
        cuts=[NEAR, LATE, by_column, by_column, NEAR],
        scratch=[total_scratch],
        cost=8,
    )(x0, part, swap(part), out1_bias, norm2_gain, norm2_shift, fc1_bias, fc1_weight, proj1_weight)

    x2, n3, q2, k2, v2, o2, p2, part = call(
        attend_second, [shaped(square, F32)] + attend_outs, [SCALARS, NEAR, NEAR, NEAR] + [LATE] * 7 + [NEAR, LATE],
        cuts=[NEAR, LATE, NEAR, NEAR, NEAR, LATE, by_head, NEAR], scratch=[bias_scratch], cost=10,
    )(scalars, x1, part, swap(part), proj1_bias, norm3_gain, norm3_shift, q2_bias, v2_bias, qk2, fresh_weight, v1,
      out2_weight)
    x3, m3, gb4, z3, du3, out_part, part, pulled, rep4, loc4 = call(
        feed_second,
        [shaped(square, F32), shaped(square), shaped(square), hidden_out, hidden_out]
        + [shaped((mid, model)), shaped((mid, model))] + feed_sums,
        [SCALARS, NEAR, NEAR, NEAR] + [LATE] * 5 + [NEAR, by_column, by_row],
        cuts=[NEAR] * 10,
        scratch=[total_scratch, total_scratch],
        vmem=BIG_BYTES,
        cost=12,
    )(scalars, x2, part, swap(part), out2_bias, norm4_gain, norm4_shift, fc2_bias, cotangent, swap(cotangent),
      fc2_weight, proj2_weight)
    pulled_other = swap(pulled)
    out_other = swap(part)
    first = Sum(scalars, FIRST_ORDERS, count, [(m3, [du3]), (gb4, [z3])], 2 * hidden)

    g3, gb3, dq2, dk2, dv2, df2, part, rep3, loc3 = call(
        pull_second, pull_outs + [shaped(narrow, F32), shaped(narrow)] + sums_outs,
        [NEAR] * 4 + [LATE] + [NEAR] * 3 + [by_head] + [LATE] * 3 + [AFTER], cuts=[NEAR] * 9,
        scratch=pull_scratch, cost=14,
    )(gb4, pulled, pulled_other, x3, norm4_gain, q2, k2, v2, p2, qk2, fresh_weight, out2_weight, first.keep)
    part_other = swap(part)
    second = Sum(
        scalars, SECOND_ORDERS, count, [(gb3, [o2]), (n3, [dq2, dk2, df2])], 3 * local + 2 * 128, far=(o2, n3)
    )

    g2, gb2, du1, pulled, rep2, loc2 = call(
        feed_pull,
        [shaped(square, F32), shaped(square), hidden_out] + feed_sums,
        [NEAR, NEAR, NEAR, NEAR, LATE, by_column, by_column, by_row, AFTER],
        cuts=[NEAR] * 6,
        scratch=[total_scratch],
        cost=8,
    )(g3, part, part_other, x2, norm3_gain, pull1, fc1_weight, proj1_weight, second.keep)
    pulled_other = swap(pulled)
    third = Sum(scalars, THIRD_ORDERS, count, [(m1, [du1])], hidden, far=(m1,))
    first.fold(third.first)
    fourth = Sum(scalars, FOURTH_ORDERS, count, [(gb2, [z1])], hidden, [first.keep], far=(z1,))
    second.fold(fourth.first)

    g1, gb1, dq1, dk1, dv1, own_part, part, rep1, loc1 = call(
        functools.partial(pull_first, fresh=fresh),
        pull_outs + [shaped(narrow), shaped((mid, model)), shaped((mid, model))] + sums_outs[1:],
        [SCALARS] + [NEAR] * 4 + [LATE] * 3 + [NEAR, by_head, LATE, NEAR, LATE, AFTER],
        cuts=[NEAR] * 9,
        scratch=pull_scratch + [pltpu.VMEM(narrow, F32), pltpu.VMEM(square, BF16)],
        cost=12,
    )(scalars, g2, pulled, pulled_other, x1, norm2_gain, q1, k1, v1, p1, qkv1, dv2, out1_weight, second.keep)
    part_other = swap(part)
    first.fold(g1)
    fifth = Sum(
        scalars, FIFTH_ORDERS, count, [(gb1, [o1]), (n1, [dq1, dk1, dv1])], 4 * local, [first.keep], far=(o1, n1)
    )
    tokens_grad, packed = call(
        pull_tokens, [shaped((mid, model)), shaped((PACKED, model), F32)],
        [SCALARS] + [NEAR] * 4 + [LATE] + [NEAR] * 8 + [AFTER], cuts=[LATE, NEAR], cost=3,
    )(scalars, g1, own_part, part_other, x0, norm1_gain, rep4, rep3, rep2, rep1, loc4, loc3, loc2, loc1, fifth.first)
    packed = Spread(packed, count)

    third.fold(packed.values)
    fourth.fold(third.keep, beside=packed)
    second.fold(fourth.keep)
    fifth.fold(second.keep, beside=packed)
    first.fold(fifth.keep)
    layer_output = call(finish_layer, shaped((mid, model)), [SCALARS, NEAR, NEAR, NEAR, LATE, AFTER], cost=2)(
        scalars, x3, out_part, out_other, proj2_bias, first.keep
    )
    third.fold(layer_output)
    second.fold(third.keep, beside=packed)
    fourth.fold(second.keep)
    sum_fc2, sum_proj2 = first.finish(hidden, hidden, after=[fourth.keep])
    fifth.fold(sum_fc2, beside=packed)
    third.fold(fifth.keep)
    fourth.fold(third.keep)
    sum_out2, sum_qk2, sum_v2 = second.finish(local, (1, local, local), fresh, after=[fourth.keep])
    fifth.fold(sum_out2)
    (sum_fc1,) = third.finish(hidden, after=[fifth.keep])
    (sum_proj1,) = fourth.finish(hidden, after=[sum_fc1])
    sum_out1, sum_qkv1 = fifth.finish(local, (0, local, local, local), after=[sum_proj1])
    sum_qkv1 = sum_qkv1.transpose(1, 0, 2)

    packed = packed.finish()
    vector, small = shaped((model,), F32), shaped((2 * fresh,), F32)
    long_vector = shaped((2 * hidden,), F32)
    (
        sum_gain1, sum_shift1, sum_qv1_bias, sum_out1_bias, sum_gain2, sum_shift2, sum_fc1_bias, sum_proj1_bias,
        sum_gain3, sum_shift3, sum_q2_bias, sum_v2_bias, sum_out2_bias, sum_gain4, sum_shift4, sum_fc2_bias,
        sum_proj2_bias,
    ) = call(
        unpack_sums,
        [vector, vector, shaped((2, model), F32), vector, vector, vector, long_vector, vector,
         vector, vector, vector, small, vector, vector, vector, long_vector, vector],
        [SCALARS, NEAR, NEAR],
        cost=2,
    )(scalars, packed, swap(packed))
    return (
        layer_output, tokens_grad, sum_gain1, sum_shift1, sum_qkv1, sum_qv1_bias, sum_out1.T, sum_out1_bias,
        sum_gain2, sum_shift2, sum_fc1, sum_fc1_bias, sum_proj1.T, sum_proj1_bias, sum_gain3, sum_shift3, sum_qk2,
        sum_v2, sum_q2_bias, sum_v2_bias, sum_out2.T, sum_out2_bias, sum_gain4, sum_shift4, sum_fc2, sum_fc2_bias,
        sum_proj2.T, sum_proj2_bias,
    )


def solution(mesh):
    rows, copied = P(("seq", "tp"), None), P()
    columns, deep = P(None, "tp"), P("tp", None)
    wide, long = P("seq", "tp"), P("tp", "seq")
    count = mesh.shape["seq"]

    def body(*arguments):
        return on_device(count, *arguments)

    return jax.shard_map(
        body,
        mesh=mesh,
        in_specs=(
            rows, P("seq"), rows, copied, copied, P(None, None, "tp"), columns, deep, copied,
            copied, copied, columns, P("tp"), deep, copied, copied, copied,
            P(None, None, "tp"), columns, P("tp"), P("tp"), deep, copied, copied, copied, columns,
            P("tp"), deep, copied,
        ),
        out_specs=(
            rows, rows, copied, copied, P("seq", None, "tp"), copied, long, copied,
            copied, copied, wide, copied, long, copied, copied, copied, P("seq", None, "tp"),
            wide, copied, copied, long, copied, copied, copied, wide, copied,
            long, copied,
        ),
        check_vma=False,
    )
```

```python
import functools

import jax
import jax.numpy as jnp
import numpy as np
from jax import lax
from jax.experimental import pallas as pl
from jax.experimental.pallas import tpu as pltpu
from jax.sharding import PartitionSpec as P

HEAD_DIM = 64
F32 = jnp.float32
BF16 = jnp.bfloat16


def half(values):
    return values.astype(BF16)


def full(values):
    return values.astype(F32)


def dot(left, right):
    return lax.dot_general(left, right, (((1,), (0,)), ((), ())), preferred_element_type=F32)


def dot_nt(left, right):
    return lax.dot_general(left, right, (((1,), (1,)), ((), ())), preferred_element_type=F32)


def dot_tn(left, right):
    return lax.dot_general(left, right, (((0,), (0,)), ((), ())), preferred_element_type=F32)


def swap(values):
    return lax.ppermute(values, "tp", [(0, 1), (1, 0)])


BLOCK = 256
HIDDEN_CUT = 2
VMEM_BYTES, BIG_BYTES = 16 * 1024 * 1024, 16 * 1024 * 1024


class Arriving:
    def __init__(self, source, buffer, sems, first, cut):
        self.source, self.buffer, self.shape, self.dtype = source, buffer, source.shape, source.dtype
        axis, count = cut
        size = source.shape[axis] // count
        self.copies = []
        for index in range(count):
            at = (slice(None),) * axis + (pl.ds(index * size, size),)
            here, there = (source, buffer) if count == 1 else (source.at[at], buffer.at[at])
            self.copies.append(pltpu.make_async_copy(here, there, sems.at[first + index]))
        self.waiting = set(range(count))

    def start(self, index):
        if index < len(self.copies):
            self.copies[index].start()

    def piece(self, index):
        if index in self.waiting:
            self.waiting.remove(index)
            self.copies[index].wait()
        return self.buffer

    def whole(self):
        for index in range(len(self.copies)):
            self.piece(index)
        return self.buffer

    def __getitem__(self, at):
        return self.whole()[at]


class Held:
    def __init__(self, ref):
        self.buffer, self.shape, self.dtype, self.copies = ref, ref.shape, ref.dtype, [None]

    def piece(self, index):
        return self.buffer

    def send(self, index=0):
        pass

    def __getitem__(self, at):
        return self.buffer[at]

    def __setitem__(self, at, value):
        self.buffer[at] = value


class Leaving:
    def __init__(self, target, buffer, sems, first, cut):
        self.target, self.buffer, self.shape, self.dtype = target, buffer, target.shape, target.dtype
        axis, count = cut
        size = target.shape[axis] // count
        self.copies = []
        for index in range(count):
            at = (slice(None),) * axis + (pl.ds(index * size, size),)
            here, there = (buffer, target) if count == 1 else (buffer.at[at], target.at[at])
            self.copies.append(pltpu.make_async_copy(here, there, sems.at[first + index]))
        self.held = set(range(count))

    def send(self, index=0):
        self.held.remove(index)
        self.copies[index].start()

    def finish(self):
        for index in sorted(self.held):
            self.send(index)

    def __getitem__(self, at):
        return self.buffer[at]

    def __setitem__(self, at, value):
        self.buffer[at] = value


SCALARS, AFTER, NEAR, LATE = "scalars", "after", "near", (0, 1)


SPACES = {SCALARS: pltpu.SMEM, NEAR: pltpu.VMEM, AFTER: pl.ANY}


def placed(operand, kind):
    if kind in (SCALARS, AFTER):
        return operand
    return pltpu.with_memory_space_constraint(operand, pltpu.VMEM if kind == NEAR else pltpu.HBM)


TOLD = 0.75


def call(body, outs, ins, cuts=None, scratch=(), cost=1.0, vmem=None):
    single = not isinstance(outs, (list, tuple))
    outs = [outs] if single else list(outs)
    cuts = list(cuts) if cuts is not None else [LATE] * len(outs)
    late = [index for index, kind in enumerate(ins) if isinstance(kind, tuple)]
    in_counts = [ins[index][1] for index in late]
    far = [index for index, kind in enumerate(cuts) if isinstance(kind, tuple)]
    out_counts = [cuts[index][1] for index in far]

    def wrapped(*refs):
        refs = list(refs)
        operands, refs = refs[: len(ins)], refs[len(ins) :]
        targets, refs = refs[: len(outs)], refs[len(outs) :]
        extra, refs = refs[: len(scratch)], refs[len(scratch) :]
        in_buffers, refs = refs[: len(late)], refs[len(late) :]
        out_buffers, sems = refs[: len(far)], refs[len(far) :]
        in_sems, out_sems = sems[0] if late else None, sems[-1] if far else None
        arriving = {
            index: Arriving(operands[index], in_buffers[at], in_sems, sum(in_counts[:at]), ins[index])
            for at, index in enumerate(late)
        }
        for index in range(max(in_counts, default=0)):
            for operand in arriving.values():
                operand.start(index)
        leaving = {
            index: Leaving(targets[index], out_buffers[at], out_sems, sum(out_counts[:at]), cuts[index])
            for at, index in enumerate(far)
        }
        results = [leaving[index] if index in leaving else Held(target) for index, target in enumerate(targets)]
        given = [
            arriving[index] if index in arriving else Held(operands[index]) if kind == NEAR else operands[index]
            for index, kind in enumerate(ins)
            if kind != AFTER
        ]
        body(*given, *results, *extra)
        for operand in arriving.values():
            operand.whole()
        for result in leaving.values():
            result.finish()
        for result in leaving.values():
            for copy in result.copies:
                copy.wait()

    def run(*operands):
        buffers = [pltpu.VMEM(operands[index].shape, operands[index].dtype) for index in late]
        buffers += [pltpu.VMEM(outs[index].shape, outs[index].dtype) for index in far]
        sems = [pltpu.SemaphoreType.DMA((sum(counts),)) for counts in (in_counts, out_counts) if counts]
        results = pl.pallas_call(
            wrapped,
            out_shape=[
                (pltpu.VMEM if kind == NEAR else pltpu.HBM)(out.shape, out.dtype) for out, kind in zip(outs, cuts)
            ],
            in_specs=[pl.BlockSpec(memory_space=SPACES.get(kind, pltpu.HBM)) for kind in ins],
            out_specs=[pl.BlockSpec(memory_space=SPACES.get(kind, pltpu.HBM)) for kind in cuts],
            scratch_shapes=list(scratch) + buffers + sems,
            compiler_params=pltpu.CompilerParams(vmem_limit_bytes=vmem or VMEM_BYTES),
            cost_estimate=pl.CostEstimate(
                flops=int(cost * TOLD * 1.1e9), bytes_accessed=int(cost * TOLD * 3.4e6), transcendentals=0
            ),
        )(*(placed(operand, kind) for operand, kind in zip(operands, ins)))
        return results[0] if single else results

    return run


def shaped(shape, kind=BF16):
    return jax.ShapeDtypeStruct(shape, kind)


def row(ref):
    return full(ref[...][None, :])


def norm_stats(values):
    mean = jnp.mean(values, axis=-1, keepdims=True)
    centered = values - mean
    scale = lax.rsqrt(jnp.mean(centered * centered, axis=-1, keepdims=True) + 1e-05)
    return centered * scale, scale


def norm_backward(grad, values, gain):
    hat, scale = norm_stats(values)
    inner = grad * gain
    mean_inner = jnp.mean(inner, axis=-1, keepdims=True)
    mean_hat = jnp.mean(inner * hat, axis=-1, keepdims=True)
    pulled = scale * (inner - mean_inner - hat * mean_hat)
    return (
        pulled,
        jnp.sum(grad * hat, axis=0, keepdims=True),
        jnp.sum(grad, axis=0, keepdims=True),
    )


def gelu_both(values):
    square = values * values
    bent = jnp.tanh(values * (0.7978845608028654 + 0.035677408136300125 * square))
    rise = 0.5 + 0.5 * bent
    slope = 0.7978845608028654 + 0.10703222440890038 * square
    pull = rise + (0.5 * values) * (1.0 - bent * bent) * slope
    return values * rise, pull


def head_lanes(width, which):
    lane = lax.broadcasted_iota(jnp.int32, (1, width), 1)
    return (lane // HEAD_DIM) == which


def keep_lanes(values, lanes):
    return jnp.where(lanes, values, jnp.zeros_like(values))


def fill_bias(bias_ref, length):
    query = lax.broadcasted_iota(jnp.int32, bias_ref.shape, 0)
    key = lax.broadcasted_iota(jnp.int32, bias_ref.shape, 1)
    bias_ref[...] = jnp.where((key <= query) & (key < length), 0.0, -1e30)


def turned_heads(pair):
    turned = full(pair).T
    return [half(turned[which * HEAD_DIM : (which + 1) * HEAD_DIM]) for which in range(2)]


def attend_rows(q_ref, k_ref, v_ref, o_ref, p_ref, bias_ref, length):
    fill_bias(bias_ref, length)
    for pair in range(q_ref.shape[1] // 128):
        lanes = slice(pair * 128, pair * 128 + 128)
        keys, values = k_ref[:, lanes], v_ref[:, lanes]
        total = None
        for which in range(2):
            mask = head_lanes(128, which)
            query = keep_lanes(q_ref[:, lanes] * 0.125, mask).astype(BF16)
            scores = dot_nt(query, keys) + bias_ref[...]
            weights = jnp.exp(scores - jnp.max(scores, axis=-1, keepdims=True))
            weights = weights * (1.0 / jnp.sum(weights, axis=-1, keepdims=True))
            p_ref[2 * pair + which] = half(weights.T)
            p_ref.send(2 * pair + which)
            mixed = dot(half(weights), keep_lanes(values, mask))
            total = mixed if total is None else total + mixed
        o_ref[:, lanes] = half(total)


def attend_first(scal_ref, mine_ref, other_ref, gain_ref, shift_ref, bias_refs, w_ref, out_ref,
                 x_ref, n_ref, q_ref, k_ref, v_ref, o_ref, p_ref, part_ref, bias_ref):
    core, length = scal_ref[0], scal_ref[1]
    mid = mine_ref.shape[0]
    x_ref[pl.ds(pl.multiple_of(core * mid, mid), mid), :] = mine_ref[...]
    x_ref[pl.ds(pl.multiple_of((1 - core) * mid, mid), mid), :] = other_ref[...]
    hat, _ = norm_stats(full(x_ref[...]))
    normed = half(hat * row(gain_ref) + row(shift_ref))
    n_ref[...] = normed
    x_ref.send()
    n_ref.send()
    q_ref[...] = half(dot(normed, w_ref.piece(0)[0]) + full(bias_refs[0:1, :]))
    k_ref[...] = half(dot(normed, w_ref.piece(1)[1]))
    v_ref[...] = half(dot(normed, w_ref.piece(2)[2]) + full(bias_refs[1:2, :]))
    for ref in (q_ref, k_ref, v_ref):
        ref.send()
    attend_rows(q_ref, k_ref, v_ref, o_ref, p_ref, bias_ref, length)
    o_ref.send()
    part_ref[...] = half(dot(o_ref[...], out_ref[...]))


def attend_second(scal_ref, prev_ref, mine_ref, other_ref, before_ref, gain_ref, shift_ref, qb_ref, fb_ref,
                  w_ref, f_ref, v1_ref, out_ref,
                  x_ref, n_ref, q_ref, k_ref, v_ref, o_ref, p_ref, part_ref, bias_ref):
    length = scal_ref[1]
    x_ref[...] = prev_ref[...] + (full(mine_ref[...]) + full(other_ref[...])) + row(before_ref)
    hat, _ = norm_stats(x_ref[...])
    normed = half(hat * row(gain_ref) + row(shift_ref))
    n_ref[...] = normed
    x_ref.send()
    n_ref.send()
    fresh = f_ref.shape[0]
    q_ref[...] = half(dot(normed, w_ref.piece(0)[0]) + row(qb_ref))
    k_ref[...] = half(dot(normed, w_ref.piece(1)[1]))
    v_ref[...] = v1_ref[...]
    v_ref[:, :fresh] = half(dot_nt(normed, f_ref[...]) + row(fb_ref))
    for ref in (q_ref, k_ref, v_ref):
        ref.send()
    attend_rows(q_ref, k_ref, v_ref, o_ref, p_ref, bias_ref, length)
    o_ref.send()
    part_ref[...] = half(dot(o_ref[...], out_ref[...]))


def attend_pull(q_ref, k_ref, v_ref, p_ref, do_ref, dq_ref, dk_ref, dv_ref, ds_ref):
    rows, width = q_ref.shape
    heads = width // HEAD_DIM
    blocks = rows // BLOCK
    ones = jnp.ones((16, rows), BF16)
    for pair in range(heads // 2):
        lanes = slice(pair * 128, pair * 128 + 128)
        keys, values = turned_heads(k_ref[:, lanes]), v_ref[:, lanes]
        pulled_query, queries, grads = {}, {}, {}
        for which in range(2):
            head = 2 * pair + which
            p_ref.piece(head)
            mask = head_lanes(128, which)
            queries[which] = keep_lanes(q_ref[:, lanes] * 0.125, mask).astype(BF16)
            grads[which] = keep_lanes(do_ref[:, lanes], mask)
            for block in range(blocks):
                start, stop = block * BLOCK, (block + 1) * BLOCK
                pulled = dot_nt(values[:stop], grads[which][start:stop])
                weights = full(p_ref.buffer[head, :stop, start:stop])
                total = dot(ones[:, :stop], p_ref.buffer[head, :stop, start:stop])[0:1, :]
                centre = jnp.sum(weights * pulled, axis=0, keepdims=True) * (1.0 / total)
                score_grad = half(weights * (pulled - centre))
                ds_ref[which, :stop, start:stop] = score_grad
                pulled_query[block, which] = dot(keys[which][:, :stop], score_grad)
        for block in range(blocks):
            start, stop = block * BLOCK, (block + 1) * BLOCK
            joined = jnp.concatenate([pulled_query[block, 0], pulled_query[block, 1]], axis=0) * 0.125
            dq_ref[start:stop, lanes] = half(joined.T)
            dk_ref[start:stop, lanes] = half(
                dot(ds_ref[0, start:stop, start:], queries[0][start:])
                + dot(ds_ref[1, start:stop, start:], queries[1][start:])
            )
            dv_ref[start:stop, lanes] = dot(
                p_ref.buffer[2 * pair, start:stop, start:], grads[0][start:]
            ) + dot(p_ref.buffer[2 * pair + 1, start:stop, start:], grads[1][start:])


def column_sum(values):
    return jnp.sum(full(values), axis=0, keepdims=True)


def pull_second(g4_ref, mine_ref, other_ref, x_ref, gain_ref, out_ref, q_ref, k_ref, v_ref, p_ref, w_ref, f_ref,
                g_ref, gb_ref, dq_ref, dk_ref, dv_ref, dvb_ref, part_ref, rep_ref, loc_ref,
                do_ref, ds_ref):
    grad = full(mine_ref[...]) + full(other_ref[...])
    pulled, gain, shift = norm_backward(grad, x_ref[...], row(gain_ref))
    g_ref[...] = full(g4_ref[...]) + pulled
    rep_ref[...] = jnp.zeros_like(rep_ref)
    loc_ref[...] = jnp.zeros_like(loc_ref)
    rep_ref[0:1, :] = gain
    rep_ref[1:2, :] = shift
    rep_ref[2:3, :] = column_sum(g_ref[...])
    gb_ref[...] = half(g_ref[...])
    g_ref.send()
    gb_ref.send()
    do_ref[...] = half(dot_nt(gb_ref[...], out_ref[...]))
    attend_pull(q_ref, k_ref, v_ref, p_ref, do_ref, dq_ref, dk_ref, dv_ref, ds_ref)
    fresh = f_ref.shape[0]
    dvb_ref[...] = half(dv_ref[...])
    fresh_grad = dvb_ref[:, :fresh]
    part_ref[...] = half(
        dot_nt(dq_ref[...], w_ref[0]) + dot_nt(dk_ref[...], w_ref[1]) + dot(fresh_grad, f_ref[...])
    )
    loc_ref[0:1, :] = column_sum(dq_ref[...])
    loc_ref[1:2, :] = column_sum(dvb_ref[...])


def pull_first(scal_ref, g2_ref, mine_ref, other_ref, x_ref, gain_ref, out_ref, q_ref, k_ref, v_ref, p_ref, w_ref, reused_ref,
               g_ref, gb_ref, dq_ref, dk_ref, dv_ref, own_ref, part_ref, rep_ref, loc_ref,
               do_ref, ds_ref, dv_full, partial, *, fresh):
    grad = full(mine_ref[...]) + full(other_ref[...])
    pulled, gain, shift = norm_backward(grad, x_ref[...], row(gain_ref))
    g_ref[...] = g2_ref[...] + pulled
    rep_ref[...] = jnp.zeros_like(rep_ref)
    loc_ref[...] = jnp.zeros_like(loc_ref)
    rep_ref[0:1, :] = gain
    rep_ref[1:2, :] = shift
    rep_ref[2:3, :] = column_sum(g_ref[...])
    gb_ref[...] = half(g_ref[...])
    g_ref.send()
    gb_ref.send()
    do_ref[...] = half(dot_nt(gb_ref[...], out_ref[...]))
    attend_pull(q_ref, k_ref, v_ref, p_ref, do_ref, dq_ref, dk_ref, dv_full, ds_ref)
    column = lax.broadcasted_iota(jnp.int32, (1, dv_full.shape[1]), 1)
    dv_ref[...] = half(dv_full[...] + jnp.where(column >= fresh, reused_ref[...], 0.0))
    partial[...] = half(
        dot_nt(dq_ref[...], w_ref[0]) + dot_nt(dk_ref[...], w_ref[1]) + dot_nt(dv_ref[...], w_ref[2])
    )
    core, mid = scal_ref[0], own_ref.shape[0]
    own_ref[...] = partial[pl.ds(pl.multiple_of(core * mid, mid), mid), :]
    part_ref[...] = partial[pl.ds(pl.multiple_of((1 - core) * mid, mid), mid), :]
    loc_ref[0:1, :] = column_sum(dq_ref[...])
    loc_ref[1:2, :] = column_sum(dv_ref[...])


ROW_BLOCK = 256


def hidden_spans(ref):
    size = ref.shape[1] // HIDDEN_CUT
    return [slice(index * size, (index + 1) * size) for index in range(HIDDEN_CUT)]


def add_to(total, span, value, fresh):
    total[span, :] = value if fresh else total[span, :] + value


def feed_first(prev_ref, mine_ref, other_ref, before_ref, gain_ref, shift_ref, bias_ref, fc_ref, proj_ref,
               x_ref, m_ref, z_ref, pull_ref, part_ref, total):
    x_ref[...] = full(prev_ref[...]) + (full(mine_ref[...]) + full(other_ref[...])) + row(before_ref)
    x_ref.send()
    hat, _ = norm_stats(x_ref[...])
    m_ref[...] = half(hat * row(gain_ref) + row(shift_ref))
    m_ref.send()
    for index, columns in enumerate(hidden_spans(fc_ref)):
        fc, proj = fc_ref.piece(index), proj_ref.piece(index)
        bias = full(bias_ref[columns][None, :])
        for low in range(0, m_ref.shape[0], ROW_BLOCK):
            span = slice(low, low + ROW_BLOCK)
            value, pull = gelu_both(dot(m_ref[span, :], fc[:, columns]) + bias)
            value = half(value)
            z_ref[span, columns] = value
            pull_ref[span, columns] = half(pull)
            add_to(total, span, dot(value, proj[columns, :]), index == 0)
        z_ref.send(index)
        pull_ref.send(index)
    part_ref[...] = half(total[...])


def feed_second(scal_ref, prev_ref, mine_ref, other_ref, before_ref, gain_ref, shift_ref, bias_ref,
                cot_ref, cot_other_ref, fc_ref, proj_ref,
                x_ref, m_ref, g_ref, z_ref, du_ref, own_ref, part_ref, pulled_ref, rep_ref, loc_ref, total, pulled_total):
    core, length = scal_ref[0], scal_ref[1]
    x_ref[...] = prev_ref[...] + (full(mine_ref[...]) + full(other_ref[...])) + row(before_ref)
    x_ref.send()
    hat, _ = norm_stats(x_ref[...])
    m_ref[...] = half(hat * row(gain_ref) + row(shift_ref))
    m_ref.send()
    mid = cot_ref.shape[0]
    place = lax.broadcasted_iota(jnp.int32, (mid, 1), 0)
    for source, owner in ((cot_ref, core), (cot_other_ref, 1 - core)):
        base = pl.multiple_of(owner * mid, mid)
        alive = (place + base < length).astype(F32)
        g_ref[pl.ds(base, mid), :] = half(full(source[...]) * alive)
    g_ref.send()
    rep_ref[...] = jnp.zeros_like(rep_ref)
    loc_ref[...] = jnp.zeros_like(loc_ref)
    rep_ref[0:1, :] = column_sum(g_ref[...])
    for index, columns in enumerate(hidden_spans(fc_ref)):
        fc, proj = fc_ref.piece(index), proj_ref.piece(index)
        bias = full(bias_ref[columns][None, :])
        sums = None
        for low in range(0, m_ref.shape[0], ROW_BLOCK):
            span = slice(low, low + ROW_BLOCK)
            value, pull = gelu_both(dot(m_ref[span, :], fc[:, columns]) + bias)
            value = half(value)
            z_ref[span, columns] = value
            add_to(total, span, dot(value, proj[columns, :]), index == 0)
            du = half(dot_nt(g_ref[span, :], proj[columns, :]) * pull)
            du_ref[span, columns] = du
            add_to(pulled_total, span, dot_nt(du, fc[:, columns]), index == 0)
            sums = column_sum(du) if sums is None else sums + column_sum(du)
        loc_ref[0:1, columns] = sums
        z_ref.send(index)
        du_ref.send(index)
    own_ref[...] = half(total[pl.ds(pl.multiple_of(core * mid, mid), mid), :])
    part_ref[...] = half(total[pl.ds(pl.multiple_of((1 - core) * mid, mid), mid), :])
    pulled_ref[...] = half(pulled_total[...])


def feed_pull(g3_ref, mine_ref, other_ref, xin_ref, gain_ref, pull_ref, fc_ref, proj_ref,
              g_ref, gb_ref, du_ref, pulled_ref, rep_ref, loc_ref, pulled_total):
    grad = full(mine_ref[...]) + full(other_ref[...])
    pulled, gain, shift = norm_backward(grad, xin_ref[...], row(gain_ref))
    g_ref[...] = g3_ref[...] + pulled
    g_ref.send()
    rep_ref[...] = jnp.zeros_like(rep_ref)
    loc_ref[...] = jnp.zeros_like(loc_ref)
    rep_ref[0:1, :] = gain
    rep_ref[1:2, :] = shift
    rep_ref[2:3, :] = column_sum(g_ref[...])
    gb_ref[...] = half(g_ref[...])
    gb_ref.send()
    for index, columns in enumerate(hidden_spans(fc_ref)):
        fc, proj = fc_ref.piece(index), proj_ref.piece(index)
        pull = pull_ref.piece(index)
        sums = None
        for low in range(0, gb_ref.shape[0], ROW_BLOCK):
            span = slice(low, low + ROW_BLOCK)
            du = half(dot_nt(gb_ref[span, :], proj[columns, :]) * full(pull[span, columns]))
            du_ref[span, columns] = du
            add_to(pulled_total, span, dot_nt(du, fc[:, columns]), index == 0)
            sums = column_sum(du) if sums is None else sums + column_sum(du)
        loc_ref[0:1, columns] = sums
        du_ref.send(index)
    pulled_ref[...] = half(pulled_total[...])


PACKED, SHARED = 24, 10


def pull_tokens(scal_ref, g1_ref, mine_ref, other_ref, x_ref, gain_ref,
                rep4_ref, rep3_ref, rep2_ref, rep1_ref, loc4_ref, loc3_ref, loc2_ref, loc1_ref,
                out_ref, pack_ref):
    mid, model = out_ref.shape
    own = pl.ds(pl.multiple_of(scal_ref[0] * mid, mid), mid)
    grad = full(mine_ref[...]) + full(other_ref[...])
    pulled, gain, shift = norm_backward(grad, full(x_ref[own, :]), row(gain_ref))
    out_ref[...] = half(g1_ref[own, :] + pulled)
    pack_ref[...] = jnp.zeros_like(pack_ref)
    pack_ref[0:1, :] = rep4_ref[0:1, :]
    for index, ref in enumerate((rep3_ref, rep2_ref, rep1_ref)):
        pack_ref[1 + 3 * index : 4 + 3 * index, :] = ref[0:3, :]
    pack_ref[SHARED : SHARED + 1, :] = gain
    pack_ref[SHARED + 1 : SHARED + 2, :] = shift
    for index, ref in enumerate((loc4_ref, loc2_ref)):
        for part in range(2):
            at = SHARED + 2 + 2 * index + part
            pack_ref[at : at + 1, :] = ref[0:1, part * model : (part + 1) * model]
    for index, ref in enumerate((loc3_ref, loc1_ref)):
        at = SHARED + 6 + index
        for part in range(2):
            pack_ref[at : at + 1, part * model // 2 : (part + 1) * model // 2] = ref[part : part + 1, :]


def unpack_sums(scal_ref, mine_ref, other_ref, *outs):
    first = scal_ref[0] == 0
    (gain1, shift1, qv1, out1, gain2, shift2, fc1, proj1,
     gain3, shift3, q2, v2, out2, gain4, shift4, fc2, proj2) = outs
    same = (proj2, gain4, shift4, out2, gain3, shift3, proj1, gain2, shift2, out1)
    for index, ref in enumerate(same):
        ref[...] = mine_ref[index, :]
    for index, ref in enumerate((gain1, shift1)):
        ref[...] = mine_ref[SHARED + index, :] + other_ref[SHARED + index, :]
    model = gain1.shape[0]

    def both(at):
        mine, other = mine_ref[at : at + 1, :], other_ref[at : at + 1, :]
        return jnp.where(first, mine, other), jnp.where(first, other, mine)

    for index, ref in enumerate((fc2, fc1)):
        for part in range(2):
            for core, value in enumerate(both(SHARED + 2 + 2 * index + part)):
                at = (2 * core + part) * model
                ref[at : at + model] = value[0]
    low, high = both(SHARED + 6)
    middle = model // 2
    q2[:middle] = low[0, :middle]
    q2[middle:] = high[0, :middle]
    fresh = v2.shape[0] // 2
    v2[...] = jnp.concatenate([low[:, middle : middle + fresh], high[:, middle : middle + fresh]], axis=1)[0]
    low, high = both(SHARED + 7)
    for part in range(2):
        span = slice(part * middle, (part + 1) * middle)
        qv1[part : part + 1, :middle] = low[:, span]
        qv1[part : part + 1, middle:] = high[:, span]


def finish_layer(scal_ref, x_ref, mine_ref, other_ref, before_ref, out_ref):
    mid = out_ref.shape[0]
    base = pl.multiple_of(scal_ref[0] * mid, mid)
    own = pl.ds(base, mid)
    total = x_ref[own, :] + (full(mine_ref[...]) + full(other_ref[...])) + row(before_ref)
    place = lax.broadcasted_iota(jnp.int32, (mid, 1), 0)
    out_ref[...] = half(total * (place + base < scal_ref[1]).astype(F32))


FIRST_ORDERS = ((1, 0, 2, 3), (2, 0, 1, 3))
SECOND_ORDERS = ((1, 3, 0, 2), (0, 2, 1, 3))
THIRD_ORDERS = ((1, 3, 2, 0), (1, 2, 0, 3))
FOURTH_ORDERS = ((2, 0, 1, 3), (3, 0, 1, 2))
FIFTH_ORDERS = ((0, 1, 2, 3), (1, 0, 3, 2))


def bit_orders(orders, bits):
    return [[bit for bit in order if bit < bits] + list(range(4, bits)) for order in orders]


def row_table(orders, count):
    bits = count.bit_length() - 1
    table = np.zeros((count, 2, count), np.int32)
    for core, order in enumerate(bit_orders(orders, bits)):
        for me in range(count):
            for block in range(count):
                place = 0
                for bit in order:
                    place = 2 * place + (((block ^ me) >> bit) & 1)
                table[me, core, block] = place
    return table.reshape(count * 2, count)


def fold_pairs(orders, count, phase):
    bits = count.bit_length() - 1
    pairs = []
    for core, order in enumerate(bit_orders(orders, bits)):
        for me in range(count):
            pairs.append((2 * me + core, 2 * (me ^ (1 << order[phase])) + core))
    return pairs


def weight_grads(scalars, orders, count, products, width, after, far):
    operands = [operand for rows, rights in products for operand in (rows, *rights)]
    depth, model = products[0][0].shape
    span = model // count
    bits = count.bit_length() - 1
    lists = bit_orders(orders, bits)

    def kind_of(operand):
        if not any(operand is other for other in far):
            return NEAR
        return (1, 2) if operand.shape[1] > model else LATE

    def body(scal_ref, *refs):
        keep_ref, send_ref, turned = refs[len(refs) - 3 :]
        core, me = scal_ref[0], scal_ref[2]

        def turn(ref):
            columns = ref[...].T
            for index in range(count):
                apart = index ^ me
                places = [
                    sum(((apart >> bit) & 1) << (bits - 1 - at) for at, bit in enumerate(order)) for order in lists
                ]
                place = jnp.where(core == 0, places[0], places[1])
                at = pl.ds(pl.multiple_of(place * span, 16), span)
                turned[at, :] = columns[index * span : (index + 1) * span]

        start, taken = 0, 0
        for _, rights in products:
            turn(refs[taken])
            for ref in refs[taken + 1 : taken + 1 + len(rights)]:
                size = min(ref.shape[1], width - start)
                step = size // len(ref.copies)
                for index in range(len(ref.copies)):
                    columns = slice(index * step, (index + 1) * step)
                    at = slice(start + index * step, start + (index + 1) * step)
                    right = ref.piece(index)[:, columns]
                    send_ref[:, at] = half(dot(turned[model // 2 :, :], right))
                    keep_ref[:, at] = half(dot(turned[: model // 2, :], right))
                start += size
            taken += 1 + len(rights)

    return call(
        body,
        [shaped((model // 2, width))] * 2,
        [SCALARS] + [kind_of(operand) for operand in operands] + [AFTER] * len(after),
        cuts=[NEAR, NEAR],
        scratch=[pltpu.VMEM((model, depth), BF16)],
        cost=width / 3072 * 5,
        vmem=GRAD_BYTES,
    )(scalars, *operands, *after)


def weight_grads_plain(orders, count, products, width):
    model = products[0][0].shape[1]
    parts = [dot_tn(rows, right) for rows, rights in products for right in rights]
    product = half(jnp.concatenate(parts, axis=1)[:, :width])
    if count == 1:
        return product, product
    table = jnp.asarray(row_table(orders, count))
    me = 2 * lax.axis_index("seq") + lax.axis_index("tp")
    table = lax.dynamic_index_in_dim(table, me, 0, keepdims=False)
    back = jnp.zeros((count,), jnp.int32).at[table].set(jnp.arange(count, dtype=jnp.int32))
    placed = jnp.take(product.reshape(count, model // count, width), back, axis=0)
    placed = placed.reshape(model, width)
    return placed[: model // 2], placed[model // 2 :]


GRAD_BYTES = 12 * 1024 * 1024
SMALL_BYTES = 8 * 1024 * 1024


def fold(keep, other, after, extra=()):
    rows, width = keep.shape
    left = rows // 2
    if left % 16:
        total = half(full(keep) + full(other))
        return [total[:left], total[left:]] + ([extra[0] + extra[1]] if extra else [])

    def body(keep_ref, other_ref, *refs):
        if extra:
            refs[-1][...] = refs[0][...] + refs[1][...]
        kept_ref, send_ref = refs[len(extra) : len(extra) + 2]
        send_ref[...] = half(full(keep_ref[left:, :]) + full(other_ref[left:, :]))
        kept_ref[...] = half(full(keep_ref[:left, :]) + full(other_ref[:left, :]))

    outs = [shaped((left, width))] * 2 + [shaped(value.shape, F32) for value in extra[:1]]
    kinds = [NEAR] * (2 + len(extra)) + [AFTER] * len(after)
    return call(body, outs, kinds, cuts=[NEAR] * len(outs), cost=2, vmem=SMALL_BYTES)(keep, other, *extra, *after)


def fold_last(keep, other, cuts, after):
    rows, width = keep.shape
    plan, outs, start = [], [], 0
    for cut in cuts:
        stack, parts = (None, cut) if not isinstance(cut, tuple) else (cut[0], cut[1:])
        parts = (parts,) if stack is None else parts
        plan.append((stack, [(start + sum(parts[:i]), part) for i, part in enumerate(parts)]))
        start += sum(parts)
        shape = (rows, parts[0])
        if stack is not None:
            shape = shape[:stack] + (len(parts),) + shape[stack:]
        outs.append(shaped(shape, F32))

    def body(keep_ref, other_ref, *refs):
        for (stack, spans), ref in zip(plan, refs):
            for index, (low, size) in enumerate(spans):
                span = slice(low, low + size)
                value = full(keep_ref[:, span]) + full(other_ref[:, span])
                if stack is None:
                    ref[...] = value
                elif stack == 0:
                    ref[index] = value
                else:
                    ref[:, index, :] = value

    if rows != 48:
        total = full(keep) + full(other)
        cuts = [[total[:, low : low + size] for low, size in spans] for _, spans in plan]
        return [pieces[0] if stack is None else jnp.stack(pieces, stack) for (stack, _), pieces in zip(plan, cuts)]
    kinds = [NEAR, NEAR] + [AFTER] * len(after)
    return call(body, outs, kinds, cuts=[LATE] * len(outs), cost=2, vmem=SMALL_BYTES)(keep, other, *after)


class Sum:
    def __init__(self, scalars, orders, count, products, width, after=(), far=()):
        self.orders, self.count, self.phase = orders, count, 0
        self.bits = count.bit_length() - 1
        if count > 1 and (products[0][0].shape[1] // count) % 16 == 0:
            self.keep, self.send = weight_grads(scalars, orders, count, products, width, tuple(after), far)
        else:
            self.keep, self.send = weight_grads_plain(orders, count, products, width)
        self.first = self.keep
        if self.bits:
            self.move()
        else:
            self.other = jnp.zeros_like(self.keep)

    def move(self):
        pairs = fold_pairs(self.orders, self.count, self.phase)
        self.other = lax.ppermute(self.send, ("seq", "tp"), pairs)

    def fold(self, *after, beside=None):
        if self.phase + 1 < self.bits:
            self.phase += 1
            extra = beside.terms() if beside is not None else ()
            results = fold(self.keep, self.other, tuple(after), extra)
            self.keep, self.send = results[:2]
            if extra:
                beside.take(results[2])
            self.move()
        return self.keep

    def finish(self, *cuts, after=()):
        while self.phase + 1 < self.bits:
            self.fold()
        return fold_last(self.keep, self.other, cuts, tuple(after))


class Spread:
    def __init__(self, values, count):
        self.values, self.count, self.distance = values, count, 1
        self.move()

    def move(self):
        if self.distance < self.count:
            pairs = [(index, index ^ self.distance) for index in range(self.count)]
            self.other = lax.ppermute(self.values, "seq", pairs)

    def terms(self):
        return (self.values, self.other) if self.distance < self.count else ()

    def take(self, total):
        self.values = total
        self.distance *= 2
        self.move()

    def finish(self):
        while self.distance < self.count:
            self.take(self.values + self.other)
        return self.values


def on_device(count, *arguments):
    (
        tokens, seq_lengths, cotangent, norm1_gain, norm1_shift, qkv1_weight, qv1_bias, out1_weight, out1_bias,
        norm2_gain, norm2_shift, fc1_weight, fc1_bias, proj1_weight, proj1_bias, norm3_gain, norm3_shift,
        qk2_weight, v2_weight, q2_bias, v2_bias, out2_weight, out2_bias, norm4_gain, norm4_shift, fc2_weight,
        fc2_bias, proj2_weight, proj2_bias,
    ) = arguments
    mid, model = tokens.shape
    rows = 2 * mid
    local = qkv1_weight.shape[2]
    fresh = v2_weight.shape[1]
    hidden = fc1_weight.shape[1]
    core = lax.axis_index("tp")
    scalars = jnp.stack([core, seq_lengths[0], lax.axis_index("seq")]).astype(jnp.int32)
    qkv1 = qkv1_weight.transpose(1, 0, 2)
    qk2 = qk2_weight.transpose(1, 0, 2)
    fresh_weight = v2_weight.T

    square, narrow = (rows, model), (rows, local)
    heads = local // HEAD_DIM
    by_head = (0, heads)
    weights_out = shaped((heads, rows, rows))
    bias_scratch = pltpu.VMEM((rows, rows), F32)
    attend_outs = [shaped(square)] + [shaped(narrow)] * 4 + [weights_out, shaped(square)]
    pull_scratch = [pltpu.VMEM(narrow, BF16), pltpu.VMEM((2, rows, rows), BF16)]
    pull_outs = [shaped(square, F32), shaped(square), shaped(narrow), shaped(narrow)]
    sums_outs = [shaped(square), shaped((8, model), F32), shaped((8, local), F32)]
    total_scratch = pltpu.VMEM(square, F32)
    hidden_out, by_column, by_row = shaped((rows, hidden)), (1, HIDDEN_CUT), (0, HIDDEN_CUT)
    feed_sums = [shaped(square), shaped((8, model), F32), shaped((8, hidden), F32)]

    x0, n1, q1, k1, v1, o1, p1, part = call(
        attend_first, [shaped(square)] + attend_outs, [SCALARS, LATE, NEAR] + [LATE] * 5,
        cuts=[NEAR, LATE, LATE, LATE, NEAR, LATE, by_head, NEAR], scratch=[bias_scratch], cost=8,
    )(scalars, tokens, swap(tokens), norm1_gain, norm1_shift, qv1_bias, qkv1, out1_weight)
    x1, m1, z1, pull1, part = call(
        feed_first,
        [shaped(square, F32), shaped(square), hidden_out, hidden_out, shaped(square)],
        [NEAR, NEAR, NEAR] + [LATE] * 4 + [by_column, by_row],
        cuts=[NEAR, LATE, by_column, by_column, NEAR],
        scratch=[total_scratch],
        cost=8,
    )(x0, part, swap(part), out1_bias, norm2_gain, norm2_shift, fc1_bias, fc1_weight, proj1_weight)

    x2, n3, q2, k2, v2, o2, p2, part = call(
        attend_second, [shaped(square, F32)] + attend_outs, [SCALARS, NEAR, NEAR, NEAR] + [LATE] * 5 + [(0, 2), LATE, NEAR, LATE],
        cuts=[NEAR, LATE, NEAR, NEAR, NEAR, LATE, by_head, NEAR], scratch=[bias_scratch], cost=10,
    )(scalars, x1, part, swap(part), proj1_bias, norm3_gain, norm3_shift, q2_bias, v2_bias, qk2, fresh_weight, v1,
      out2_weight)
    x3, m3, gb4, z3, du3, out_part, part, pulled, rep4, loc4 = call(
        feed_second,
        [shaped(square, F32), shaped(square), shaped(square), hidden_out, hidden_out]
        + [shaped((mid, model)), shaped((mid, model))] + feed_sums,
        [SCALARS, NEAR, NEAR, NEAR] + [LATE] * 5 + [NEAR, by_column, by_row],
        cuts=[NEAR] * 10,
        scratch=[total_scratch, total_scratch],
        vmem=BIG_BYTES,
        cost=12,
    )(scalars, x2, part, swap(part), out2_bias, norm4_gain, norm4_shift, fc2_bias, cotangent, swap(cotangent),
      fc2_weight, proj2_weight)
    pulled_other = swap(pulled)
    out_other = swap(part)
    first = Sum(scalars, FIRST_ORDERS, count, [(m3, [du3]), (gb4, [z3])], 2 * hidden)

    g3, gb3, dq2, dk2, dv2, df2, part, rep3, loc3 = call(
        pull_second, pull_outs + [shaped(narrow, F32), shaped(narrow)] + sums_outs,
        [NEAR] * 4 + [LATE, LATE] + [NEAR] * 3 + [by_head] + [LATE] * 2 + [AFTER], cuts=[NEAR] * 9,
        scratch=pull_scratch, cost=14,
    )(gb4, pulled, pulled_other, x3, norm4_gain, out2_weight, q2, k2, v2, p2, qk2, fresh_weight, first.keep)
    part_other = swap(part)
    second = Sum(
        scalars, SECOND_ORDERS, count, [(gb3, [o2]), (n3, [dq2, dk2, df2])], 3 * local + 2 * 128, far=(o2, n3)
    )

    g2, gb2, du1, pulled, rep2, loc2 = call(
        feed_pull,
        [shaped(square, F32), shaped(square), hidden_out] + feed_sums,
        [NEAR, NEAR, NEAR, NEAR, LATE, by_column, by_column, by_row, AFTER],
        cuts=[NEAR] * 6,
        scratch=[total_scratch],
        cost=8,
    )(g3, part, part_other, x2, norm3_gain, pull1, fc1_weight, proj1_weight, second.keep)
    pulled_other = swap(pulled)
    third = Sum(scalars, THIRD_ORDERS, count, [(m1, [du1])], hidden, far=(m1,))
    fourth = Sum(scalars, FOURTH_ORDERS, count, [(gb2, [z1])], hidden, [third.first], far=(z1,))
    first.fold(fourth.first)

    g1, gb1, dq1, dk1, dv1, own_part, part, rep1, loc1 = call(
        functools.partial(pull_first, fresh=fresh),
        pull_outs + [shaped(narrow), shaped((mid, model)), shaped((mid, model))] + sums_outs[1:],
        [SCALARS] + [NEAR] * 4 + [LATE] * 4 + [NEAR, by_head, LATE, NEAR, AFTER],
        cuts=[NEAR] * 9,
        scratch=pull_scratch + [pltpu.VMEM(narrow, F32), pltpu.VMEM(square, BF16)],
        cost=12,
    )(scalars, g2, pulled, pulled_other, x1, norm2_gain, out1_weight, q1, k1, v1, p1, qkv1, dv2, first.keep)
    part_other = swap(part)
    second.fold(g1)
    first.fold(second.keep)
    fifth = Sum(
        scalars, FIFTH_ORDERS, count, [(gb1, [o1]), (n1, [dq1, dk1, dv1])], 4 * local, [first.keep], far=(o1, n1)
    )
    tokens_grad, packed = call(
        pull_tokens, [shaped((mid, model)), shaped((PACKED, model), F32)],
        [SCALARS] + [NEAR] * 4 + [LATE] + [NEAR] * 8 + [AFTER], cuts=[LATE, NEAR], cost=3,
    )(scalars, g1, own_part, part_other, x0, norm1_gain, rep4, rep3, rep2, rep1, loc4, loc3, loc2, loc1, fifth.first)
    packed = Spread(packed, count)

    second.fold(packed.values)
    third.fold(second.keep)
    layer_output = call(finish_layer, shaped((mid, model)), [SCALARS, NEAR, NEAR, NEAR, LATE, AFTER], cost=2)(
        scalars, x3, out_part, out_other, proj2_bias, third.keep
    )
    fourth.fold(layer_output, beside=packed)
    fifth.fold(fourth.keep)
    third.fold(fifth.keep, beside=packed)
    second.fold(third.keep)
    first.fold(second.keep, beside=packed)
    sum_out2, sum_qk2, sum_v2 = second.finish(local, (1, local, local), fresh, after=[first.keep])
    third.fold(sum_out2, beside=packed)
    fourth.fold(third.keep)
    fifth.fold(fourth.keep)
    sum_fc2, sum_proj2 = first.finish(hidden, hidden, after=[fifth.keep])
    (sum_fc1,) = third.finish(hidden, after=[sum_fc2])
    fourth.fold(sum_fc1)
    fifth.fold(fourth.keep)
    (sum_proj1,) = fourth.finish(hidden, after=[fifth.keep])
    sum_out1, sum_qkv1 = fifth.finish(local, (0, local, local, local), after=[sum_proj1])
    sum_qkv1 = sum_qkv1.transpose(1, 0, 2)

    packed = packed.finish()
    vector, small = shaped((model,), F32), shaped((2 * fresh,), F32)
    long_vector = shaped((2 * hidden,), F32)
    (
        sum_gain1, sum_shift1, sum_qv1_bias, sum_out1_bias, sum_gain2, sum_shift2, sum_fc1_bias, sum_proj1_bias,
        sum_gain3, sum_shift3, sum_q2_bias, sum_v2_bias, sum_out2_bias, sum_gain4, sum_shift4, sum_fc2_bias,
        sum_proj2_bias,
    ) = call(
        unpack_sums,
        [vector, vector, shaped((2, model), F32), vector, vector, vector, long_vector, vector,
         vector, vector, vector, small, vector, vector, vector, long_vector, vector],
        [SCALARS, NEAR, NEAR],
        cost=2,
    )(scalars, packed, swap(packed))
    return (
        layer_output, tokens_grad, sum_gain1, sum_shift1, sum_qkv1, sum_qv1_bias, sum_out1.T, sum_out1_bias,
        sum_gain2, sum_shift2, sum_fc1, sum_fc1_bias, sum_proj1.T, sum_proj1_bias, sum_gain3, sum_shift3, sum_qk2,
        sum_v2, sum_q2_bias, sum_v2_bias, sum_out2.T, sum_out2_bias, sum_gain4, sum_shift4, sum_fc2, sum_fc2_bias,
        sum_proj2.T, sum_proj2_bias,
    )


def solution(mesh):
    rows, copied = P(("seq", "tp"), None), P()
    columns, deep = P(None, "tp"), P("tp", None)
    wide, long = P("seq", "tp"), P("tp", "seq")
    count = mesh.shape["seq"]

    def body(*arguments):
        return on_device(count, *arguments)

    return jax.shard_map(
        body,
        mesh=mesh,
        in_specs=(
            rows, P("seq"), rows, copied, copied, P(None, None, "tp"), columns, deep, copied,
            copied, copied, columns, P("tp"), deep, copied, copied, copied,
            P(None, None, "tp"), columns, P("tp"), P("tp"), deep, copied, copied, copied, columns,
            P("tp"), deep, copied,
        ),
        out_specs=(
            rows, rows, copied, copied, P("seq", None, "tp"), copied, long, copied,
            copied, copied, wide, copied, long, copied, copied, copied, P("seq", None, "tp"),
            wide, copied, copied, long, copied, copied, copied, wide, copied,
            long, copied,
        ),
        check_vma=False,
    )
```

```python
import functools

import jax
import jax.numpy as jnp
import numpy as np
from jax import lax
from jax.experimental import pallas as pl
from jax.experimental.pallas import tpu as pltpu
from jax.sharding import PartitionSpec as P

HEAD_DIM = 64
F32 = jnp.float32
BF16 = jnp.bfloat16


def half(values):
    return values.astype(BF16)


def full(values):
    return values.astype(F32)


def dot(left, right):
    return lax.dot_general(left, right, (((1,), (0,)), ((), ())), preferred_element_type=F32)


def dot_nt(left, right):
    return lax.dot_general(left, right, (((1,), (1,)), ((), ())), preferred_element_type=F32)


def dot_tn(left, right):
    return lax.dot_general(left, right, (((0,), (0,)), ((), ())), preferred_element_type=F32)


def swap(values):
    return lax.ppermute(values, "tp", [(0, 1), (1, 0)])


BLOCK = 256
HIDDEN_CUT = 2
VMEM_BYTES, BIG_BYTES = 16 * 1024 * 1024, 16 * 1024 * 1024


class Arriving:
    def __init__(self, source, buffer, sems, first, cut):
        self.source, self.buffer, self.shape, self.dtype = source, buffer, source.shape, source.dtype
        axis, count = cut
        size = source.shape[axis] // count
        self.copies = []
        for index in range(count):
            at = (slice(None),) * axis + (pl.ds(index * size, size),)
            here, there = (source, buffer) if count == 1 else (source.at[at], buffer.at[at])
            self.copies.append(pltpu.make_async_copy(here, there, sems.at[first + index]))
        self.waiting = set(range(count))

    def start(self, index):
        if index < len(self.copies):
            self.copies[index].start()

    def piece(self, index):
        if index in self.waiting:
            self.waiting.remove(index)
            self.copies[index].wait()
        return self.buffer

    def whole(self):
        for index in range(len(self.copies)):
            self.piece(index)
        return self.buffer

    def __getitem__(self, at):
        return self.whole()[at]


class Held:
    def __init__(self, ref):
        self.buffer, self.shape, self.dtype, self.copies = ref, ref.shape, ref.dtype, [None]

    def piece(self, index):
        return self.buffer

    def send(self, index=0):
        pass

    def __getitem__(self, at):
        return self.buffer[at]

    def __setitem__(self, at, value):
        self.buffer[at] = value


class Leaving:
    def __init__(self, target, buffer, sems, first, cut):
        self.target, self.buffer, self.shape, self.dtype = target, buffer, target.shape, target.dtype
        axis, count = cut
        size = target.shape[axis] // count
        self.copies = []
        for index in range(count):
            at = (slice(None),) * axis + (pl.ds(index * size, size),)
            here, there = (buffer, target) if count == 1 else (buffer.at[at], target.at[at])
            self.copies.append(pltpu.make_async_copy(here, there, sems.at[first + index]))
        self.held = set(range(count))

    def send(self, index=0):
        self.held.remove(index)
        self.copies[index].start()

    def finish(self):
        for index in sorted(self.held):
            self.send(index)

    def __getitem__(self, at):
        return self.buffer[at]

    def __setitem__(self, at, value):
        self.buffer[at] = value


SCALARS, AFTER, NEAR, LATE = "scalars", "after", "near", (0, 1)


SPACES = {SCALARS: pltpu.SMEM, NEAR: pltpu.VMEM, AFTER: pl.ANY}


def placed(operand, kind):
    if kind in (SCALARS, AFTER):
        return operand
    return pltpu.with_memory_space_constraint(operand, pltpu.VMEM if kind == NEAR else pltpu.HBM)


TOLD = 0.75


def call(body, outs, ins, cuts=None, scratch=(), cost=1.0, vmem=None):
    single = not isinstance(outs, (list, tuple))
    outs = [outs] if single else list(outs)
    cuts = list(cuts) if cuts is not None else [LATE] * len(outs)
    late = [index for index, kind in enumerate(ins) if isinstance(kind, tuple)]
    in_counts = [ins[index][1] for index in late]
    far = [index for index, kind in enumerate(cuts) if isinstance(kind, tuple)]
    out_counts = [cuts[index][1] for index in far]

    def wrapped(*refs):
        refs = list(refs)
        operands, refs = refs[: len(ins)], refs[len(ins) :]
        targets, refs = refs[: len(outs)], refs[len(outs) :]
        extra, refs = refs[: len(scratch)], refs[len(scratch) :]
        in_buffers, refs = refs[: len(late)], refs[len(late) :]
        out_buffers, sems = refs[: len(far)], refs[len(far) :]
        in_sems, out_sems = sems[0] if late else None, sems[-1] if far else None
        arriving = {
            index: Arriving(operands[index], in_buffers[at], in_sems, sum(in_counts[:at]), ins[index])
            for at, index in enumerate(late)
        }
        for index in range(max(in_counts, default=0)):
            for operand in arriving.values():
                operand.start(index)
        leaving = {
            index: Leaving(targets[index], out_buffers[at], out_sems, sum(out_counts[:at]), cuts[index])
            for at, index in enumerate(far)
        }
        results = [leaving[index] if index in leaving else Held(target) for index, target in enumerate(targets)]
        given = [
            arriving[index] if index in arriving else Held(operands[index]) if kind == NEAR else operands[index]
            for index, kind in enumerate(ins)
            if kind != AFTER
        ]
        body(*given, *results, *extra)
        for operand in arriving.values():
            operand.whole()
        for result in leaving.values():
            result.finish()
        for result in leaving.values():
            for copy in result.copies:
                copy.wait()

    def run(*operands):
        buffers = [pltpu.VMEM(operands[index].shape, operands[index].dtype) for index in late]
        buffers += [pltpu.VMEM(outs[index].shape, outs[index].dtype) for index in far]
        sems = [pltpu.SemaphoreType.DMA((sum(counts),)) for counts in (in_counts, out_counts) if counts]
        results = pl.pallas_call(
            wrapped,
            out_shape=[
                (pltpu.VMEM if kind == NEAR else pltpu.HBM)(out.shape, out.dtype) for out, kind in zip(outs, cuts)
            ],
            in_specs=[pl.BlockSpec(memory_space=SPACES.get(kind, pltpu.HBM)) for kind in ins],
            out_specs=[pl.BlockSpec(memory_space=SPACES.get(kind, pltpu.HBM)) for kind in cuts],
            scratch_shapes=list(scratch) + buffers + sems,
            compiler_params=pltpu.CompilerParams(vmem_limit_bytes=vmem or VMEM_BYTES),
            cost_estimate=pl.CostEstimate(
                flops=int(cost * TOLD * 1.1e9), bytes_accessed=int(cost * TOLD * 3.4e6), transcendentals=0
            ),
        )(*(placed(operand, kind) for operand, kind in zip(operands, ins)))
        return results[0] if single else results

    return run


def shaped(shape, kind=BF16):
    return jax.ShapeDtypeStruct(shape, kind)


def row(ref):
    return full(ref[...][None, :])


def norm_stats(values):
    mean = jnp.mean(values, axis=-1, keepdims=True)
    centered = values - mean
    scale = lax.rsqrt(jnp.mean(centered * centered, axis=-1, keepdims=True) + 1e-05)
    return centered * scale, scale


def norm_backward(grad, values, gain):
    hat, scale = norm_stats(values)
    inner = grad * gain
    mean_inner = jnp.mean(inner, axis=-1, keepdims=True)
    mean_hat = jnp.mean(inner * hat, axis=-1, keepdims=True)
    pulled = scale * (inner - mean_inner - hat * mean_hat)
    return (
        pulled,
        jnp.sum(grad * hat, axis=0, keepdims=True),
        jnp.sum(grad, axis=0, keepdims=True),
    )


def gelu_both(values):
    square = values * values
    rise = 0.5 + 0.5 * jnp.tanh(values * (0.7978845608028654 + 0.035677408136300125 * square))
    value = values * rise
    slope = 1.5957691216057308 + 0.21406444881780076 * square
    return value, rise + value * (1.0 - rise) * slope


def head_lanes(width, which):
    lane = lax.broadcasted_iota(jnp.int32, (1, width), 1)
    return (lane // HEAD_DIM) == which


def keep_lanes(values, lanes):
    return jnp.where(lanes, values, jnp.zeros_like(values))


def fill_bias(bias_ref, length):
    query = lax.broadcasted_iota(jnp.int32, bias_ref.shape, 0)
    key = lax.broadcasted_iota(jnp.int32, bias_ref.shape, 1)
    bias_ref[...] = jnp.where((key <= query) & (key < length), 0.0, -1e30)


def turned_heads(pair):
    turned = full(pair).T
    return [half(turned[which * HEAD_DIM : (which + 1) * HEAD_DIM]) for which in range(2)]


def attend_rows(q_ref, k_ref, v_ref, o_ref, p_ref, bias_ref, length):
    fill_bias(bias_ref, length)
    for pair in range(q_ref.shape[1] // 128):
        lanes = slice(pair * 128, pair * 128 + 128)
        keys, values = k_ref[:, lanes], v_ref[:, lanes]
        total = None
        for which in range(2):
            mask = head_lanes(128, which)
            query = keep_lanes(q_ref[:, lanes] * 0.125, mask).astype(BF16)
            scores = dot_nt(query, keys) + bias_ref[...]
            weights = jnp.exp(scores - jnp.max(scores, axis=-1, keepdims=True))
            weights = weights * (1.0 / jnp.sum(weights, axis=-1, keepdims=True))
            p_ref[2 * pair + which] = half(weights.T)
            p_ref.send(2 * pair + which)
            mixed = dot(half(weights), keep_lanes(values, mask))
            total = mixed if total is None else total + mixed
        o_ref[:, lanes] = half(total)


def attend_first(scal_ref, mine_ref, other_ref, gain_ref, shift_ref, bias_refs, w_ref, out_ref,
                 x_ref, n_ref, q_ref, k_ref, v_ref, o_ref, p_ref, part_ref, bias_ref):
    core, length = scal_ref[0], scal_ref[1]
    mid = mine_ref.shape[0]
    x_ref[pl.ds(pl.multiple_of(core * mid, mid), mid), :] = mine_ref[...]
    x_ref[pl.ds(pl.multiple_of((1 - core) * mid, mid), mid), :] = other_ref[...]
    hat, _ = norm_stats(full(x_ref[...]))
    normed = half(hat * row(gain_ref) + row(shift_ref))
    n_ref[...] = normed
    x_ref.send()
    n_ref.send()
    q_ref[...] = half(dot(normed, w_ref.piece(0)[0]) + full(bias_refs[0:1, :]))
    k_ref[...] = half(dot(normed, w_ref.piece(1)[1]))
    v_ref[...] = half(dot(normed, w_ref.piece(2)[2]) + full(bias_refs[1:2, :]))
    for ref in (q_ref, k_ref, v_ref):
        ref.send()
    attend_rows(q_ref, k_ref, v_ref, o_ref, p_ref, bias_ref, length)
    o_ref.send()
    part_ref[...] = half(dot(o_ref[...], out_ref[...]))


def attend_second(scal_ref, prev_ref, mine_ref, other_ref, before_ref, gain_ref, shift_ref, qb_ref, fb_ref,
                  w_ref, f_ref, v1_ref, out_ref,
                  x_ref, n_ref, q_ref, k_ref, v_ref, o_ref, p_ref, part_ref, bias_ref):
    length = scal_ref[1]
    x_ref[...] = prev_ref[...] + (full(mine_ref[...]) + full(other_ref[...])) + row(before_ref)
    hat, _ = norm_stats(x_ref[...])
    normed = half(hat * row(gain_ref) + row(shift_ref))
    n_ref[...] = normed
    x_ref.send()
    n_ref.send()
    fresh = f_ref.shape[0]
    q_ref[...] = half(dot(normed, w_ref.piece(0)[0]) + row(qb_ref))
    k_ref[...] = half(dot(normed, w_ref.piece(1)[1]))
    v_ref[...] = v1_ref[...]
    v_ref[:, :fresh] = half(dot_nt(normed, f_ref[...]) + row(fb_ref))
    for ref in (q_ref, k_ref, v_ref):
        ref.send()
    attend_rows(q_ref, k_ref, v_ref, o_ref, p_ref, bias_ref, length)
    o_ref.send()
    part_ref[...] = half(dot(o_ref[...], out_ref[...]))


def attend_pull(q_ref, k_ref, v_ref, p_ref, do_ref, dq_ref, dk_ref, dv_ref, ds_ref):
    rows, width = q_ref.shape
    heads = width // HEAD_DIM
    blocks = rows // BLOCK
    ones = jnp.ones((16, rows), BF16)
    for pair in range(heads // 2):
        lanes = slice(pair * 128, pair * 128 + 128)
        keys, values = turned_heads(k_ref[:, lanes]), v_ref[:, lanes]
        pulled_query, queries, grads = {}, {}, {}
        for which in range(2):
            head = 2 * pair + which
            p_ref.piece(head)
            mask = head_lanes(128, which)
            queries[which] = keep_lanes(q_ref[:, lanes] * 0.125, mask).astype(BF16)
            grads[which] = keep_lanes(do_ref[:, lanes], mask)
            for block in range(blocks):
                start, stop = block * BLOCK, (block + 1) * BLOCK
                pulled = dot_nt(values[:stop], grads[which][start:stop])
                weights = full(p_ref.buffer[head, :stop, start:stop])
                total = dot(ones[:, :stop], p_ref.buffer[head, :stop, start:stop])[0:1, :]
                centre = jnp.sum(weights * pulled, axis=0, keepdims=True) * (1.0 / total)
                score_grad = half(weights * (pulled - centre))
                ds_ref[which, :stop, start:stop] = score_grad
                pulled_query[block, which] = dot(keys[which][:, :stop], score_grad)
        for block in range(blocks):
            start, stop = block * BLOCK, (block + 1) * BLOCK
            joined = jnp.concatenate([pulled_query[block, 0], pulled_query[block, 1]], axis=0) * 0.125
            dq_ref[start:stop, lanes] = half(joined.T)
            dk_ref[start:stop, lanes] = half(
                dot(ds_ref[0, start:stop, start:], queries[0][start:])
                + dot(ds_ref[1, start:stop, start:], queries[1][start:])
            )
            dv_ref[start:stop, lanes] = dot(
                p_ref.buffer[2 * pair, start:stop, start:], grads[0][start:]
            ) + dot(p_ref.buffer[2 * pair + 1, start:stop, start:], grads[1][start:])


def column_sum(values):
    return jnp.sum(full(values), axis=0, keepdims=True)


def pull_second(g4_ref, mine_ref, other_ref, x_ref, gain_ref, out_ref, q_ref, k_ref, v_ref, p_ref, w_ref, f_ref,
                g_ref, gb_ref, dq_ref, dk_ref, dv_ref, dvb_ref, part_ref, rep_ref, loc_ref,
                do_ref, ds_ref):
    grad = full(mine_ref[...]) + full(other_ref[...])
    pulled, gain, shift = norm_backward(grad, x_ref[...], row(gain_ref))
    g_ref[...] = full(g4_ref[...]) + pulled
    rep_ref[...] = jnp.zeros_like(rep_ref)
    loc_ref[...] = jnp.zeros_like(loc_ref)
    rep_ref[0:1, :] = gain
    rep_ref[1:2, :] = shift
    rep_ref[2:3, :] = column_sum(g_ref[...])
    gb_ref[...] = half(g_ref[...])
    g_ref.send()
    gb_ref.send()
    do_ref[...] = half(dot_nt(gb_ref[...], out_ref[...]))
    attend_pull(q_ref, k_ref, v_ref, p_ref, do_ref, dq_ref, dk_ref, dv_ref, ds_ref)
    fresh = f_ref.shape[0]
    dvb_ref[...] = half(dv_ref[...])
    fresh_grad = dvb_ref[:, :fresh]
    part_ref[...] = half(
        dot_nt(dq_ref[...], w_ref[0]) + dot_nt(dk_ref[...], w_ref[1]) + dot(fresh_grad, f_ref[...])
    )
    loc_ref[0:1, :] = column_sum(dq_ref[...])
    loc_ref[1:2, :] = column_sum(dvb_ref[...])


def pull_first(scal_ref, g2_ref, mine_ref, other_ref, x_ref, gain_ref, out_ref, q_ref, k_ref, v_ref, p_ref, w_ref, reused_ref,
               g_ref, gb_ref, dq_ref, dk_ref, dv_ref, own_ref, part_ref, rep_ref, loc_ref,
               do_ref, ds_ref, dv_full, partial, *, fresh):
    grad = full(mine_ref[...]) + full(other_ref[...])
    pulled, gain, shift = norm_backward(grad, x_ref[...], row(gain_ref))
    g_ref[...] = g2_ref[...] + pulled
    rep_ref[...] = jnp.zeros_like(rep_ref)
    loc_ref[...] = jnp.zeros_like(loc_ref)
    rep_ref[0:1, :] = gain
    rep_ref[1:2, :] = shift
    rep_ref[2:3, :] = column_sum(g_ref[...])
    gb_ref[...] = half(g_ref[...])
    g_ref.send()
    gb_ref.send()
    do_ref[...] = half(dot_nt(gb_ref[...], out_ref[...]))
    attend_pull(q_ref, k_ref, v_ref, p_ref, do_ref, dq_ref, dk_ref, dv_full, ds_ref)
    column = lax.broadcasted_iota(jnp.int32, (1, dv_full.shape[1]), 1)
    dv_ref[...] = half(dv_full[...] + jnp.where(column >= fresh, reused_ref[...], 0.0))
    partial[...] = half(
        dot_nt(dq_ref[...], w_ref[0]) + dot_nt(dk_ref[...], w_ref[1]) + dot_nt(dv_ref[...], w_ref[2])
    )
    core, mid = scal_ref[0], own_ref.shape[0]
    own_ref[...] = partial[pl.ds(pl.multiple_of(core * mid, mid), mid), :]
    part_ref[...] = partial[pl.ds(pl.multiple_of((1 - core) * mid, mid), mid), :]
    loc_ref[0:1, :] = column_sum(dq_ref[...])
    loc_ref[1:2, :] = column_sum(dv_ref[...])


ROW_BLOCK = 256


def hidden_spans(ref):
    size = ref.shape[1] // HIDDEN_CUT
    return [slice(index * size, (index + 1) * size) for index in range(HIDDEN_CUT)]


def add_to(total, span, value, fresh):
    total[span, :] = value if fresh else total[span, :] + value


def feed_first(prev_ref, mine_ref, other_ref, before_ref, gain_ref, shift_ref, bias_ref, fc_ref, proj_ref,
               x_ref, m_ref, z_ref, pull_ref, part_ref, total):
    x_ref[...] = full(prev_ref[...]) + (full(mine_ref[...]) + full(other_ref[...])) + row(before_ref)
    x_ref.send()
    hat, _ = norm_stats(x_ref[...])
    m_ref[...] = half(hat * row(gain_ref) + row(shift_ref))
    m_ref.send()
    for index, columns in enumerate(hidden_spans(fc_ref)):
        fc, proj = fc_ref.piece(index), proj_ref.piece(index)
        bias = full(bias_ref[columns][None, :])
        for low in range(0, m_ref.shape[0], ROW_BLOCK):
            span = slice(low, low + ROW_BLOCK)
            value, pull = gelu_both(dot(m_ref[span, :], fc[:, columns]) + bias)
            value = half(value)
            z_ref[span, columns] = value
            pull_ref[span, columns] = half(pull)
            add_to(total, span, dot(value, proj[columns, :]), index == 0)
        z_ref.send(index)
        pull_ref.send(index)
    part_ref[...] = half(total[...])


def feed_second(scal_ref, prev_ref, mine_ref, other_ref, before_ref, gain_ref, shift_ref, bias_ref,
                cot_ref, cot_other_ref, fc_ref, proj_ref,
                x_ref, m_ref, g_ref, z_ref, du_ref, own_ref, part_ref, pulled_ref, rep_ref, loc_ref, total, pulled_total):
    core, length = scal_ref[0], scal_ref[1]
    x_ref[...] = prev_ref[...] + (full(mine_ref[...]) + full(other_ref[...])) + row(before_ref)
    x_ref.send()
    hat, _ = norm_stats(x_ref[...])
    m_ref[...] = half(hat * row(gain_ref) + row(shift_ref))
    m_ref.send()
    mid = cot_ref.shape[0]
    place = lax.broadcasted_iota(jnp.int32, (mid, 1), 0)
    for source, owner in ((cot_ref, core), (cot_other_ref, 1 - core)):
        base = pl.multiple_of(owner * mid, mid)
        alive = (place + base < length).astype(F32)
        g_ref[pl.ds(base, mid), :] = half(full(source[...]) * alive)
    g_ref.send()
    rep_ref[...] = jnp.zeros_like(rep_ref)
    loc_ref[...] = jnp.zeros_like(loc_ref)
    rep_ref[0:1, :] = column_sum(g_ref[...])
    for index, columns in enumerate(hidden_spans(fc_ref)):
        fc, proj = fc_ref.piece(index), proj_ref.piece(index)
        bias = full(bias_ref[columns][None, :])
        sums = None
        for low in range(0, m_ref.shape[0], ROW_BLOCK):
            span = slice(low, low + ROW_BLOCK)
            value, pull = gelu_both(dot(m_ref[span, :], fc[:, columns]) + bias)
            value = half(value)
            z_ref[span, columns] = value
            add_to(total, span, dot(value, proj[columns, :]), index == 0)
            du = half(dot_nt(g_ref[span, :], proj[columns, :]) * pull)
            du_ref[span, columns] = du
            add_to(pulled_total, span, dot_nt(du, fc[:, columns]), index == 0)
            sums = column_sum(du) if sums is None else sums + column_sum(du)
        loc_ref[0:1, columns] = sums
        z_ref.send(index)
        du_ref.send(index)
    own_ref[...] = half(total[pl.ds(pl.multiple_of(core * mid, mid), mid), :])
    part_ref[...] = half(total[pl.ds(pl.multiple_of((1 - core) * mid, mid), mid), :])
    pulled_ref[...] = half(pulled_total[...])


def feed_pull(g3_ref, mine_ref, other_ref, xin_ref, gain_ref, pull_ref, fc_ref, proj_ref,
              g_ref, gb_ref, du_ref, pulled_ref, rep_ref, loc_ref, pulled_total):
    grad = full(mine_ref[...]) + full(other_ref[...])
    pulled, gain, shift = norm_backward(grad, xin_ref[...], row(gain_ref))
    g_ref[...] = g3_ref[...] + pulled
    g_ref.send()
    rep_ref[...] = jnp.zeros_like(rep_ref)
    loc_ref[...] = jnp.zeros_like(loc_ref)
    rep_ref[0:1, :] = gain
    rep_ref[1:2, :] = shift
    rep_ref[2:3, :] = column_sum(g_ref[...])
    gb_ref[...] = half(g_ref[...])
    gb_ref.send()
    for index, columns in enumerate(hidden_spans(fc_ref)):
        fc, proj = fc_ref.piece(index), proj_ref.piece(index)
        pull = pull_ref.piece(index)
        sums = None
        for low in range(0, gb_ref.shape[0], ROW_BLOCK):
            span = slice(low, low + ROW_BLOCK)
            du = half(dot_nt(gb_ref[span, :], proj[columns, :]) * full(pull[span, columns]))
            du_ref[span, columns] = du
            add_to(pulled_total, span, dot_nt(du, fc[:, columns]), index == 0)
            sums = column_sum(du) if sums is None else sums + column_sum(du)
        loc_ref[0:1, columns] = sums
        du_ref.send(index)
    pulled_ref[...] = half(pulled_total[...])


PACKED, SHARED = 24, 10


def pull_tokens(scal_ref, g1_ref, mine_ref, other_ref, x_ref, gain_ref,
                rep4_ref, rep3_ref, rep2_ref, rep1_ref, loc4_ref, loc3_ref, loc2_ref, loc1_ref,
                out_ref, pack_ref):
    mid, model = out_ref.shape
    own = pl.ds(pl.multiple_of(scal_ref[0] * mid, mid), mid)
    grad = full(mine_ref[...]) + full(other_ref[...])
    pulled, gain, shift = norm_backward(grad, full(x_ref[own, :]), row(gain_ref))
    out_ref[...] = half(g1_ref[own, :] + pulled)
    pack_ref[...] = jnp.zeros_like(pack_ref)
    pack_ref[0:1, :] = rep4_ref[0:1, :]
    for index, ref in enumerate((rep3_ref, rep2_ref, rep1_ref)):
        pack_ref[1 + 3 * index : 4 + 3 * index, :] = ref[0:3, :]
    pack_ref[SHARED : SHARED + 1, :] = gain
    pack_ref[SHARED + 1 : SHARED + 2, :] = shift
    for index, ref in enumerate((loc4_ref, loc2_ref)):
        for part in range(2):
            at = SHARED + 2 + 2 * index + part
            pack_ref[at : at + 1, :] = ref[0:1, part * model : (part + 1) * model]
    for index, ref in enumerate((loc3_ref, loc1_ref)):
        at = SHARED + 6 + index
        for part in range(2):
            pack_ref[at : at + 1, part * model // 2 : (part + 1) * model // 2] = ref[part : part + 1, :]


def unpack_sums(scal_ref, mine_ref, other_ref, *outs):
    first = scal_ref[0] == 0
    (gain1, shift1, qv1, out1, gain2, shift2, fc1, proj1,
     gain3, shift3, q2, v2, out2, gain4, shift4, fc2, proj2) = outs
    same = (proj2, gain4, shift4, out2, gain3, shift3, proj1, gain2, shift2, out1)
    for index, ref in enumerate(same):
        ref[...] = mine_ref[index, :]
    for index, ref in enumerate((gain1, shift1)):
        ref[...] = mine_ref[SHARED + index, :] + other_ref[SHARED + index, :]
    model = gain1.shape[0]

    def both(at):
        mine, other = mine_ref[at : at + 1, :], other_ref[at : at + 1, :]
        return jnp.where(first, mine, other), jnp.where(first, other, mine)

    for index, ref in enumerate((fc2, fc1)):
        for part in range(2):
            for core, value in enumerate(both(SHARED + 2 + 2 * index + part)):
                at = (2 * core + part) * model
                ref[at : at + model] = value[0]
    low, high = both(SHARED + 6)
    middle = model // 2
    q2[:middle] = low[0, :middle]
    q2[middle:] = high[0, :middle]
    fresh = v2.shape[0] // 2
    v2[...] = jnp.concatenate([low[:, middle : middle + fresh], high[:, middle : middle + fresh]], axis=1)[0]
    low, high = both(SHARED + 7)
    for part in range(2):
        span = slice(part * middle, (part + 1) * middle)
        qv1[part : part + 1, :middle] = low[:, span]
        qv1[part : part + 1, middle:] = high[:, span]


def finish_layer(scal_ref, x_ref, mine_ref, other_ref, before_ref, out_ref, ended_ref):
    ended_ref[...] = jnp.zeros(ended_ref.shape, F32)
    mid = out_ref.shape[0]
    base = pl.multiple_of(scal_ref[0] * mid, mid)
    own = pl.ds(base, mid)
    total = x_ref[own, :] + (full(mine_ref[...]) + full(other_ref[...])) + row(before_ref)
    place = lax.broadcasted_iota(jnp.int32, (mid, 1), 0)
    out_ref[...] = half(total * (place + base < scal_ref[1]).astype(F32))


FIRST_ORDERS = ((1, 0, 2, 3), (2, 0, 1, 3))
SECOND_ORDERS = ((1, 3, 0, 2), (0, 2, 1, 3))
THIRD_ORDERS = ((1, 3, 2, 0), (1, 2, 0, 3))
FOURTH_ORDERS = ((2, 0, 1, 3), (3, 0, 1, 2))
FIFTH_ORDERS = ((0, 1, 2, 3), (1, 0, 3, 2))


def bit_orders(orders, bits):
    return [[bit for bit in order if bit < bits] + list(range(4, bits)) for order in orders]


def row_table(orders, count):
    bits = count.bit_length() - 1
    table = np.zeros((count, 2, count), np.int32)
    for core, order in enumerate(bit_orders(orders, bits)):
        for me in range(count):
            for block in range(count):
                place = 0
                for bit in order:
                    place = 2 * place + (((block ^ me) >> bit) & 1)
                table[me, core, block] = place
    return table.reshape(count * 2, count)


def fold_pairs(orders, count, phase):
    bits = count.bit_length() - 1
    pairs = []
    for core, order in enumerate(bit_orders(orders, bits)):
        for me in range(count):
            pairs.append((2 * me + core, 2 * (me ^ (1 << order[phase])) + core))
    return pairs


def weight_grads(scalars, orders, count, products, width, after, far):
    operands = [operand for rows, rights in products for operand in (rows, *rights)]
    depth, model = products[0][0].shape
    span = model // count
    bits = count.bit_length() - 1
    lists = bit_orders(orders, bits)

    def kind_of(operand):
        if not any(operand is other for other in far):
            return NEAR
        return (1, 2) if operand.shape[1] > model else LATE

    def body(scal_ref, *refs):
        keep_ref, send_ref, turned = refs[len(refs) - 3 :]
        core, me = scal_ref[0], scal_ref[2]

        def turn(ref):
            columns = ref[...].T
            for index in range(count):
                apart = index ^ me
                places = [
                    sum(((apart >> bit) & 1) << (bits - 1 - at) for at, bit in enumerate(order)) for order in lists
                ]
                place = jnp.where(core == 0, places[0], places[1])
                at = pl.ds(pl.multiple_of(place * span, 16), span)
                turned[at, :] = columns[index * span : (index + 1) * span]

        start, taken = 0, 0
        for _, rights in products:
            turn(refs[taken])
            for ref in refs[taken + 1 : taken + 1 + len(rights)]:
                size = min(ref.shape[1], width - start)
                step = size // len(ref.copies)
                for index in range(len(ref.copies)):
                    columns = slice(index * step, (index + 1) * step)
                    at = slice(start + index * step, start + (index + 1) * step)
                    right = ref.piece(index)[:, columns]
                    send_ref[:, at] = half(dot(turned[model // 2 :, :], right))
                    keep_ref[:, at] = half(dot(turned[: model // 2, :], right))
                start += size
            taken += 1 + len(rights)

    return call(
        body,
        [shaped((model // 2, width))] * 2,
        [SCALARS] + [kind_of(operand) for operand in operands] + [AFTER] * len(after),
        cuts=[NEAR, NEAR],
        scratch=[pltpu.VMEM((model, depth), BF16)],
        cost=width / 3072 * 5,
        vmem=GRAD_BYTES,
    )(scalars, *operands, *after)


def weight_grads_plain(orders, count, products, width):
    model = products[0][0].shape[1]
    parts = [dot_tn(rows, right) for rows, rights in products for right in rights]
    product = half(jnp.concatenate(parts, axis=1)[:, :width])
    if count == 1:
        return product, product
    table = jnp.asarray(row_table(orders, count))
    me = 2 * lax.axis_index("seq") + lax.axis_index("tp")
    table = lax.dynamic_index_in_dim(table, me, 0, keepdims=False)
    back = jnp.zeros((count,), jnp.int32).at[table].set(jnp.arange(count, dtype=jnp.int32))
    placed = jnp.take(product.reshape(count, model // count, width), back, axis=0)
    placed = placed.reshape(model, width)
    return placed[: model // 2], placed[model // 2 :]


GRAD_BYTES = 12 * 1024 * 1024
SMALL_BYTES = 8 * 1024 * 1024


def fold(keep, other, after, extra=()):
    rows, width = keep.shape
    left = rows // 2
    if left % 16:
        total = half(full(keep) + full(other))
        return [total[:left], total[left:]] + ([extra[0] + extra[1]] if extra else [])

    def body(keep_ref, other_ref, *refs):
        if extra:
            refs[-1][...] = refs[0][...] + refs[1][...]
        kept_ref, send_ref = refs[len(extra) : len(extra) + 2]
        send_ref[...] = half(full(keep_ref[left:, :]) + full(other_ref[left:, :]))
        kept_ref[...] = half(full(keep_ref[:left, :]) + full(other_ref[:left, :]))

    outs = [shaped((left, width))] * 2 + [shaped(value.shape, F32) for value in extra[:1]]
    kinds = [NEAR] * (2 + len(extra)) + [AFTER] * len(after)
    return call(body, outs, kinds, cuts=[NEAR] * len(outs), cost=2, vmem=SMALL_BYTES)(keep, other, *extra, *after)


def fold_last(keep, other, cuts, after):
    rows, width = keep.shape
    plan, outs, start = [], [], 0
    for cut in cuts:
        stack, parts = (None, cut) if not isinstance(cut, tuple) else (cut[0], cut[1:])
        parts = (parts,) if stack is None else parts
        plan.append((stack, [(start + sum(parts[:i]), part) for i, part in enumerate(parts)]))
        start += sum(parts)
        shape = (rows, parts[0])
        if stack is not None:
            shape = shape[:stack] + (len(parts),) + shape[stack:]
        outs.append(shaped(shape, F32))

    def body(keep_ref, other_ref, *refs):
        refs[-1][...] = jnp.zeros(refs[-1].shape, F32)
        for (stack, spans), ref in zip(plan, refs):
            for index, (low, size) in enumerate(spans):
                span = slice(low, low + size)
                value = full(keep_ref[:, span]) + full(other_ref[:, span])
                if stack is None:
                    ref[...] = value
                elif stack == 0:
                    ref[index] = value
                else:
                    ref[:, index, :] = value

    if rows != 48:
        total = full(keep) + full(other)
        cuts = [[total[:, low : low + size] for low, size in spans] for _, spans in plan]
        results = [pieces[0] if stack is None else jnp.stack(pieces, stack) for (stack, _), pieces in zip(plan, cuts)]
        return results + [keep]
    kinds = [NEAR, NEAR] + [AFTER] * len(after)
    places = [LATE] * len(outs) + [NEAR]
    outs.append(shaped((8, 128), F32))
    return call(body, outs, kinds, cuts=places, cost=2, vmem=SMALL_BYTES)(keep, other, *after)


class Sum:
    def __init__(self, scalars, orders, count, products, width, after=(), far=()):
        self.orders, self.count, self.phase = orders, count, 0
        self.bits = count.bit_length() - 1
        if count > 1 and (products[0][0].shape[1] // count) % 16 == 0:
            self.keep, self.send = weight_grads(scalars, orders, count, products, width, tuple(after), far)
        else:
            self.keep, self.send = weight_grads_plain(orders, count, products, width)
        self.first = self.keep
        if self.bits:
            self.move()
        else:
            self.other = jnp.zeros_like(self.keep)

    def move(self):
        pairs = fold_pairs(self.orders, self.count, self.phase)
        self.other = lax.ppermute(self.send, ("seq", "tp"), pairs)

    def fold(self, *after, beside=None):
        if self.phase + 1 < self.bits:
            self.phase += 1
            extra = beside.terms() if beside is not None else ()
            results = fold(self.keep, self.other, tuple(after), extra)
            self.keep, self.send = results[:2]
            if extra:
                beside.take(results[2])
            self.move()
        return self.keep

    def finish(self, *cuts, after=()):
        while self.phase + 1 < self.bits:
            self.fold()
        return fold_last(self.keep, self.other, cuts, tuple(after))


class Spread:
    def __init__(self, values, count):
        self.values, self.count, self.distance = values, count, 1
        self.move()

    def move(self):
        if self.distance < self.count:
            pairs = [(index, index ^ self.distance) for index in range(self.count)]
            self.other = lax.ppermute(self.values, "seq", pairs)

    def terms(self):
        return (self.values, self.other) if self.distance < self.count else ()

    def take(self, total):
        self.values = total
        self.distance *= 2
        self.move()

    def finish(self):
        while self.distance < self.count:
            self.take(self.values + self.other)
        return self.values


def on_device(count, *arguments):
    (
        tokens, seq_lengths, cotangent, norm1_gain, norm1_shift, qkv1_weight, qv1_bias, out1_weight, out1_bias,
        norm2_gain, norm2_shift, fc1_weight, fc1_bias, proj1_weight, proj1_bias, norm3_gain, norm3_shift,
        qk2_weight, v2_weight, q2_bias, v2_bias, out2_weight, out2_bias, norm4_gain, norm4_shift, fc2_weight,
        fc2_bias, proj2_weight, proj2_bias,
    ) = arguments
    mid, model = tokens.shape
    rows = 2 * mid
    local = qkv1_weight.shape[2]
    fresh = v2_weight.shape[1]
    hidden = fc1_weight.shape[1]
    core = lax.axis_index("tp")
    scalars = jnp.stack([core, seq_lengths[0], lax.axis_index("seq")]).astype(jnp.int32)
    qkv1 = qkv1_weight.transpose(1, 0, 2)
    qk2 = qk2_weight.transpose(1, 0, 2)
    fresh_weight = v2_weight.T

    square, narrow = (rows, model), (rows, local)
    heads = local // HEAD_DIM
    by_head = (0, heads)
    weights_out = shaped((heads, rows, rows))
    bias_scratch = pltpu.VMEM((rows, rows), F32)
    attend_outs = [shaped(square)] + [shaped(narrow)] * 4 + [weights_out, shaped(square)]
    pull_scratch = [pltpu.VMEM(narrow, BF16), pltpu.VMEM((2, rows, rows), BF16)]
    pull_outs = [shaped(square, F32), shaped(square), shaped(narrow), shaped(narrow)]
    sums_outs = [shaped(square), shaped((8, model), F32), shaped((8, local), F32)]
    total_scratch = pltpu.VMEM(square, F32)
    hidden_out, by_column, by_row = shaped((rows, hidden)), (1, HIDDEN_CUT), (0, HIDDEN_CUT)
    feed_sums = [shaped(square), shaped((8, model), F32), shaped((8, hidden), F32)]

    x0, n1, q1, k1, v1, o1, p1, part = call(
        attend_first, [shaped(square)] + attend_outs, [SCALARS, LATE, NEAR] + [LATE] * 5,
        cuts=[NEAR, LATE, LATE, LATE, NEAR, LATE, by_head, NEAR], scratch=[bias_scratch], cost=8,
    )(scalars, tokens, swap(tokens), norm1_gain, norm1_shift, qv1_bias, qkv1, out1_weight)
    x1, m1, z1, pull1, part = call(
        feed_first,
        [shaped(square, F32), shaped(square), hidden_out, hidden_out, shaped(square)],
        [NEAR, NEAR, NEAR] + [LATE] * 4 + [by_column, by_row],
        cuts=[NEAR, LATE, by_column, by_column, NEAR],
        scratch=[total_scratch],
        cost=8,
    )(x0, part, swap(part), out1_bias, norm2_gain, norm2_shift, fc1_bias, fc1_weight, proj1_weight)

    x2, n3, q2, k2, v2, o2, p2, part = call(
        attend_second, [shaped(square, F32)] + attend_outs, [SCALARS, NEAR, NEAR, NEAR] + [LATE] * 5 + [(0, 2), LATE, NEAR, LATE],
        cuts=[NEAR, LATE, NEAR, NEAR, NEAR, LATE, by_head, NEAR], scratch=[bias_scratch], cost=10,
    )(scalars, x1, part, swap(part), proj1_bias, norm3_gain, norm3_shift, q2_bias, v2_bias, qk2, fresh_weight, v1,
      out2_weight)
    x3, m3, gb4, z3, du3, out_part, part, pulled, rep4, loc4 = call(
        feed_second,
        [shaped(square, F32), shaped(square), shaped(square), hidden_out, hidden_out]
        + [shaped((mid, model)), shaped((mid, model))] + feed_sums,
        [SCALARS, NEAR, NEAR, NEAR] + [LATE] * 5 + [NEAR, by_column, by_row],
        cuts=[NEAR] * 10,
        scratch=[total_scratch, total_scratch],
        vmem=BIG_BYTES,
        cost=12,
    )(scalars, x2, part, swap(part), out2_bias, norm4_gain, norm4_shift, fc2_bias, cotangent, swap(cotangent),
      fc2_weight, proj2_weight)
    pulled_other = swap(pulled)
    out_other = swap(part)
    first = Sum(scalars, FIRST_ORDERS, count, [(m3, [du3]), (gb4, [z3])], 2 * hidden)

    g3, gb3, dq2, dk2, dv2, df2, part, rep3, loc3 = call(
        pull_second, pull_outs + [shaped(narrow, F32), shaped(narrow)] + sums_outs,
        [NEAR] * 4 + [LATE, LATE] + [NEAR] * 3 + [by_head] + [LATE] * 2 + [AFTER], cuts=[NEAR] * 9,
        scratch=pull_scratch, cost=14,
    )(gb4, pulled, pulled_other, x3, norm4_gain, out2_weight, q2, k2, v2, p2, qk2, fresh_weight, first.keep)
    part_other = swap(part)
    second = Sum(
        scalars, SECOND_ORDERS, count, [(gb3, [o2]), (n3, [dq2, dk2, df2])], 3 * local + 2 * 128, far=(o2, n3)
    )

    g2, gb2, du1, pulled, rep2, loc2 = call(
        feed_pull,
        [shaped(square, F32), shaped(square), hidden_out] + feed_sums,
        [NEAR, NEAR, NEAR, NEAR, LATE, by_column, by_column, by_row, AFTER],
        cuts=[NEAR] * 6,
        scratch=[total_scratch],
        cost=8,
    )(g3, part, part_other, x2, norm3_gain, pull1, fc1_weight, proj1_weight, second.keep)
    pulled_other = swap(pulled)
    third = Sum(scalars, THIRD_ORDERS, count, [(m1, [du1])], hidden, far=(m1,))
    fourth = Sum(scalars, FOURTH_ORDERS, count, [(gb2, [z1])], hidden, [third.first], far=(z1,))
    first.fold(fourth.first)

    g1, gb1, dq1, dk1, dv1, own_part, part, rep1, loc1 = call(
        functools.partial(pull_first, fresh=fresh),
        pull_outs + [shaped(narrow), shaped((mid, model)), shaped((mid, model))] + sums_outs[1:],
        [SCALARS] + [NEAR] * 4 + [LATE] * 4 + [NEAR, by_head, LATE, NEAR, AFTER],
        cuts=[NEAR] * 9,
        scratch=pull_scratch + [pltpu.VMEM(narrow, F32), pltpu.VMEM(square, BF16)],
        cost=12,
    )(scalars, g2, pulled, pulled_other, x1, norm2_gain, out1_weight, q1, k1, v1, p1, qkv1, dv2, first.keep)
    part_other = swap(part)
    second.fold(g1)
    first.fold(second.keep)
    fifth = Sum(
        scalars, FIFTH_ORDERS, count, [(gb1, [o1]), (n1, [dq1, dk1, dv1])], 4 * local, [first.keep], far=(o1, n1)
    )
    tokens_grad, packed = call(
        pull_tokens, [shaped((mid, model)), shaped((PACKED, model), F32)],
        [SCALARS] + [NEAR] * 4 + [LATE] + [NEAR] * 8 + [AFTER], cuts=[LATE, NEAR], cost=3,
    )(scalars, g1, own_part, part_other, x0, norm1_gain, rep4, rep3, rep2, rep1, loc4, loc3, loc2, loc1, fifth.first)
    packed = Spread(packed, count)

    second.fold(packed.values)
    third.fold(second.keep)
    layer_output, ended = call(
        finish_layer, [shaped((mid, model)), shaped((8, 128), F32)], [SCALARS, NEAR, NEAR, NEAR, LATE, AFTER],
        cuts=[LATE, NEAR], cost=2,
    )(
        scalars, x3, out_part, out_other, proj2_bias, third.keep
    )
    fourth.fold(ended, beside=packed)
    fifth.fold(fourth.keep)
    third.fold(fifth.keep, beside=packed)
    second.fold(third.keep)
    first.fold(second.keep, beside=packed)
    sum_out2, sum_qk2, sum_v2, ended = second.finish(local, (1, local, local), fresh, after=[first.keep])
    third.fold(ended, beside=packed)
    fourth.fold(third.keep)
    fifth.fold(fourth.keep)
    sum_fc2, sum_proj2, ended = first.finish(hidden, hidden, after=[fifth.keep])
    sum_fc1, ended = third.finish(hidden, after=[ended])
    fourth.fold(ended)
    fifth.fold(fourth.keep)
    sum_proj1, ended = fourth.finish(hidden, after=[fifth.keep])
    sum_out1, sum_qkv1, _ = fifth.finish(local, (0, local, local, local), after=[ended])
    sum_qkv1 = sum_qkv1.transpose(1, 0, 2)

    packed = packed.finish()
    vector, small = shaped((model,), F32), shaped((2 * fresh,), F32)
    long_vector = shaped((2 * hidden,), F32)
    (
        sum_gain1, sum_shift1, sum_qv1_bias, sum_out1_bias, sum_gain2, sum_shift2, sum_fc1_bias, sum_proj1_bias,
        sum_gain3, sum_shift3, sum_q2_bias, sum_v2_bias, sum_out2_bias, sum_gain4, sum_shift4, sum_fc2_bias,
        sum_proj2_bias,
    ) = call(
        unpack_sums,
        [vector, vector, shaped((2, model), F32), vector, vector, vector, long_vector, vector,
         vector, vector, vector, small, vector, vector, vector, long_vector, vector],
        [SCALARS, NEAR, NEAR],
        cost=2,
    )(scalars, packed, swap(packed))
    return (
        layer_output, tokens_grad, sum_gain1, sum_shift1, sum_qkv1, sum_qv1_bias, sum_out1.T, sum_out1_bias,
        sum_gain2, sum_shift2, sum_fc1, sum_fc1_bias, sum_proj1.T, sum_proj1_bias, sum_gain3, sum_shift3, sum_qk2,
        sum_v2, sum_q2_bias, sum_v2_bias, sum_out2.T, sum_out2_bias, sum_gain4, sum_shift4, sum_fc2, sum_fc2_bias,
        sum_proj2.T, sum_proj2_bias,
    )


def solution(mesh):
    rows, copied = P(("seq", "tp"), None), P()
    columns, deep = P(None, "tp"), P("tp", None)
    wide, long = P("seq", "tp"), P("tp", "seq")
    count = mesh.shape["seq"]

    def body(*arguments):
        return on_device(count, *arguments)

    return jax.shard_map(
        body,
        mesh=mesh,
        in_specs=(
            rows, P("seq"), rows, copied, copied, P(None, None, "tp"), columns, deep, copied,
            copied, copied, columns, P("tp"), deep, copied, copied, copied,
            P(None, None, "tp"), columns, P("tp"), P("tp"), deep, copied, copied, copied, columns,
            P("tp"), deep, copied,
        ),
        out_specs=(
            rows, rows, copied, copied, P("seq", None, "tp"), copied, long, copied,
            copied, copied, wide, copied, long, copied, copied, copied, P("seq", None, "tp"),
            wide, copied, copied, long, copied, copied, copied, wide, copied,
            long, copied,
        ),
        check_vma=False,
    )
```

```python
import functools

import jax
import jax.numpy as jnp
import numpy as np
from jax import lax
from jax.experimental import pallas as pl
from jax.experimental.pallas import tpu as pltpu
from jax.sharding import PartitionSpec as P

HEAD_DIM = 64
F32 = jnp.float32
BF16 = jnp.bfloat16


def half(values):
    return values.astype(BF16)


def full(values):
    return values.astype(F32)


def dot(left, right):
    return lax.dot_general(left, right, (((1,), (0,)), ((), ())), preferred_element_type=F32)


def dot_nt(left, right):
    return lax.dot_general(left, right, (((1,), (1,)), ((), ())), preferred_element_type=F32)


def dot_tn(left, right):
    return lax.dot_general(left, right, (((0,), (0,)), ((), ())), preferred_element_type=F32)


def swap(values):
    return lax.ppermute(values, "tp", [(0, 1), (1, 0)])


BLOCK = 256
HIDDEN_CUT = 2
VMEM_BYTES, BIG_BYTES = 16 * 1024 * 1024, 16 * 1024 * 1024


class Arriving:
    def __init__(self, source, buffer, sems, first, cut):
        self.source, self.buffer, self.shape, self.dtype = source, buffer, source.shape, source.dtype
        axis, count = cut
        size = source.shape[axis] // count
        self.copies = []
        for index in range(count):
            at = (slice(None),) * axis + (pl.ds(index * size, size),)
            here, there = (source, buffer) if count == 1 else (source.at[at], buffer.at[at])
            self.copies.append(pltpu.make_async_copy(here, there, sems.at[first + index]))
        self.waiting = set(range(count))

    def start(self, index):
        if index < len(self.copies):
            self.copies[index].start()

    def piece(self, index):
        if index in self.waiting:
            self.waiting.remove(index)
            self.copies[index].wait()
        return self.buffer

    def whole(self):
        for index in range(len(self.copies)):
            self.piece(index)
        return self.buffer

    def __getitem__(self, at):
        return self.whole()[at]


class Held:
    def __init__(self, ref):
        self.buffer, self.shape, self.dtype, self.copies = ref, ref.shape, ref.dtype, [None]

    def piece(self, index):
        return self.buffer

    def send(self, index=0):
        pass

    def __getitem__(self, at):
        return self.buffer[at]

    def __setitem__(self, at, value):
        self.buffer[at] = value


class Leaving:
    def __init__(self, target, buffer, sems, first, cut):
        self.target, self.buffer, self.shape, self.dtype = target, buffer, target.shape, target.dtype
        axis, count = cut
        size = target.shape[axis] // count
        self.copies = []
        for index in range(count):
            at = (slice(None),) * axis + (pl.ds(index * size, size),)
            here, there = (buffer, target) if count == 1 else (buffer.at[at], target.at[at])
            self.copies.append(pltpu.make_async_copy(here, there, sems.at[first + index]))
        self.held = set(range(count))

    def send(self, index=0):
        self.held.remove(index)
        self.copies[index].start()

    def finish(self):
        for index in sorted(self.held):
            self.send(index)

    def __getitem__(self, at):
        return self.buffer[at]

    def __setitem__(self, at, value):
        self.buffer[at] = value


SCALARS, AFTER, NEAR, LATE = "scalars", "after", "near", (0, 1)


SPACES = {SCALARS: pltpu.SMEM, NEAR: pltpu.VMEM, AFTER: pl.ANY}


def placed(operand, kind):
    if kind in (SCALARS, AFTER):
        return operand
    return pltpu.with_memory_space_constraint(operand, pltpu.VMEM if kind == NEAR else pltpu.HBM)


TOLD = 0.75


def call(body, outs, ins, cuts=None, scratch=(), cost=1.0, vmem=None):
    single = not isinstance(outs, (list, tuple))
    outs = [outs] if single else list(outs)
    cuts = list(cuts) if cuts is not None else [LATE] * len(outs)
    late = [index for index, kind in enumerate(ins) if isinstance(kind, tuple)]
    in_counts = [ins[index][1] for index in late]
    far = [index for index, kind in enumerate(cuts) if isinstance(kind, tuple)]
    out_counts = [cuts[index][1] for index in far]

    def wrapped(*refs):
        refs = list(refs)
        operands, refs = refs[: len(ins)], refs[len(ins) :]
        targets, refs = refs[: len(outs)], refs[len(outs) :]
        extra, refs = refs[: len(scratch)], refs[len(scratch) :]
        in_buffers, refs = refs[: len(late)], refs[len(late) :]
        out_buffers, sems = refs[: len(far)], refs[len(far) :]
        in_sems, out_sems = sems[0] if late else None, sems[-1] if far else None
        arriving = {
            index: Arriving(operands[index], in_buffers[at], in_sems, sum(in_counts[:at]), ins[index])
            for at, index in enumerate(late)
        }
        for index in range(max(in_counts, default=0)):
            for operand in arriving.values():
                operand.start(index)
        leaving = {
            index: Leaving(targets[index], out_buffers[at], out_sems, sum(out_counts[:at]), cuts[index])
            for at, index in enumerate(far)
        }
        results = [leaving[index] if index in leaving else Held(target) for index, target in enumerate(targets)]
        given = [
            arriving[index] if index in arriving else Held(operands[index]) if kind == NEAR else operands[index]
            for index, kind in enumerate(ins)
            if kind != AFTER
        ]
        body(*given, *results, *extra)
        for operand in arriving.values():
            operand.whole()
        for result in leaving.values():
            result.finish()
        for result in leaving.values():
            for copy in result.copies:
                copy.wait()

    def run(*operands):
        buffers = [pltpu.VMEM(operands[index].shape, operands[index].dtype) for index in late]
        buffers += [pltpu.VMEM(outs[index].shape, outs[index].dtype) for index in far]
        sems = [pltpu.SemaphoreType.DMA((sum(counts),)) for counts in (in_counts, out_counts) if counts]
        results = pl.pallas_call(
            wrapped,
            out_shape=[
                (pltpu.VMEM if kind == NEAR else pltpu.HBM)(out.shape, out.dtype) for out, kind in zip(outs, cuts)
            ],
            in_specs=[pl.BlockSpec(memory_space=SPACES.get(kind, pltpu.HBM)) for kind in ins],
            out_specs=[pl.BlockSpec(memory_space=SPACES.get(kind, pltpu.HBM)) for kind in cuts],
            scratch_shapes=list(scratch) + buffers + sems,
            compiler_params=pltpu.CompilerParams(vmem_limit_bytes=vmem or VMEM_BYTES),
            cost_estimate=pl.CostEstimate(
                flops=int(cost * TOLD * 1.1e9), bytes_accessed=int(cost * TOLD * 3.4e6), transcendentals=0
            ),
        )(*(placed(operand, kind) for operand, kind in zip(operands, ins)))
        return results[0] if single else results

    return run


def shaped(shape, kind=BF16):
    return jax.ShapeDtypeStruct(shape, kind)


def row(ref):
    return full(ref[...][None, :])


def norm_stats(values):
    mean = jnp.mean(values, axis=-1, keepdims=True)
    centered = values - mean
    scale = lax.rsqrt(jnp.mean(centered * centered, axis=-1, keepdims=True) + 1e-05)
    return centered * scale, scale


def norm_backward(grad, values, gain):
    hat, scale = norm_stats(values)
    inner = grad * gain
    mean_inner = jnp.mean(inner, axis=-1, keepdims=True)
    mean_hat = jnp.mean(inner * hat, axis=-1, keepdims=True)
    pulled = scale * (inner - mean_inner - hat * mean_hat)
    return (
        pulled,
        jnp.sum(grad * hat, axis=0, keepdims=True),
        jnp.sum(grad, axis=0, keepdims=True),
    )


def gelu_both(values):
    square = values * values
    rise = 0.5 + 0.5 * jnp.tanh(values * (0.7978845608028654 + 0.035677408136300125 * square))
    value = values * rise
    slope = 1.5957691216057308 + 0.21406444881780076 * square
    return value, rise + value * (1.0 - rise) * slope


def head_lanes(width, which):
    lane = lax.broadcasted_iota(jnp.int32, (1, width), 1)
    return (lane // HEAD_DIM) == which


def keep_lanes(values, lanes):
    return jnp.where(lanes, values, jnp.zeros_like(values))


def fill_bias(bias_ref, length):
    query = lax.broadcasted_iota(jnp.int32, bias_ref.shape, 0)
    key = lax.broadcasted_iota(jnp.int32, bias_ref.shape, 1)
    bias_ref[...] = jnp.where((key <= query) & (key < length), 0.0, -1e30)


def turned_heads(pair):
    turned = full(pair).T
    return [half(turned[which * HEAD_DIM : (which + 1) * HEAD_DIM]) for which in range(2)]


def attend_rows(q_ref, k_ref, v_ref, o_ref, p_ref, bias_ref, length):
    fill_bias(bias_ref, length)
    for pair in range(q_ref.shape[1] // 128):
        lanes = slice(pair * 128, pair * 128 + 128)
        keys, values = k_ref[:, lanes], v_ref[:, lanes]
        total = None
        for which in range(2):
            mask = head_lanes(128, which)
            query = keep_lanes(q_ref[:, lanes] * 0.125, mask).astype(BF16)
            scores = dot_nt(query, keys) + bias_ref[...]
            weights = jnp.exp(scores - jnp.max(scores, axis=-1, keepdims=True))
            weights = weights * (1.0 / jnp.sum(weights, axis=-1, keepdims=True))
            p_ref[2 * pair + which] = half(weights.T)
            p_ref.send(2 * pair + which)
            mixed = dot(half(weights), keep_lanes(values, mask))
            total = mixed if total is None else total + mixed
        o_ref[:, lanes] = half(total)


def attend_first(scal_ref, mine_ref, other_ref, gain_ref, shift_ref, bias_refs, w_ref, out_ref,
                 x_ref, n_ref, q_ref, k_ref, v_ref, o_ref, p_ref, part_ref, bias_ref):
    core, length = scal_ref[0], scal_ref[1]
    mid = mine_ref.shape[0]
    x_ref[pl.ds(pl.multiple_of(core * mid, mid), mid), :] = mine_ref[...]
    x_ref[pl.ds(pl.multiple_of((1 - core) * mid, mid), mid), :] = other_ref[...]
    hat, _ = norm_stats(full(x_ref[...]))
    normed = half(hat * row(gain_ref) + row(shift_ref))
    n_ref[...] = normed
    x_ref.send()
    n_ref.send()
    q_ref[...] = half(dot(normed, w_ref.piece(0)[0]) + full(bias_refs[0:1, :]))
    k_ref[...] = half(dot(normed, w_ref.piece(1)[1]))
    v_ref[...] = half(dot(normed, w_ref.piece(2)[2]) + full(bias_refs[1:2, :]))
    for ref in (q_ref, k_ref, v_ref):
        ref.send()
    attend_rows(q_ref, k_ref, v_ref, o_ref, p_ref, bias_ref, length)
    o_ref.send()
    part_ref[...] = half(dot(o_ref[...], out_ref[...]))


def attend_second(scal_ref, prev_ref, mine_ref, other_ref, before_ref, gain_ref, shift_ref, qb_ref, fb_ref,
                  w_ref, f_ref, v1_ref, out_ref,
                  x_ref, n_ref, q_ref, k_ref, v_ref, o_ref, p_ref, part_ref, bias_ref):
    length = scal_ref[1]
    x_ref[...] = prev_ref[...] + (full(mine_ref[...]) + full(other_ref[...])) + row(before_ref)
    hat, _ = norm_stats(x_ref[...])
    normed = half(hat * row(gain_ref) + row(shift_ref))
    n_ref[...] = normed
    x_ref.send()
    n_ref.send()
    fresh = f_ref.shape[0]
    q_ref[...] = half(dot(normed, w_ref.piece(0)[0]) + row(qb_ref))
    k_ref[...] = half(dot(normed, w_ref.piece(1)[1]))
    v_ref[...] = v1_ref[...]
    v_ref[:, :fresh] = half(dot_nt(normed, f_ref[...]) + row(fb_ref))
    for ref in (q_ref, k_ref, v_ref):
        ref.send()
    attend_rows(q_ref, k_ref, v_ref, o_ref, p_ref, bias_ref, length)
    o_ref.send()
    part_ref[...] = half(dot(o_ref[...], out_ref[...]))


def attend_pull(q_ref, k_ref, v_ref, p_ref, do_ref, dq_ref, dk_ref, dv_ref, ds_ref):
    rows, width = q_ref.shape
    heads = width // HEAD_DIM
    blocks = rows // BLOCK
    ones = jnp.ones((16, rows), BF16)
    for pair in range(heads // 2):
        lanes = slice(pair * 128, pair * 128 + 128)
        keys, values = turned_heads(k_ref[:, lanes]), v_ref[:, lanes]
        pulled_query, queries, grads = {}, {}, {}
        for which in range(2):
            head = 2 * pair + which
            p_ref.piece(head)
            mask = head_lanes(128, which)
            queries[which] = keep_lanes(q_ref[:, lanes] * 0.125, mask).astype(BF16)
            grads[which] = keep_lanes(do_ref[:, lanes], mask)
            for block in range(blocks):
                start, stop = block * BLOCK, (block + 1) * BLOCK
                pulled = dot_nt(values[:stop], grads[which][start:stop])
                weights = full(p_ref.buffer[head, :stop, start:stop])
                total = dot(ones[:, :stop], p_ref.buffer[head, :stop, start:stop])[0:1, :]
                centre = jnp.sum(weights * pulled, axis=0, keepdims=True) * (1.0 / total)
                score_grad = half(weights * (pulled - centre))
                ds_ref[which, :stop, start:stop] = score_grad
                pulled_query[block, which] = dot(keys[which][:, :stop], score_grad)
        for block in range(blocks):
            start, stop = block * BLOCK, (block + 1) * BLOCK
            joined = jnp.concatenate([pulled_query[block, 0], pulled_query[block, 1]], axis=0) * 0.125
            dq_ref[start:stop, lanes] = half(joined.T)
            dk_ref[start:stop, lanes] = half(
                dot(ds_ref[0, start:stop, start:], queries[0][start:])
                + dot(ds_ref[1, start:stop, start:], queries[1][start:])
            )
            dv_ref[start:stop, lanes] = dot(
                p_ref.buffer[2 * pair, start:stop, start:], grads[0][start:]
            ) + dot(p_ref.buffer[2 * pair + 1, start:stop, start:], grads[1][start:])


def column_sum(values):
    return jnp.sum(full(values), axis=0, keepdims=True)


def pull_second(g4_ref, mine_ref, other_ref, x_ref, gain_ref, out_ref, q_ref, k_ref, v_ref, p_ref, w_ref, f_ref,
                g_ref, gb_ref, dq_ref, dk_ref, dv_ref, dvb_ref, part_ref, rep_ref, loc_ref,
                do_ref, ds_ref):
    grad = full(mine_ref[...]) + full(other_ref[...])
    pulled, gain, shift = norm_backward(grad, x_ref[...], row(gain_ref))
    g_ref[...] = full(g4_ref[...]) + pulled
    rep_ref[...] = jnp.zeros_like(rep_ref)
    loc_ref[...] = jnp.zeros_like(loc_ref)
    rep_ref[0:1, :] = gain
    rep_ref[1:2, :] = shift
    rep_ref[2:3, :] = column_sum(g_ref[...])
    gb_ref[...] = half(g_ref[...])
    g_ref.send()
    gb_ref.send()
    do_ref[...] = half(dot_nt(gb_ref[...], out_ref[...]))
    attend_pull(q_ref, k_ref, v_ref, p_ref, do_ref, dq_ref, dk_ref, dv_ref, ds_ref)
    fresh = f_ref.shape[0]
    dvb_ref[...] = half(dv_ref[...])
    fresh_grad = dvb_ref[:, :fresh]
    part_ref[...] = half(
        dot_nt(dq_ref[...], w_ref[0]) + dot_nt(dk_ref[...], w_ref[1]) + dot(fresh_grad, f_ref[...])
    )
    loc_ref[0:1, :] = column_sum(dq_ref[...])
    loc_ref[1:2, :] = column_sum(dvb_ref[...])


def pull_first(scal_ref, g2_ref, mine_ref, other_ref, x_ref, gain_ref, out_ref, q_ref, k_ref, v_ref, p_ref, w_ref, reused_ref,
               g_ref, gb_ref, dq_ref, dk_ref, dv_ref, own_ref, part_ref, rep_ref, loc_ref,
               do_ref, ds_ref, dv_full, partial, *, fresh):
    grad = full(mine_ref[...]) + full(other_ref[...])
    pulled, gain, shift = norm_backward(grad, x_ref[...], row(gain_ref))
    g_ref[...] = g2_ref[...] + pulled
    rep_ref[...] = jnp.zeros_like(rep_ref)
    loc_ref[...] = jnp.zeros_like(loc_ref)
    rep_ref[0:1, :] = gain
    rep_ref[1:2, :] = shift
    rep_ref[2:3, :] = column_sum(g_ref[...])
    gb_ref[...] = half(g_ref[...])
    g_ref.send()
    gb_ref.send()
    do_ref[...] = half(dot_nt(gb_ref[...], out_ref[...]))
    attend_pull(q_ref, k_ref, v_ref, p_ref, do_ref, dq_ref, dk_ref, dv_full, ds_ref)
    column = lax.broadcasted_iota(jnp.int32, (1, dv_full.shape[1]), 1)
    dv_ref[...] = half(dv_full[...] + jnp.where(column >= fresh, reused_ref[...], 0.0))
    partial[...] = half(
        dot_nt(dq_ref[...], w_ref[0]) + dot_nt(dk_ref[...], w_ref[1]) + dot_nt(dv_ref[...], w_ref[2])
    )
    core, mid = scal_ref[0], own_ref.shape[0]
    own_ref[...] = partial[pl.ds(pl.multiple_of(core * mid, mid), mid), :]
    part_ref[...] = partial[pl.ds(pl.multiple_of((1 - core) * mid, mid), mid), :]
    loc_ref[0:1, :] = column_sum(dq_ref[...])
    loc_ref[1:2, :] = column_sum(dv_ref[...])


ROW_BLOCK = 256


def hidden_spans(ref):
    size = ref.shape[1] // HIDDEN_CUT
    return [slice(index * size, (index + 1) * size) for index in range(HIDDEN_CUT)]


def add_to(total, span, value, fresh):
    total[span, :] = value if fresh else total[span, :] + value


def feed_first(prev_ref, mine_ref, other_ref, before_ref, gain_ref, shift_ref, bias_ref, fc_ref, proj_ref,
               x_ref, m_ref, z_ref, pull_ref, part_ref, total):
    x_ref[...] = full(prev_ref[...]) + (full(mine_ref[...]) + full(other_ref[...])) + row(before_ref)
    x_ref.send()
    hat, _ = norm_stats(x_ref[...])
    m_ref[...] = half(hat * row(gain_ref) + row(shift_ref))
    m_ref.send()
    for index, columns in enumerate(hidden_spans(fc_ref)):
        fc, proj = fc_ref.piece(index), proj_ref.piece(index)
        bias = full(bias_ref[columns][None, :])
        for low in range(0, m_ref.shape[0], ROW_BLOCK):
            span = slice(low, low + ROW_BLOCK)
            value, pull = gelu_both(dot(m_ref[span, :], fc[:, columns]) + bias)
            value = half(value)
            z_ref[span, columns] = value
            pull_ref[span, columns] = half(pull)
            add_to(total, span, dot(value, proj[columns, :]), index == 0)
        z_ref.send(index)
        pull_ref.send(index)
    part_ref[...] = half(total[...])


def feed_second(scal_ref, prev_ref, mine_ref, other_ref, before_ref, gain_ref, shift_ref, bias_ref,
                cot_ref, cot_other_ref, fc_ref, proj_ref,
                x_ref, m_ref, g_ref, z_ref, du_ref, own_ref, part_ref, pulled_ref, rep_ref, loc_ref, total, pulled_total):
    core, length = scal_ref[0], scal_ref[1]
    x_ref[...] = prev_ref[...] + (full(mine_ref[...]) + full(other_ref[...])) + row(before_ref)
    x_ref.send()
    hat, _ = norm_stats(x_ref[...])
    m_ref[...] = half(hat * row(gain_ref) + row(shift_ref))
    m_ref.send()
    mid = cot_ref.shape[0]
    place = lax.broadcasted_iota(jnp.int32, (mid, 1), 0)
    for source, owner in ((cot_ref, core), (cot_other_ref, 1 - core)):
        base = pl.multiple_of(owner * mid, mid)
        alive = (place + base < length).astype(F32)
        g_ref[pl.ds(base, mid), :] = half(full(source[...]) * alive)
    g_ref.send()
    rep_ref[...] = jnp.zeros_like(rep_ref)
    loc_ref[...] = jnp.zeros_like(loc_ref)
    rep_ref[0:1, :] = column_sum(g_ref[...])
    for index, columns in enumerate(hidden_spans(fc_ref)):
        fc, proj = fc_ref.piece(index), proj_ref.piece(index)
        bias = full(bias_ref[columns][None, :])
        sums = None
        for low in range(0, m_ref.shape[0], ROW_BLOCK):
            span = slice(low, low + ROW_BLOCK)
            value, pull = gelu_both(dot(m_ref[span, :], fc[:, columns]) + bias)
            value = half(value)
            z_ref[span, columns] = value
            add_to(total, span, dot(value, proj[columns, :]), index == 0)
            du = half(dot_nt(g_ref[span, :], proj[columns, :]) * pull)
            du_ref[span, columns] = du
            add_to(pulled_total, span, dot_nt(du, fc[:, columns]), index == 0)
            sums = column_sum(du) if sums is None else sums + column_sum(du)
        loc_ref[0:1, columns] = sums
        z_ref.send(index)
        du_ref.send(index)
    own_ref[...] = half(total[pl.ds(pl.multiple_of(core * mid, mid), mid), :])
    part_ref[...] = half(total[pl.ds(pl.multiple_of((1 - core) * mid, mid), mid), :])
    pulled_ref[...] = half(pulled_total[...])


def feed_pull(g3_ref, mine_ref, other_ref, xin_ref, gain_ref, pull_ref, fc_ref, proj_ref,
              g_ref, gb_ref, du_ref, pulled_ref, rep_ref, loc_ref, pulled_total):
    grad = full(mine_ref[...]) + full(other_ref[...])
    pulled, gain, shift = norm_backward(grad, xin_ref[...], row(gain_ref))
    g_ref[...] = g3_ref[...] + pulled
    g_ref.send()
    rep_ref[...] = jnp.zeros_like(rep_ref)
    loc_ref[...] = jnp.zeros_like(loc_ref)
    rep_ref[0:1, :] = gain
    rep_ref[1:2, :] = shift
    rep_ref[2:3, :] = column_sum(g_ref[...])
    gb_ref[...] = half(g_ref[...])
    gb_ref.send()
    for index, columns in enumerate(hidden_spans(fc_ref)):
        fc, proj = fc_ref.piece(index), proj_ref.piece(index)
        pull = pull_ref.piece(index)
        sums = None
        for low in range(0, gb_ref.shape[0], ROW_BLOCK):
            span = slice(low, low + ROW_BLOCK)
            du = half(dot_nt(gb_ref[span, :], proj[columns, :]) * full(pull[span, columns]))
            du_ref[span, columns] = du
            add_to(pulled_total, span, dot_nt(du, fc[:, columns]), index == 0)
            sums = column_sum(du) if sums is None else sums + column_sum(du)
        loc_ref[0:1, columns] = sums
        du_ref.send(index)
    pulled_ref[...] = half(pulled_total[...])


PACKED, SHARED = 24, 10


def pull_tokens(scal_ref, g1_ref, mine_ref, other_ref, x_ref, gain_ref,
                rep4_ref, rep3_ref, rep2_ref, rep1_ref, loc4_ref, loc3_ref, loc2_ref, loc1_ref,
                out_ref, pack_ref):
    mid, model = out_ref.shape
    own = pl.ds(pl.multiple_of(scal_ref[0] * mid, mid), mid)
    grad = full(mine_ref[...]) + full(other_ref[...])
    pulled, gain, shift = norm_backward(grad, full(x_ref[own, :]), row(gain_ref))
    out_ref[...] = half(g1_ref[own, :] + pulled)
    pack_ref[...] = jnp.zeros_like(pack_ref)
    pack_ref[0:1, :] = rep4_ref[0:1, :]
    for index, ref in enumerate((rep3_ref, rep2_ref, rep1_ref)):
        pack_ref[1 + 3 * index : 4 + 3 * index, :] = ref[0:3, :]
    pack_ref[SHARED : SHARED + 1, :] = gain
    pack_ref[SHARED + 1 : SHARED + 2, :] = shift
    for index, ref in enumerate((loc4_ref, loc2_ref)):
        for part in range(2):
            at = SHARED + 2 + 2 * index + part
            pack_ref[at : at + 1, :] = ref[0:1, part * model : (part + 1) * model]
    for index, ref in enumerate((loc3_ref, loc1_ref)):
        at = SHARED + 6 + index
        for part in range(2):
            pack_ref[at : at + 1, part * model // 2 : (part + 1) * model // 2] = ref[part : part + 1, :]


def unpack_sums(scal_ref, mine_ref, other_ref, *outs):
    first = scal_ref[0] == 0
    (gain1, shift1, qv1, out1, gain2, shift2, fc1, proj1,
     gain3, shift3, q2, v2, out2, gain4, shift4, fc2, proj2) = outs
    same = (proj2, gain4, shift4, out2, gain3, shift3, proj1, gain2, shift2, out1)
    for index, ref in enumerate(same):
        ref[...] = mine_ref[index, :]
    for index, ref in enumerate((gain1, shift1)):
        ref[...] = mine_ref[SHARED + index, :] + other_ref[SHARED + index, :]
    model = gain1.shape[0]

    def both(at):
        mine, other = mine_ref[at : at + 1, :], other_ref[at : at + 1, :]
        return jnp.where(first, mine, other), jnp.where(first, other, mine)

    for index, ref in enumerate((fc2, fc1)):
        for part in range(2):
            for core, value in enumerate(both(SHARED + 2 + 2 * index + part)):
                at = (2 * core + part) * model
                ref[at : at + model] = value[0]
    low, high = both(SHARED + 6)
    middle = model // 2
    q2[:middle] = low[0, :middle]
    q2[middle:] = high[0, :middle]
    fresh = v2.shape[0] // 2
    v2[...] = jnp.concatenate([low[:, middle : middle + fresh], high[:, middle : middle + fresh]], axis=1)[0]
    low, high = both(SHARED + 7)
    for part in range(2):
        span = slice(part * middle, (part + 1) * middle)
        qv1[part : part + 1, :middle] = low[:, span]
        qv1[part : part + 1, middle:] = high[:, span]


def finish_layer(scal_ref, x_ref, mine_ref, other_ref, before_ref, out_ref, ended_ref):
    ended_ref[...] = jnp.zeros(ended_ref.shape, F32)
    mid = out_ref.shape[0]
    base = pl.multiple_of(scal_ref[0] * mid, mid)
    own = pl.ds(base, mid)
    total = x_ref[own, :] + (full(mine_ref[...]) + full(other_ref[...])) + row(before_ref)
    place = lax.broadcasted_iota(jnp.int32, (mid, 1), 0)
    out_ref[...] = half(total * (place + base < scal_ref[1]).astype(F32))


FIRST_ORDERS = ((0, 1, 2, 3), (1, 0, 3, 2))
SECOND_ORDERS = ((0, 2, 1, 3), (2, 3, 1, 0))
THIRD_ORDERS = ((0, 2, 1, 3), (1, 0, 2, 3))
FOURTH_ORDERS = ((3, 1, 0, 2), (2, 0, 1, 3))
FIFTH_ORDERS = ((0, 1, 3, 2), (1, 0, 2, 3))


def bit_orders(orders, bits):
    return [[bit for bit in order if bit < bits] + list(range(4, bits)) for order in orders]


def row_table(orders, count):
    bits = count.bit_length() - 1
    table = np.zeros((count, 2, count), np.int32)
    for core, order in enumerate(bit_orders(orders, bits)):
        for me in range(count):
            for block in range(count):
                place = 0
                for bit in order:
                    place = 2 * place + (((block ^ me) >> bit) & 1)
                table[me, core, block] = place
    return table.reshape(count * 2, count)


def fold_pairs(orders, count, phase):
    bits = count.bit_length() - 1
    pairs = []
    for core, order in enumerate(bit_orders(orders, bits)):
        for me in range(count):
            pairs.append((2 * me + core, 2 * (me ^ (1 << order[phase])) + core))
    return pairs


def weight_grads(scalars, orders, count, products, width, after, far):
    operands = [operand for rows, rights in products for operand in (rows, *rights)]
    depth, model = products[0][0].shape
    span = model // count
    bits = count.bit_length() - 1
    lists = bit_orders(orders, bits)

    def kind_of(operand):
        if not any(operand is other for other in far):
            return NEAR
        return (1, 2) if operand.shape[1] > model else LATE

    def body(scal_ref, *refs):
        keep_ref, send_ref, turned = refs[len(refs) - 3 :]
        core, me = scal_ref[0], scal_ref[2]

        def turn(ref):
            columns = ref[...].T
            for index in range(count):
                apart = index ^ me
                places = [
                    sum(((apart >> bit) & 1) << (bits - 1 - at) for at, bit in enumerate(order)) for order in lists
                ]
                place = jnp.where(core == 0, places[0], places[1])
                at = pl.ds(pl.multiple_of(place * span, 16), span)
                turned[at, :] = columns[index * span : (index + 1) * span]

        start, taken = 0, 0
        for _, rights in products:
            turn(refs[taken])
            for ref in refs[taken + 1 : taken + 1 + len(rights)]:
                size = min(ref.shape[1], width - start)
                step = size // len(ref.copies)
                for index in range(len(ref.copies)):
                    columns = slice(index * step, (index + 1) * step)
                    at = slice(start + index * step, start + (index + 1) * step)
                    right = ref.piece(index)[:, columns]
                    send_ref[:, at] = half(dot(turned[model // 2 :, :], right))
                    keep_ref[:, at] = half(dot(turned[: model // 2, :], right))
                start += size
            taken += 1 + len(rights)

    return call(
        body,
        [shaped((model // 2, width))] * 2,
        [SCALARS] + [kind_of(operand) for operand in operands] + [AFTER] * len(after),
        cuts=[NEAR, NEAR],
        scratch=[pltpu.VMEM((model, depth), BF16)],
        cost=width / 3072 * 5,
        vmem=GRAD_BYTES,
    )(scalars, *operands, *after)


def weight_grads_plain(orders, count, products, width):
    model = products[0][0].shape[1]
    parts = [dot_tn(rows, right) for rows, rights in products for right in rights]
    product = half(jnp.concatenate(parts, axis=1)[:, :width])
    if count == 1:
        return product, product
    table = jnp.asarray(row_table(orders, count))
    me = 2 * lax.axis_index("seq") + lax.axis_index("tp")
    table = lax.dynamic_index_in_dim(table, me, 0, keepdims=False)
    back = jnp.zeros((count,), jnp.int32).at[table].set(jnp.arange(count, dtype=jnp.int32))
    placed = jnp.take(product.reshape(count, model // count, width), back, axis=0)
    placed = placed.reshape(model, width)
    return placed[: model // 2], placed[model // 2 :]


GRAD_BYTES = 12 * 1024 * 1024
SMALL_BYTES = 8 * 1024 * 1024


def fold(keep, other, after, extra=()):
    rows, width = keep.shape
    left = rows // 2
    if left % 16:
        total = half(full(keep) + full(other))
        return [total[:left], total[left:]] + ([extra[0] + extra[1]] if extra else [])

    def body(keep_ref, other_ref, *refs):
        if extra:
            refs[-1][...] = refs[0][...] + refs[1][...]
        kept_ref, send_ref = refs[len(extra) : len(extra) + 2]
        send_ref[...] = half(full(keep_ref[left:, :]) + full(other_ref[left:, :]))
        kept_ref[...] = half(full(keep_ref[:left, :]) + full(other_ref[:left, :]))

    outs = [shaped((left, width))] * 2 + [shaped(value.shape, F32) for value in extra[:1]]
    kinds = [NEAR] * (2 + len(extra)) + [AFTER] * len(after)
    return call(body, outs, kinds, cuts=[NEAR] * len(outs), cost=2, vmem=SMALL_BYTES)(keep, other, *extra, *after)


def fold_last(keep, other, cuts, after):
    rows, width = keep.shape
    plan, outs, start = [], [], 0
    for cut in cuts:
        stack, parts = (None, cut) if not isinstance(cut, tuple) else (cut[0], cut[1:])
        parts = (parts,) if stack is None else parts
        plan.append((stack, [(start + sum(parts[:i]), part) for i, part in enumerate(parts)]))
        start += sum(parts)
        shape = (rows, parts[0])
        if stack is not None:
            shape = shape[:stack] + (len(parts),) + shape[stack:]
        outs.append(shaped(shape, F32))

    def body(keep_ref, other_ref, *refs):
        refs[-1][...] = jnp.zeros(refs[-1].shape, F32)
        for (stack, spans), ref in zip(plan, refs):
            for index, (low, size) in enumerate(spans):
                span = slice(low, low + size)
                value = full(keep_ref[:, span]) + full(other_ref[:, span])
                if stack is None:
                    ref[...] = value
                elif stack == 0:
                    ref[index] = value
                else:
                    ref[:, index, :] = value

    if rows != 48:
        total = full(keep) + full(other)
        cuts = [[total[:, low : low + size] for low, size in spans] for _, spans in plan]
        results = [pieces[0] if stack is None else jnp.stack(pieces, stack) for (stack, _), pieces in zip(plan, cuts)]
        return results + [keep]
    kinds = [NEAR, NEAR] + [AFTER] * len(after)
    places = [LATE] * len(outs) + [NEAR]
    outs.append(shaped((8, 128), F32))
    return call(body, outs, kinds, cuts=places, cost=2, vmem=SMALL_BYTES)(keep, other, *after)


class Sum:
    def __init__(self, scalars, orders, count, products, width, after=(), far=()):
        self.orders, self.count, self.phase = orders, count, 0
        self.bits = count.bit_length() - 1
        if count > 1 and (products[0][0].shape[1] // count) % 16 == 0:
            self.keep, self.send = weight_grads(scalars, orders, count, products, width, tuple(after), far)
        else:
            self.keep, self.send = weight_grads_plain(orders, count, products, width)
        self.first = self.keep
        if self.bits:
            self.move()
        else:
            self.other = jnp.zeros_like(self.keep)

    def move(self):
        pairs = fold_pairs(self.orders, self.count, self.phase)
        self.other = lax.ppermute(self.send, ("seq", "tp"), pairs)

    def fold(self, *after, beside=None):
        if self.phase + 1 < self.bits:
            self.phase += 1
            extra = beside.terms() if beside is not None else ()
            results = fold(self.keep, self.other, tuple(after), extra)
            self.keep, self.send = results[:2]
            if extra:
                beside.take(results[2])
            self.move()
        return self.keep

    def finish(self, *cuts, after=()):
        while self.phase + 1 < self.bits:
            self.fold()
        return fold_last(self.keep, self.other, cuts, tuple(after))


class Spread:
    def __init__(self, values, count):
        self.values, self.count, self.distance = values, count, 1
        self.move()

    def move(self):
        if self.distance < self.count:
            pairs = [(index, index ^ self.distance) for index in range(self.count)]
            self.other = lax.ppermute(self.values, "seq", pairs)

    def terms(self):
        return (self.values, self.other) if self.distance < self.count else ()

    def take(self, total):
        self.values = total
        self.distance *= 2
        self.move()

    def finish(self):
        while self.distance < self.count:
            self.take(self.values + self.other)
        return self.values


def on_device(count, *arguments):
    (
        tokens, seq_lengths, cotangent, norm1_gain, norm1_shift, qkv1_weight, qv1_bias, out1_weight, out1_bias,
        norm2_gain, norm2_shift, fc1_weight, fc1_bias, proj1_weight, proj1_bias, norm3_gain, norm3_shift,
        qk2_weight, v2_weight, q2_bias, v2_bias, out2_weight, out2_bias, norm4_gain, norm4_shift, fc2_weight,
        fc2_bias, proj2_weight, proj2_bias,
    ) = arguments
    mid, model = tokens.shape
    rows = 2 * mid
    local = qkv1_weight.shape[2]
    fresh = v2_weight.shape[1]
    hidden = fc1_weight.shape[1]
    core = lax.axis_index("tp")
    scalars = jnp.stack([core, seq_lengths[0], lax.axis_index("seq")]).astype(jnp.int32)
    qkv1 = qkv1_weight.transpose(1, 0, 2)
    qk2 = qk2_weight.transpose(1, 0, 2)
    fresh_weight = v2_weight.T

    square, narrow = (rows, model), (rows, local)
    heads = local // HEAD_DIM
    by_head = (0, heads)
    weights_out = shaped((heads, rows, rows))
    bias_scratch = pltpu.VMEM((rows, rows), F32)
    attend_outs = [shaped(square)] + [shaped(narrow)] * 4 + [weights_out, shaped(square)]
    pull_scratch = [pltpu.VMEM(narrow, BF16), pltpu.VMEM((2, rows, rows), BF16)]
    pull_outs = [shaped(square, F32), shaped(square), shaped(narrow), shaped(narrow)]
    sums_outs = [shaped(square), shaped((8, model), F32), shaped((8, local), F32)]
    total_scratch = pltpu.VMEM(square, F32)
    hidden_out, by_column, by_row = shaped((rows, hidden)), (1, HIDDEN_CUT), (0, HIDDEN_CUT)
    feed_sums = [shaped(square), shaped((8, model), F32), shaped((8, hidden), F32)]

    x0, n1, q1, k1, v1, o1, p1, part = call(
        attend_first, [shaped(square)] + attend_outs, [SCALARS, LATE, NEAR] + [LATE] * 5,
        cuts=[NEAR, LATE, LATE, LATE, NEAR, LATE, by_head, NEAR], scratch=[bias_scratch], cost=8,
    )(scalars, tokens, swap(tokens), norm1_gain, norm1_shift, qv1_bias, qkv1, out1_weight)
    cot_other = swap(cotangent)
    x1, m1, z1, pull1, part = call(
        feed_first,
        [shaped(square, F32), shaped(square), hidden_out, hidden_out, shaped(square)],
        [NEAR, NEAR, NEAR] + [LATE] * 4 + [by_column, by_row, AFTER],
        cuts=[NEAR, LATE, by_column, by_column, NEAR],
        scratch=[total_scratch],
        cost=8,
    )(x0, part, swap(part), out1_bias, norm2_gain, norm2_shift, fc1_bias, fc1_weight, proj1_weight, cot_other)

    x2, n3, q2, k2, v2, o2, p2, part = call(
        attend_second, [shaped(square, F32)] + attend_outs, [SCALARS, NEAR, NEAR, NEAR] + [LATE] * 5 + [(0, 2), LATE, NEAR, LATE],
        cuts=[NEAR, LATE, NEAR, NEAR, NEAR, LATE, NEAR, NEAR], scratch=[bias_scratch], cost=10,
    )(scalars, x1, part, swap(part), proj1_bias, norm3_gain, norm3_shift, q2_bias, v2_bias, qk2, fresh_weight, v1,
      out2_weight)
    x3, m3, gb4, z3, du3, out_part, part, pulled, rep4, loc4 = call(
        feed_second,
        [shaped(square, F32), shaped(square), shaped(square), hidden_out, hidden_out]
        + [shaped((mid, model)), shaped((mid, model))] + feed_sums,
        [SCALARS, NEAR, NEAR, NEAR] + [LATE] * 5 + [NEAR, by_column, by_row],
        cuts=[NEAR] * 10,
        scratch=[total_scratch, total_scratch],
        vmem=BIG_BYTES,
        cost=12,
    )(scalars, x2, part, swap(part), out2_bias, norm4_gain, norm4_shift, fc2_bias, cotangent, cot_other,
      fc2_weight, proj2_weight)
    pulled_other = swap(pulled)
    out_other = swap(part)
    first = Sum(scalars, FIRST_ORDERS, count, [(m3, [du3]), (gb4, [z3])], 2 * hidden)

    g3, gb3, dq2, dk2, dv2, df2, part, rep3, loc3 = call(
        pull_second, pull_outs + [shaped(narrow, F32), shaped(narrow)] + sums_outs,
        [NEAR] * 4 + [LATE, LATE] + [NEAR] * 4 + [LATE] * 2 + [AFTER], cuts=[NEAR] * 9,
        scratch=pull_scratch, cost=14,
    )(gb4, pulled, pulled_other, x3, norm4_gain, out2_weight, q2, k2, v2, p2, qk2, fresh_weight, first.keep)
    part_other = swap(part)
    second = Sum(
        scalars, SECOND_ORDERS, count, [(gb3, [o2]), (n3, [dq2, dk2, df2])], 3 * local + 2 * 128, far=(o2, n3)
    )

    g2, gb2, du1, pulled, rep2, loc2 = call(
        feed_pull,
        [shaped(square, F32), shaped(square), hidden_out] + feed_sums,
        [NEAR, NEAR, NEAR, NEAR, LATE, by_column, by_column, by_row, AFTER],
        cuts=[NEAR] * 6,
        scratch=[total_scratch],
        cost=8,
    )(g3, part, part_other, x2, norm3_gain, pull1, fc1_weight, proj1_weight, second.keep)
    pulled_other = swap(pulled)
    third = Sum(scalars, THIRD_ORDERS, count, [(m1, [du1])], hidden, far=(m1,))
    fourth = Sum(scalars, FOURTH_ORDERS, count, [(gb2, [z1])], hidden, [third.first], far=(z1,))
    first.fold(fourth.first)

    g1, gb1, dq1, dk1, dv1, own_part, part, rep1, loc1 = call(
        functools.partial(pull_first, fresh=fresh),
        pull_outs + [shaped(narrow), shaped((mid, model)), shaped((mid, model))] + sums_outs[1:],
        [SCALARS] + [NEAR] * 4 + [LATE] * 4 + [NEAR, by_head, LATE, NEAR, AFTER],
        cuts=[NEAR] * 9,
        scratch=pull_scratch + [pltpu.VMEM(narrow, F32), pltpu.VMEM(square, BF16)],
        cost=12,
    )(scalars, g2, pulled, pulled_other, x1, norm2_gain, out1_weight, q1, k1, v1, p1, qkv1, dv2, first.keep)
    part_other = swap(part)
    second.fold(g1)
    first.fold(second.keep)
    fifth = Sum(
        scalars, FIFTH_ORDERS, count, [(gb1, [o1]), (n1, [dq1, dk1, dv1])], 4 * local, [first.keep], far=(o1, n1)
    )
    tokens_grad, packed = call(
        pull_tokens, [shaped((mid, model)), shaped((PACKED, model), F32)],
        [SCALARS] + [NEAR] * 4 + [LATE] + [NEAR] * 8 + [AFTER], cuts=[LATE, NEAR], cost=3,
    )(scalars, g1, own_part, part_other, x0, norm1_gain, rep4, rep3, rep2, rep1, loc4, loc3, loc2, loc1, fifth.first)
    packed = Spread(packed, count)

    second.fold(packed.values)
    third.fold(second.keep)
    layer_output, ended = call(
        finish_layer, [shaped((mid, model)), shaped((8, 128), F32)], [SCALARS, NEAR, NEAR, NEAR, LATE, AFTER],
        cuts=[LATE, NEAR], cost=2,
    )(
        scalars, x3, out_part, out_other, proj2_bias, third.keep
    )
    fourth.fold(ended, beside=packed)
    fifth.fold(fourth.keep)
    third.fold(fifth.keep, beside=packed)
    second.fold(third.keep)
    first.fold(second.keep, beside=packed)
    sum_out2, sum_qk2, sum_v2, ended = second.finish(local, (1, local, local), fresh, after=[first.keep])
    third.fold(ended, beside=packed)
    fourth.fold(third.keep)
    fifth.fold(fourth.keep)
    sum_fc2, sum_proj2, ended = first.finish(hidden, hidden, after=[fifth.keep])
    sum_fc1, ended = third.finish(hidden, after=[ended])
    fourth.fold(ended)
    fifth.fold(fourth.keep)
    sum_proj1, ended = fourth.finish(hidden, after=[fifth.keep])
    sum_out1, sum_qkv1, _ = fifth.finish(local, (0, local, local, local), after=[ended])
    sum_qkv1 = sum_qkv1.transpose(1, 0, 2)

    packed = packed.finish()
    vector, small = shaped((model,), F32), shaped((2 * fresh,), F32)
    long_vector = shaped((2 * hidden,), F32)
    (
        sum_gain1, sum_shift1, sum_qv1_bias, sum_out1_bias, sum_gain2, sum_shift2, sum_fc1_bias, sum_proj1_bias,
        sum_gain3, sum_shift3, sum_q2_bias, sum_v2_bias, sum_out2_bias, sum_gain4, sum_shift4, sum_fc2_bias,
        sum_proj2_bias,
    ) = call(
        unpack_sums,
        [vector, vector, shaped((2, model), F32), vector, vector, vector, long_vector, vector,
         vector, vector, vector, small, vector, vector, vector, long_vector, vector],
        [SCALARS, NEAR, NEAR],
        cost=2,
    )(scalars, packed, swap(packed))
    return (
        layer_output, tokens_grad, sum_gain1, sum_shift1, sum_qkv1, sum_qv1_bias, sum_out1.T, sum_out1_bias,
        sum_gain2, sum_shift2, sum_fc1, sum_fc1_bias, sum_proj1.T, sum_proj1_bias, sum_gain3, sum_shift3, sum_qk2,
        sum_v2, sum_q2_bias, sum_v2_bias, sum_out2.T, sum_out2_bias, sum_gain4, sum_shift4, sum_fc2, sum_fc2_bias,
        sum_proj2.T, sum_proj2_bias,
    )


def solution(mesh):
    rows, copied = P(("seq", "tp"), None), P()
    columns, deep = P(None, "tp"), P("tp", None)
    wide, long = P("seq", "tp"), P("tp", "seq")
    count = mesh.shape["seq"]

    def body(*arguments):
        return on_device(count, *arguments)

    return jax.shard_map(
        body,
        mesh=mesh,
        in_specs=(
            rows, P("seq"), rows, copied, copied, P(None, None, "tp"), columns, deep, copied,
            copied, copied, columns, P("tp"), deep, copied, copied, copied,
            P(None, None, "tp"), columns, P("tp"), P("tp"), deep, copied, copied, copied, columns,
            P("tp"), deep, copied,
        ),
        out_specs=(
            rows, rows, copied, copied, P("seq", None, "tp"), copied, long, copied,
            copied, copied, wide, copied, long, copied, copied, copied, P("seq", None, "tp"),
            wide, copied, copied, long, copied, copied, copied, wide, copied,
            long, copied,
        ),
        check_vma=False,
    )
```
